32 devices in a mesh: dp: 8 (over z, y), group: 4 (over x, core).
Axes of the slice: x: 2, y: 2, z: 4, core: 2. Of those that a mesh axis runs over, the one named last changes fastest.
Arguments:
- features: bfloat16 [65536, 602], P(('dp', 'group')), may hold values from -6.7 to 6.7
- labels: int32 [65536], P(('dp', 'group')), may hold values from 0 to 40
- neighbors: int32 [65536, 8], P(('dp', 'group')), may hold values from 0 to 2047
- degree: int32 [65536], P(('dp', 'group')), may hold values from 1 to 8
- node_counts: int32 [65536], P(('dp', 'group')), may hold values from 1 to 72, as said below
- edge_counts: int32 [65536, 8], P(('dp', 'group')), may hold values from 1 to 8
- live_nodes: int32 [32], P(('dp', 'group')), may hold values from 1365 to 2048, as said below
- input_weight: float32 [602, 512], P(None, ('dp', 'group')), may hold values from -0.25 to 0.25
- pair_weight: float32 [3, 512, 1024], P(None, None, ('dp', 'group')), may hold values from -0.25 to 0.25
- proj_weight: float32 [3, 1024, 512], P(None, ('dp', 'group')), may hold values from -0.1875 to 0.1875
- head_weight: float32 [512, 41], P(('dp', 'group')), may hold values from -0.25 to 0.25
- input_first: float32 [602, 512], P(None, ('dp', 'group')), may hold values from -0.0024414062 to 0.0024414062
- pair_first: float32 [3, 512, 1024], P(None, None, ('dp', 'group')), may hold values from -0.0024414062 to 0.0024414062
- proj_first: float32 [3, 1024, 512], P(None, ('dp', 'group')), may hold values from -0.0024414062 to 0.0024414062
- head_first: float32 [512, 41], P(('dp', 'group')), may hold values from -0.0078125 to 0.0078125
- input_second: float32 [602, 512], P(None, ('dp', 'group')), may hold values from 2.4414062e-08 to 1.953125e-07
- pair_second: float32 [3, 512, 1024], P(None, None, ('dp', 'group')), may hold values from 2.4414062e-08 to 1.953125e-07
- proj_second: float32 [3, 1024, 512], P(None, ('dp', 'group')), may hold values from 2.4414062e-08 to 1.953125e-07
- head_second: float32 [512, 41], P(('dp', 'group')), may hold values from 3.4332277e-07 to 2.7465821e-06
Outputs:
- mean_loss: float32 [], replicated
- weight_mean: float32 [], replicated
- input_new: float32 [602, 512], P(None, ('dp', 'group'))
- pair_new: float32 [3, 512, 1024], P(None, None, ('dp', 'group'))
- proj_new: float32 [3, 1024, 512], P(None, ('dp', 'group'))
- head_new: float32 [512, 41], P(('dp', 'group'))
- input_first_new: float32 [602, 512], P(None, ('dp', 'group'))
- pair_first_new: float32 [3, 512, 1024], P(None, None, ('dp', 'group'))
- proj_first_new: float32 [3, 1024, 512], P(None, ('dp', 'group'))
- head_first_new: float32 [512, 41], P(('dp', 'group'))
- input_second_new: float32 [602, 512], P(None, ('dp', 'group'))
- pair_second_new: float32 [3, 512, 1024], P(None, None, ('dp', 'group'))
- proj_second_new: float32 [3, 1024, 512], P(None, ('dp', 'group'))
- head_second_new: float32 [512, 41], P(('dp', 'group'))
- input_copy: bfloat16 [602, 512], P(None, ('dp', 'group'))
- pair_copy: bfloat16 [3, 512, 1024], P(None, None, ('dp', 'group'))
- proj_copy: bfloat16 [3, 1024, 512], P(None, ('dp', 'group'))
- head_copy: bfloat16 [512, 41], P(('dp', 'group'))
The draws below stay inside these ranges and needn't reach their ends.
Inputs may be any that keep to these rules, and one draw needn't show every extreme that they name: `node_counts`: each subgraph's counts are a random base of 1 to 8 times a factor of 1 to 3 that grows with the subgraph's index along dp, times another of 1 to 3 that grows with its index along group. `live_nodes`: some subgraph has exactly 2048 real nodes and some exactly (4096) // 3.
All inputs are finite; a program needn't handle non-finite values.
Results may differ from the reference program's by a relative error of at most 0.0049.
The reference program's roundings to bfloat16 on the way count: a program that leaves them out, or rounds other values in their place, can miss the bound.
Values may be sent and summed in bfloat16 or wider, within the bound.
A program may use at most 192 MiB of HBM per device.

```python
import math
import jax
import jax.numpy as jnp
from jax import lax

D = 512
F = 602
C = 41
LAYERS = 3
DEG = 8
STEP = 5
NODES_DEV = 2048
TOTAL_NODES = 65536
N_DP = 8
N_GROUP = 4


def draw_features(key, part):
    key = jax.random.fold_in(key, 37)
    offset_key, noise_key = jax.random.split(key)
    offset = jax.random.uniform(offset_key, (1, F), jnp.float32, -1.7, 1.7)
    noise = jnp.clip(jax.random.normal(noise_key, (TOTAL_NODES, F), jnp.float32), -5.0, 5.0)
    return (offset + noise).astype(jnp.bfloat16)


def draw_node_counts(key, part):
    key = jax.random.fold_in(key, 11)
    devices = N_DP * N_GROUP
    base = jax.random.randint(key, (NODES_DEV * devices,), 1, 9)
    device = jnp.arange(NODES_DEV * devices, dtype=jnp.int32) // NODES_DEV
    row_rise = 1 + 2 * (device // N_GROUP) // max(N_DP - 1, 1)
    col_rise = 1 + 2 * (device % N_GROUP) // max(N_GROUP - 1, 1)
    return (base * row_rise * col_rise).astype(jnp.int32)


def draw_live_nodes(key, part):
    key = jax.random.fold_in(key, 23)
    devices = N_DP * N_GROUP
    lowest = 2 * NODES_DEV // 3
    first_key, second_key = jax.random.split(key)
    values = jax.random.randint(first_key, (devices,), lowest, NODES_DEV + 1)
    order = jax.random.permutation(second_key, devices)
    values = values.at[order[0]].set(NODES_DEV).at[order[1]].set(lowest)
    return values.astype(jnp.int32)


def place_ends(array, own_key, low, high):
    spot = [jax.random.randint(jax.random.fold_in(own_key, axis), (), 0, length) for axis, length in enumerate(array.shape)]
    longest = array.shape.index(max(array.shape))
    neighbour = spot[:longest] + [(spot[longest] + 1) % array.shape[longest]] + spot[longest + 1:]
    return array.at[tuple(spot)].set(low).at[tuple(neighbour)].set(high)


def block_levels(key, dims, shards, low, largest):
    factor_of, own = 1.0, jax.random.fold_in(key, 6)
    for axis_at, blocks in shards:
        steps = jnp.exp(jax.random.uniform(jax.random.fold_in(own, axis_at), (blocks,), jnp.float32, low / len(shards), largest / len(shards)))
        factor_of = factor_of * jnp.repeat(steps, dims[axis_at] // blocks).reshape([-1 if axis == axis_at else 1 for axis in range(len(dims))])
    return factor_of


def normal_values(key, shape, scale, most, shards=(), held_as=jnp.bfloat16):
    result = jax.random.normal(key, shape, jnp.float32) * scale
    if len(shards) > 0:
        result = block_levels(key, shape, shards, -0.22, 0.18) * result
    return jnp.clip(result, min=-most, max=most).astype(held_as)


def setup_inputs(seed: int = 0) -> dict:
    key_list = jax.random.split(jax.random.key(seed), 20)
    features = draw_features(jax.random.fold_in(key_list[19], 71), 0)
    labels = place_ends(jax.random.randint(key_list[1], (TOTAL_NODES,), 0, C), jax.random.fold_in(key_list[1], 1), 0, C - 1).astype(jnp.int32)
    neighbors = place_ends(jax.random.randint(key_list[2], (TOTAL_NODES, DEG), 0, NODES_DEV), jax.random.fold_in(key_list[2], 1), 0, NODES_DEV - 1).astype(jnp.int32)
    degree = place_ends(jax.random.randint(key_list[3], (TOTAL_NODES,), 1, DEG + 1), jax.random.fold_in(key_list[3], 1), 1, DEG).astype(jnp.int32)
    node_counts = draw_node_counts(jax.random.fold_in(key_list[19], 71), 0)
    edge_counts = place_ends(jax.random.randint(key_list[5], (TOTAL_NODES, DEG), 1, 9), jax.random.fold_in(key_list[5], 1), 1, 8).astype(jnp.int32)
    live_nodes = draw_live_nodes(jax.random.fold_in(key_list[19], 71), 0)
    input_weight = normal_values(key_list[7], (F, D), F ** -0.5, 0.25, ((1, 32),), jnp.float32)
    pair_weight = normal_values(key_list[8], (LAYERS, D, 2 * D), D ** -0.5, 0.25, ((2, 32),), jnp.float32)
    proj_weight = normal_values(key_list[9], (LAYERS, 2 * D, D), (2 * D) ** -0.5, 0.1875, ((1, 32),), jnp.float32)
    head_weight = normal_values(key_list[10], (D, C), D ** -0.5, 0.25, ((0, 32),), jnp.float32)
    input_first = normal_values(key_list[11], (F, D), (0.04 / (NODES_DEV * N_DP * N_GROUP) ** 0.5), 0.0024414062, ((1, 32),), jnp.float32)
    pair_first = normal_values(key_list[12], (LAYERS, D, 2 * D), (0.04 / (NODES_DEV * N_DP * N_GROUP) ** 0.5), 0.0024414062, ((2, 32),), jnp.float32)
    proj_first = normal_values(key_list[13], (LAYERS, 2 * D, D), (0.04 / (NODES_DEV * N_DP * N_GROUP) ** 0.5), 0.0024414062, ((1, 32),), jnp.float32)
    head_first = normal_values(key_list[14], (D, C), (0.15 / (NODES_DEV * N_DP * N_GROUP) ** 0.5), 0.0078125, ((0, 32),), jnp.float32)
    input_second = jnp.clip(jnp.exp(math.log(1.9531249506599124e-07) - 2.0794415 * jax.random.uniform(key_list[15], (F, D), jnp.float32) ** block_levels(key_list[15], (F, D), ((1, 32),), -0.2, 0.2)), 2.4414061883248905e-08, 1.9531249506599124e-07)
    pair_second = jnp.clip(jnp.exp(math.log(1.9531249506599124e-07) - 2.0794415 * jax.random.uniform(key_list[16], (LAYERS, D, 2 * D), jnp.float32) ** block_levels(key_list[16], (LAYERS, D, 2 * D), ((2, 32),), -0.2, 0.2)), 2.4414061883248905e-08, 1.9531249506599124e-07)
    proj_second = jnp.clip(jnp.exp(math.log(1.9531249506599124e-07) - 2.0794415 * jax.random.uniform(key_list[17], (LAYERS, 2 * D, D), jnp.float32) ** block_levels(key_list[17], (LAYERS, 2 * D, D), ((1, 32),), -0.2, 0.2)), 2.4414061883248905e-08, 1.9531249506599124e-07)
    head_second = jnp.clip(jnp.exp(math.log(2.7465821403893642e-06) - 2.0794415 * jax.random.uniform(key_list[18], (D, C), jnp.float32) ** block_levels(key_list[18], (D, C), ((0, 32),), -0.2, 0.2)), 3.4332276754867053e-07, 2.7465821403893642e-06)
    return dict(features=features, labels=labels, neighbors=neighbors, degree=degree, node_counts=node_counts, edge_counts=edge_counts, live_nodes=live_nodes, input_weight=input_weight, pair_weight=pair_weight, proj_weight=proj_weight, head_weight=head_weight, input_first=input_first, pair_first=pair_first, proj_first=proj_first, head_first=head_first, input_second=input_second, pair_second=pair_second, proj_second=proj_second, head_second=head_second)


@jax.custom_vjp
def low(v):
    return lax.optimization_barrier(v.astype(jnp.bfloat16)).astype(jnp.float32)

@jax.custom_vjp
def low_back(v):
    return v

def low_keep(v):
    return (low(v), None)

def low_pass(kept, grad):
    return (grad,)

def back_keep(v):
    return (v, None)

def back_low(kept, grad):
    return (low(grad),)
low.defvjp(low_keep, low_pass)
low_back.defvjp(back_keep, back_low)
learn_rate = 0.03
beta_first = 0.5
beta_second = 0.5
adam_eps = 1e-08
decay_rate = 0.01
norm_eps = 1e-06

def product(left, right):
    return jnp.dot(left, right, precision=lax.Precision.HIGHEST, preferred_element_type=jnp.float32)

def normalize(preact):
    active = jax.nn.gelu(preact)
    return active * lax.rsqrt(lax.optimization_barrier(jnp.mean(active * active, axis=-1, keepdims=True)) + norm_eps)

def slot_terms(neighbors, degree, live_count):
    count_nodes, fanout = neighbors.shape
    node_live = jnp.arange(count_nodes, dtype=jnp.int32) < live_count
    used = (jnp.arange(fanout, dtype=jnp.int32)[None, :] < degree[:, None]) & (neighbors < live_count) & node_live[:, None]
    return (node_live, used)

def coefficients(used, node_counts, edge_counts, total_node, total_edge):
    node_float = node_counts.astype(jnp.float32)
    edge_float = edge_counts.astype(jnp.float32)
    spread = jnp.maximum(lax.optimization_barrier(jnp.sum(used.astype(jnp.float32), axis=1)), 1.0)
    value = node_float[:, None] * total_edge / (edge_float * total_node * spread[:, None])
    return jnp.where(used, value, 0.0)

def loss_weights(node_counts, node_live, total_node, all_nodes):
    return jnp.where(node_live, total_node / (node_counts.astype(jnp.float32) * all_nodes), 0.0)

def forward(params, feats, neighbors, coefs, labels, weights, weight_sum):
    input_w, pair_w, proj_w, head_w = params
    width = pair_w.shape[1]
    hidden = low(low_back(product(feats, input_w)))
    for layer_index in range(pair_w.shape[0]):
        pooled = low(jnp.einsum('nk,nkd->nd', coefs, hidden[neighbors], precision=lax.Precision.HIGHEST))
        joined = jnp.concatenate([product(hidden, pair_w[layer_index][:, :width]), product(pooled, pair_w[layer_index][:, width:])], axis=1)
        joined = low(low_back(joined))
        preact = low_back(product(joined, proj_w[layer_index]))
        hidden = low(normalize(preact))
    logits = low_back(product(hidden, head_w))
    log_total = jax.nn.logsumexp(logits, axis=1)
    picked = jnp.take_along_axis(logits, labels[:, None], axis=1)[:, 0]
    return jnp.sum(weights * (log_total - picked)) / weight_sum

def adamw_update(weight, first, second, grad):
    first_new = beta_first * first + (1.0 - beta_first) * grad
    second_new = beta_second * second + (1.0 - beta_second) * grad * grad
    first_hat = first_new / (1.0 - beta_first ** STEP)
    second_hat = second_new / (1.0 - beta_second ** STEP)
    weight_new = weight - learn_rate * (first_hat / (jnp.sqrt(second_hat) + adam_eps) + decay_rate * weight)
    return (weight_new, first_new, second_new)

def reference(features, labels, neighbors, degree, node_counts, edge_counts, live_nodes, input_weight, pair_weight, proj_weight, head_weight, input_first, pair_first, proj_first, head_first, input_second, pair_second, proj_second, head_second):
    devices = N_DP * N_GROUP
    all_nodes = jnp.float32(NODES_DEV * devices)
    feats = features.reshape(devices, NODES_DEV, F)
    labs = labels.reshape(devices, NODES_DEV)
    nbrs = neighbors.reshape(devices, NODES_DEV, DEG)
    degs = degree.reshape(devices, NODES_DEV)
    node_parts = node_counts.reshape(devices, NODES_DEV)
    edge_parts = edge_counts.reshape(devices, NODES_DEV, DEG)

    def local_totals(inputs):
        nbr, deg, ncount, ecount, live_count = inputs
        node_live, used = slot_terms(nbr, deg, live_count)
        return (jnp.sum(jnp.where(node_live, ncount.astype(jnp.float32), 0.0)), jnp.sum(jnp.where(used, ecount.astype(jnp.float32), 0.0)))
    node_sums, edge_sums = lax.map(local_totals, (nbrs, degs, node_parts, edge_parts, live_nodes))
    total_node = jnp.sum(node_sums)
    total_edge = jnp.sum(edge_sums)

    def device_weights(ncount, live_count):
        node_live = jnp.arange(NODES_DEV, dtype=jnp.int32) < live_count
        return loss_weights(ncount, node_live, total_node, all_nodes)
    weights_all = jax.vmap(device_weights)(node_parts, live_nodes)
    weight_sum = jnp.sum(weights_all)
    masters = (input_weight, pair_weight, proj_weight, head_weight)
    params = tuple((master.astype(jnp.bfloat16).astype(jnp.float32) for master in masters))

    def device_step(carry, inputs):
        feat, lab, nbr, deg, ncount, ecount, live_count, weights = inputs
        node_live, used = slot_terms(nbr, deg, live_count)
        coefs = coefficients(used, ncount, ecount, total_node, total_edge)
        value, pullback = jax.vjp(lambda prm: forward(prm, feat.astype(jnp.float32), nbr, coefs, lab, weights, weight_sum), params)
        grads = pullback(jnp.float32(1.0))[0]
        return ((carry[0] + value, jax.tree.map(lambda total, extra: total + extra, carry[1], grads)), None)
    start = (jnp.float32(0.0), tuple((jnp.zeros_like(master) for master in masters)))
    (mean_loss, grads), _ = lax.scan(device_step, start, (feats, labs, nbrs, degs, node_parts, edge_parts, live_nodes, weights_all))
    firsts = (input_first, pair_first, proj_first, head_first)
    seconds = (input_second, pair_second, proj_second, head_second)
    results = [adamw_update(master, first, second, grad) for master, first, second, grad in zip(masters, firsts, seconds, grads)]
    news = [item[0] for item in results]
    return (mean_loss, weight_sum / all_nodes, news[0], news[1], news[2], news[3], results[0][1], results[1][1], results[2][1], results[3][1], results[0][2], results[1][2], results[2][2], results[3][2], news[0].astype(jnp.bfloat16), news[1].astype(jnp.bfloat16), news[2].astype(jnp.bfloat16), news[3].astype(jnp.bfloat16))
```

```python
import jax
import jax.numpy as jnp
from jax import lax
from jax.experimental import pallas as pl
from jax.experimental.pallas import tpu as pltpu
from jax.sharding import PartitionSpec as P

LAYERS = 3
STEP = 5
COMMON = 840.0

learn_rate = 0.03
beta_first = 0.5
beta_second = 0.5
adam_eps = 1e-08
decay_rate = 0.01
norm_eps = 1e-06

AXES = ("dp", "group")
MESH = pl.DeviceIdType.MESH
f32 = jnp.float32
bf16 = jnp.bfloat16
TILE = 512
ROWS = 64
GELU_IN = 0.7978845608028654
GELU_CUBE = 0.044715


def dot_nn(left, right):
    return jnp.dot(left, right, preferred_element_type=f32)


def dot_nt(left, right):
    return lax.dot_general(left, right, (((1,), (1,)), ((), ())), preferred_element_type=f32)


def adamw_update(weight, first, second, grad):
    first_new = beta_first * first + (1.0 - beta_first) * grad
    second_new = beta_second * second + (1.0 - beta_second) * grad * grad
    first_hat = first_new / (1.0 - beta_first**STEP)
    second_hat = second_new / (1.0 - beta_second**STEP)
    weight_new = weight - learn_rate * (
        first_hat / (jnp.sqrt(second_hat) + adam_eps) + decay_rate * weight
    )
    return (weight_new, first_new, second_new)


class Place:
    def __init__(self):
        dp, group = lax.axis_index("dp"), lax.axis_index("group")
        self.z, self.y = dp // 2, dp % 2
        self.x, self.c = group // 2, group % 2
        self.far_y, self.far_x, self.far_c = 1 - self.y, 1 - self.x, 1 - self.c
        self.sibling = (dp, group + 1 - 2 * self.c)
        self.beside_x = (dp, group + 2 - 4 * self.x)
        self.beside_y = (dp + 1 - 2 * self.y, group)
        self.later_z = [(self.z + step) % 4 for step in (1, 2, 3)]
        self.earlier_z = [(self.z + 4 - step) % 4 for step in (1, 2, 3)]
        self.to_z = [(at * 2 + self.y, group) for at in self.later_z]
        self.from_z = [(at * 2 + self.y, group) for at in self.earlier_z]

    def partners(self):
        return [self.sibling, self.beside_x, self.beside_y] + self.to_z


class Wire:
    def __init__(self, send_sems, recv_sems):
        self.send_sems, self.recv_sems = send_sems, recv_sems
        self.sent = []

    def copy(self, at, source, target, device):
        return pltpu.make_async_remote_copy(
            src_ref=source(),
            dst_ref=target(),
            send_sem=self.send_sems.at[at],
            recv_sem=self.recv_sems.at[at],
            device_id=device,
            device_id_type=MESH,
        )

    def send(self, at, source, target, device):
        self.copy(at, source, target, device).start()
        self.sent.append((at, source, target, device))

    def arrived(self, at, target, device):
        self.copy(at, target, target, device).wait_recv()

    def finish(self):
        for sent in self.sent:
            self.copy(*sent).wait_send()
        self.sent = []


def gather_steps(place, wire, region):
    z, y, x, c = place.z, place.y, place.x, place.c
    fy, fx, fc = place.far_y, place.far_x, place.far_c
    whole, low, high = slice(0, 4), slice(0, 2), slice(2, 4)

    def at(*index):
        return lambda: region(*index)

    def send(sem, index, device):
        wire.send(sem, at(*index), at(*index), device)

    for step in range(3):
        send(step, (z, y, x, c), place.to_z[step])
    yield
    for step in range(3):
        wire.arrived(step, at(place.earlier_z[step], y, x, c), place.from_z[step])
    send(3, (whole, y, x, c), place.beside_x)
    send(4, (whole, y, x, c), place.beside_y)
    send(5, (whole, y, x, c), place.sibling)
    yield
    wire.arrived(3, at(whole, y, fx, c), place.beside_x)
    send(6, (low, y, fx, c), place.beside_y)
    send(8, (whole, y, fx, c), place.sibling)
    wire.arrived(4, at(whole, fy, x, c), place.beside_y)
    send(7, (high, fy, x, c), place.beside_x)
    send(9, (whole, fy, x, c), place.sibling)
    yield
    wire.arrived(6, at(low, fy, fx, c), place.beside_y)
    wire.arrived(7, at(high, fy, fx, c), place.beside_x)
    send(10, (whole, fy, fx, c), place.sibling)
    yield
    wire.arrived(5, at(whole, y, x, fc), place.sibling)
    wire.arrived(8, at(whole, y, fx, fc), place.sibling)
    wire.arrived(9, at(whole, fy, x, fc), place.sibling)
    wire.arrived(10, at(whole, fy, fx, fc), place.sibling)
    yield


def scatter_steps(place, wire, bufs, slot, store):
    grads, from_core, out_half, in_half, out_col, in_col, out_z, in_z = bufs
    z, y, x, c = place.z, place.y, place.x, place.c
    fy, fx, fc = place.far_y, place.far_x, place.far_c
    low, high = slice(0, 2), slice(2, 4)

    def at(buf, *index):
        return lambda: buf.at[(slot, *index)]

    def both(zs, yy, xx):
        return grads[slot, zs, yy, xx, c].astype(f32) + from_core[slot, zs, yy, xx].astype(f32)

    wire.send(0, at(grads, slice(0, 4), slice(0, 2), slice(0, 2), fc), at(from_core), place.sibling)
    yield
    wire.arrived(0, at(from_core), place.sibling)
    out_half[slot, 0] = both(low, fy, fx).astype(bf16)
    wire.send(1, at(out_half, 0), at(in_half, 0), place.beside_x)
    out_half[slot, 1] = both(high, fy, fx).astype(bf16)
    wire.send(2, at(out_half, 1), at(in_half, 1), place.beside_y)
    yield
    wire.arrived(1, at(in_half, 0), place.beside_x)
    out_col[slot, 1, low] = (both(low, fy, x) + in_half[slot, 0].astype(f32)).astype(bf16)
    out_col[slot, 1, high] = both(high, fy, x).astype(bf16)
    wire.send(4, at(out_col, 1), at(in_col, 1), place.beside_y)
    wire.arrived(2, at(in_half, 1), place.beside_y)
    out_col[slot, 0, low] = both(low, y, fx).astype(bf16)
    out_col[slot, 0, high] = (both(high, y, fx) + in_half[slot, 1].astype(f32)).astype(bf16)
    wire.send(3, at(out_col, 0), at(in_col, 0), place.beside_x)
    yield
    wire.arrived(3, at(in_col, 0), place.beside_x)
    wire.arrived(4, at(in_col, 1), place.beside_y)

    def column(zz):
        beside = in_col[slot, 0, zz].astype(f32) + in_col[slot, 1, zz].astype(f32)
        return both(zz, y, x) + beside

    for step in range(3):
        out_z[slot, step] = column(place.later_z[step]).astype(bf16)
        wire.send(5 + step, at(out_z, step), at(in_z, step), place.to_z[step])
    yield
    for step in range(3):
        wire.arrived(5 + step, at(in_z, step), place.from_z[step])
    others = in_z[slot, 0].astype(f32) + in_z[slot, 1].astype(f32) + in_z[slot, 2].astype(f32)
    store(column(z) + others)
    wire.finish()
    yield


def sum_steps(place, wire, bufs, slot, store):
    out, arrive, line = bufs

    def at(buf, *index):
        return lambda: buf.at[(slot, *index)]

    for stage, device in enumerate((place.sibling, place.beside_x, place.beside_y)):
        wire.send(stage, at(out, stage), at(arrive, stage), device)
        yield
        wire.arrived(stage, at(arrive, stage), device)
        if stage < 2:
            out[slot, stage + 1] = out[slot, stage] + arrive[slot, stage]
        else:
            line[slot, place.z] = out[slot, stage] + arrive[slot, stage]
    for step in range(3):
        wire.send(3 + step, at(line, place.z), at(line, place.z), place.to_z[step])
    yield
    for step in range(3):
        wire.arrived(3 + step, at(line, place.earlier_z[step]), place.from_z[step])
    store((line[slot, 0] + line[slot, 1]) + (line[slot, 2] + line[slot, 3]))
    wire.finish()
    yield


def step(*generators):
    for generator in generators:
        next(generator)


def row_of_scalars(values):
    rows = lax.broadcasted_iota(jnp.int32, (8, 128), 0)
    block = jnp.zeros((8, 128), f32)
    for at, value in enumerate(values):
        block = jnp.where(rows == at, value, block)
    return block


def gelu(pre):
    bend = jnp.tanh(GELU_IN * (pre + GELU_CUBE * (pre * pre * pre)))
    return 0.5 * pre * (1.0 + bend), bend


def lane_chunks(tile):
    for at in range(0, TILE, 128):
        yield pl.ds(tile + at, 128), slice(at, at + 128)


def row_chunks():
    return [slice(at, at + ROWS) for at in range(0, 512, ROWS)]


def norm_forward(pre, active, out, at_pre, at_out):
    for (lanes, _), (to_lanes, _) in zip(lane_chunks(at_pre), lane_chunks(at_out)):
        square = jnp.zeros((ROWS, 128), f32)
        for row in row_chunks():
            value, _ = gelu(pre[row, lanes])
            active[row, :] = value
            square = square + value * value
        square = jnp.sum(square, axis=0, keepdims=True)
        scale = lax.rsqrt(square * (1.0 / 512) + norm_eps)
        for row in row_chunks():
            out[row, to_lanes] = (active[row, :] * scale).astype(bf16)


def norm_backward(grad, pre, active, slope, out, at_pre, at_out):
    for (lanes, inside), (to_lanes, _) in zip(lane_chunks(at_pre), lane_chunks(at_out)):
        square = jnp.zeros((ROWS, 128), f32)
        along = jnp.zeros((ROWS, 128), f32)
        for row in row_chunks():
            at = pre[row, lanes]
            value, bend = gelu(at)
            active[row, :] = value
            slope[row, :] = 0.5 * (1.0 + bend) + (0.5 * GELU_IN) * at * (1.0 - bend * bend) * (
                1.0 + (3.0 * GELU_CUBE) * (at * at)
            )
            square = square + value * value
            along = along + value * grad[row, inside]
        square = jnp.sum(square, axis=0, keepdims=True)
        along = jnp.sum(along, axis=0, keepdims=True) * (1.0 / 512)
        scale = lax.rsqrt(square * (1.0 / 512) + norm_eps)
        pull = scale * scale * scale * along
        for row in row_chunks():
            out[row, to_lanes] = (
                slope[row, :] * (scale * grad[row, inside] - active[row, :] * pull)
            ).astype(bf16)


def ticks(at, plan):
    for when, generators in plan.items():

        @pl.when(at == when)
        def _(generators=generators):
            step(*generators)


def train_kernel(
    feat_hbm, nbr, edge, degree, counts, labels, live, win_own, pair_own, proj_own, head_own,
    gin_out, gpair_out, gproj_out, ghead_out, scal_out,
    matrix, feat, hid_0, hid_1, hid_2, pool_0, pool_1, pool_2, join_0, join_1, join_2, pre_0, pre_1,
    win, weights, head, turned, head_grad, scale, inverse, terms, totals, losses,
    back, top_pre, last, active, slope,
    big_g, big_rc, big_oh, big_ih, big_ocol, big_icol, big_oz, big_iz,
    in_g, in_rc, in_oh, in_ih, in_ocol, in_icol, in_oz, in_iz,
    hd_g, hd_rc, hd_oh, hd_ih, hd_ocol, hd_icol, hd_oz, hd_iz,
    sum_out, sum_in, sum_line,
    gather_send, gather_recv, scatter_send, scatter_recv, sum_send, sum_recv, feat_sem,
):
    place = Place()
    z, y, x, c = place.z, place.y, place.x, place.c
    nodes, width, classes = nbr.shape[1], hid_0.shape[0], head_own.shape[1]
    steps = nodes // TILE
    hidden, pooled, joined, pre = (
        [hid_0, hid_1, hid_2], [pool_0, pool_1, pool_2], [join_0, join_1, join_2], [pre_0, pre_1],
    )
    top = LAYERS - 1

    barrier = pltpu.get_barrier_semaphore()
    for partner in place.partners():
        pl.semaphore_signal(barrier, inc=1, device_id=partner, device_id_type=MESH)

    feat_copy = pltpu.make_async_copy(feat_hbm, feat, feat_sem)
    feat_copy.start()
    win[z, y, x, c] = win_own[...].astype(bf16)
    for layer in range(LAYERS):
        weights[layer, 0, z, y, x, c] = pair_own[layer].astype(bf16)
        weights[layer, 1, z, y, x, c] = proj_own[layer].astype(bf16)
    head[z, y, x, c] = jnp.zeros(head.shape[4:], bf16)
    head[z, y, x, c, :, 0:classes] = head_own[...].astype(bf16)

    pl.semaphore_wait(barrier, 6)

    regions = [
        lambda zz, yy, xx, cc: win.at[zz, yy, xx, cc],
        lambda zz, yy, xx, cc: weights.at[0, 0, zz, yy, xx, cc],
        lambda zz, yy, xx, cc: weights.at[0, 1, zz, yy, xx, cc],
        lambda zz, yy, xx, cc: weights.at[1, :, zz, yy, xx, cc],
        lambda zz, yy, xx, cc: weights.at[2, :, zz, yy, xx, cc],
        lambda zz, yy, xx, cc: head.at[zz, yy, xx, cc],
    ]
    gather_wires = [Wire(gather_send.at[at], gather_recv.at[at]) for at in range(len(regions))]
    ga = [gather_steps(place, wire, region) for wire, region in zip(gather_wires, regions)]
    step(*ga)

    node_live = lax.broadcasted_iota(jnp.int32, (1, nodes), 1) < live[...]
    slot = lax.broadcasted_iota(jnp.int32, nbr.shape, 0)
    used = (slot < degree[...]) & (nbr[...] < live[...]) & node_live
    edge_float = edge[...].astype(f32)
    count_float = counts[...].astype(f32)
    spread = jnp.maximum(jnp.sum(used.astype(f32), axis=0, keepdims=True), 1.0)
    inverse[...] = jnp.where(node_live, 1.0 / count_float, 0.0)
    scale[...] = count_float / (spread * COMMON)
    sum_out[0, 0] = row_of_scalars(
        [
            jnp.sum(jnp.where(node_live, count_float, 0.0)),
            jnp.sum(jnp.where(used, edge_float, 0.0)),
            jnp.sum(inverse[...]),
        ]
    )

    def keep_totals(block):
        totals[...] = block

    total_steps = sum_steps(
        place, Wire(sum_send.at[0], sum_recv.at[0]), (sum_out, sum_in, sum_line), 0, keep_totals
    )
    step(total_steps)

    term = jnp.where(used, COMMON / edge_float, 0.0)
    summed = jnp.zeros(nbr.shape, f32)
    for k in range(nbr.shape[0]):
        summed = summed + jnp.where(nbr[k : k + 1, :] == nbr[...], term[k : k + 1, :], 0.0)
    terms[...] = summed

    @pl.loop(0, nodes // 256)
    def _(block_at):
        lanes = pl.ds(pl.multiple_of(block_at * 256, 256), 256)
        ids = [jnp.broadcast_to(nbr[k : k + 1, lanes], (16, 256)).astype(jnp.int16) for k in range(8)]
        values = [jnp.broadcast_to(terms[k : k + 1, lanes], (16, 256)).astype(bf16) for k in range(8)]

        @pl.loop(0, nodes // 64)
        def _(at):
            for part in range(4):
                row = pl.multiple_of(at * 64 + part * 16, 16)
                own = (lax.broadcasted_iota(jnp.int32, (16, 256), 0) + row).astype(jnp.int16)
                block = jnp.zeros((16, 256), bf16)
                for k in range(8):
                    block = jnp.where(ids[k] == own, values[k], block)
                matrix[pl.ds(row, 16), lanes] = block

        ticks(
            block_at,
            {
                0: [total_steps],
                1: [ga[0], ga[1], total_steps],
                2: [ga[2]],
                3: [ga[0], ga[1], total_steps],
                4: [ga[3], ga[2]],
                5: [ga[0], ga[1], total_steps],
                6: [ga[4], ga[3], ga[2]],
                7: [ga[0], ga[5]],
            },
        )

    scale[...] = scale[...] * (totals[1:2, 0:1] / totals[0:1, 0:1])
    feat_copy.wait()

    def tile_at(at):
        return pl.multiple_of(at * TILE, TILE)

    @pl.loop(0, steps)
    def _(at):
        tile = pl.ds(tile_at(at), TILE)
        hid_0[:, tile] = dot_nn(win[...].reshape(width, -1), feat[:, tile]).astype(bf16)

    def pair_of(layer):
        return weights[layer, 0].reshape(2 * width, width)

    def proj_of(layer):
        return weights[layer, 1].reshape(2 * width, width)

    def layer_tile(layer, tile):
        pooled[layer][:, tile] = (
            dot_nn(hidden[layer][...], matrix[:, tile]) * scale[:, tile]
        ).astype(bf16)
        pair = pair_of(layer)
        joined[layer][0:width, tile] = dot_nn(pair[:width], hidden[layer][:, tile]).astype(bf16)
        joined[layer][width:, tile] = dot_nn(pair[width:], pooled[layer][:, tile]).astype(bf16)
        return dot_nn(turned[...], joined[layer][:, tile])

    forward_ticks = [
        {0: [ga[3], ga[4], ga[5]], 1: [ga[3]], 2: [ga[4], ga[5]]},
        {3: [ga[4], ga[5]]},
    ]
    step(ga[1], ga[2])
    for layer in range(LAYERS - 1):
        turned[...] = proj_of(layer).T

        @pl.loop(0, steps)
        def _(at, layer=layer):
            before = tile_at(jnp.maximum(at - 1, 0))
            norm_forward(pre[layer], active, hidden[layer + 1], before, before)
            tile = pl.ds(tile_at(at), TILE)
            pre[layer][:, tile] = layer_tile(layer, tile)
            ticks(at, forward_ticks[layer])

        final = tile_at(steps - 1)
        norm_forward(pre[layer], active, hidden[layer + 1], final, final)

    turned[...] = proj_of(top).T
    head_grad[...] = jnp.zeros_like(head_grad)
    losses[...] = jnp.zeros_like(losses)
    class_row = lax.broadcasted_iota(jnp.int32, (48, TILE), 0)

    def loss_tile(at):
        start = tile_at(at)
        tile = pl.ds(start, TILE)
        head_rows = head[...].reshape(width, 128)
        norm_forward(top_pre, active, last, 0, 0)
        logits = jnp.where(class_row < classes, dot_nn(head_rows.T[0:48], last[...]), -1e30)
        most = jnp.max(logits, axis=0, keepdims=True)
        log_total = jnp.log(jnp.sum(jnp.exp(logits - most), axis=0, keepdims=True)) + most
        target = class_row == labels[:, tile]
        picked = jnp.sum(jnp.where(target, logits, 0.0), axis=0, keepdims=True)
        loss = jnp.sum(inverse[:, tile] * (log_total - picked), axis=1, keepdims=True)
        losses[...] = losses[...] + loss
        weight = inverse[:, tile] / totals[2:3, 0:1]
        grad_logits = (weight * (jnp.exp(logits - log_total) - target.astype(f32))).astype(bf16)
        grad_logits = jnp.concatenate([grad_logits, jnp.zeros((80, TILE), bf16)], axis=0)
        head_grad[...] = head_grad[...] + dot_nt(last[...], grad_logits)
        back[...] = dot_nn(head_rows, grad_logits)
        norm_backward(back, top_pre, active, slope, feat, 0, start)

    @pl.loop(0, steps)
    def _(at):
        top_pre[...] = layer_tile(top, pl.ds(tile_at(at), TILE))
        loss_tile(at)

    hd_g[0] = head_grad[...].astype(bf16).reshape(hd_g.shape[1:])
    sum_out[1, 0] = jnp.broadcast_to(losses[0:1, 0:1], (8, 128))

    def keep_loss(block):
        rows = lax.broadcasted_iota(jnp.int32, (8, 128), 0)
        all_nodes = float(nodes * 32)
        weight_mean = (totals[0:1, :] * totals[2:3, :]) / (all_nodes * all_nodes)
        scal_out[...] = jnp.where(rows == 0, block / totals[2:3, :], weight_mean)

    loss_steps = sum_steps(
        place, Wire(sum_send.at[1], sum_recv.at[1]), (sum_out, sum_in, sum_line), 1, keep_loss
    )

    def keep_head(value):
        ghead_out[...] = value[:, 0:classes]

    head_steps = scatter_steps(
        place, Wire(scatter_send.at[0], scatter_recv.at[0]),
        (hd_g, hd_rc, hd_oh, hd_ih, hd_ocol, hd_icol, hd_oz, hd_iz), 0, keep_head,
    )
    step(loss_steps, head_steps)

    def big_steps(chunk, slot, target, layer):
        def keep(value):
            target[layer] = value

        return scatter_steps(
            place, Wire(scatter_send.at[chunk], scatter_recv.at[chunk]),
            (big_g, big_rc, big_oh, big_ih, big_ocol, big_icol, big_oz, big_iz), slot, keep,
        )

    def grad_block(slot, at, left, right):
        rows = pl.ds(pl.multiple_of(at * 256, 256), 256)
        big_g[slot, at] = dot_nt(left[rows, :], right).astype(bf16).reshape(big_g.shape[2:])

    for layer in reversed(range(LAYERS)):
        chunk = 1 + 2 * (top - layer)
        grad = feat.at[0:width] if layer == top else hidden[layer + 1]
        beside = [loss_steps, head_steps] if layer == top else []

        @pl.loop(0, 4)
        def _(at, layer=layer, grad=grad):
            grad_block(0, at, joined[layer], grad[...])

        proj_steps = big_steps(chunk, 0, gproj_out, layer)
        step(proj_steps, *beside)

        @pl.loop(0, steps)
        def _(at, layer=layer, grad=grad, proj_steps=proj_steps, beside=beside):
            tile = pl.ds(tile_at(at), TILE)
            joined[layer][:, tile] = dot_nn(proj_of(layer), grad[:, tile]).astype(bf16)
            ticks(at, {1: [proj_steps] + beside, 3: [proj_steps] + beside})

        if layer == top:
            feat_copy = pltpu.make_async_copy(feat_hbm, feat, feat_sem)
            feat_copy.start()

        @pl.loop(0, 2)
        def _(at, layer=layer):
            grad_block(1, at, joined[layer], hidden[layer][...])

        step(proj_steps, *beside)

        @pl.loop(2, 4)
        def _(at, layer=layer):
            grad_block(1, at, joined[layer], pooled[layer][...])

        step(proj_steps)
        pair_steps = big_steps(chunk + 1, 1, gpair_out, layer)
        step(pair_steps)
        turned[...] = pair_of(layer).T

        @pl.loop(0, steps)
        def _(at, layer=layer):
            tile = pl.ds(tile_at(at), TILE)
            pooled[layer][:, tile] = (
                dot_nn(turned[:, width:], joined[layer][width:, tile]) * scale[:, tile]
            ).astype(bf16)

        step(pair_steps)

        @pl.loop(0, steps)
        def _(at, layer=layer, pair_steps=pair_steps):
            before = tile_at(jnp.maximum(at - 1, 0))
            if layer > 0:
                norm_backward(back, pre[layer - 1], active, slope, hidden[layer], before, before)
            tile = pl.ds(tile_at(at), TILE)
            value = dot_nn(turned[:, :width], joined[layer][:width, tile]) + dot_nt(
                pooled[layer][...], matrix[tile, :]
            )
            if layer > 0:
                back[...] = value
            else:
                hidden[layer][:, tile] = value.astype(bf16)
            ticks(at, {0: [pair_steps], 1: [pair_steps], 2: [pair_steps]})

        if layer > 0:
            final = tile_at(steps - 1)
            norm_backward(back, pre[layer - 1], active, slope, hidden[layer], final, final)

    feat_copy.wait()
    rows_in = width // 4

    @pl.loop(0, 4)
    def _(at):
        rows = pl.ds(pl.multiple_of(at * rows_in, rows_in), rows_in)
        in_g[0, at] = dot_nt(hid_0[rows, :], feat[...]).astype(bf16).reshape(in_g.shape[2:])

    def keep_in(value):
        gin_out[...] = value

    in_steps = scatter_steps(
        place, Wire(scatter_send.at[7], scatter_recv.at[7]),
        (in_g, in_rc, in_oh, in_ih, in_ocol, in_icol, in_oz, in_iz), 0, keep_in,
    )
    for _ in in_steps:
        pass
    for wire in gather_wires:
        wire.finish()


def scatter_buffers(rows, columns, slots):
    def buf(*shape):
        return pltpu.VMEM((slots, *shape, rows, columns), bf16)

    return [
        buf(4, 2, 2, 2), buf(4, 2, 2), buf(2, 2), buf(2, 2), buf(2, 4), buf(2, 4), buf(3), buf(3),
    ]


def train(feat, nbr, edge, degree, counts, labels, live, win, pair, proj, head):
    features, nodes = feat.shape
    width = pair.shape[2]
    classes = head.shape[1]
    vmem = pl.BlockSpec(memory_space=pltpu.VMEM)
    dma = pltpu.SemaphoreType.DMA
    return pl.pallas_call(
        train_kernel,
        out_shape=[
            jax.ShapeDtypeStruct(win.shape, f32),
            jax.ShapeDtypeStruct(pair.shape, f32),
            jax.ShapeDtypeStruct(proj.shape, f32),
            jax.ShapeDtypeStruct(head.shape, f32),
            jax.ShapeDtypeStruct((8, 128), f32),
        ],
        in_specs=[pl.BlockSpec(memory_space=pl.ANY)] + [vmem] * 10,
        out_specs=[vmem] * 5,
        scratch_shapes=[
            pltpu.VMEM((nodes, nodes), bf16),
            pltpu.VMEM((features, nodes), bf16),
        ]
        + [pltpu.VMEM((width, nodes), bf16)] * 3
        + [pltpu.VMEM((width, nodes), bf16)] * 3
        + [pltpu.VMEM((2 * width, nodes), bf16)] * 3
        + [pltpu.VMEM((width, nodes), f32)] * 2
        + [
            pltpu.VMEM((4, 2, 2, 2, 16, features), bf16),
            pltpu.VMEM((LAYERS, 2, 4, 2, 2, 2, 32, width), bf16),
            pltpu.VMEM((4, 2, 2, 2, 16, 128), bf16),
            pltpu.VMEM((width, 2 * width), bf16),
            pltpu.VMEM((width, 128), f32),
            pltpu.VMEM((1, nodes), f32),
            pltpu.VMEM((1, nodes), f32),
            pltpu.VMEM((8, nodes), f32),
            pltpu.VMEM((8, 128), f32),
            pltpu.VMEM((8, 128), f32),
            pltpu.VMEM((width, TILE), f32),
            pltpu.VMEM((width, TILE), f32),
            pltpu.VMEM((width, TILE), bf16),
            pltpu.VMEM((width, 128), f32),
            pltpu.VMEM((width, 128), f32),
        ]
        + scatter_buffers(32, width, 2)
        + scatter_buffers(16, features, 1)
        + scatter_buffers(16, 128, 1)
        + [
            pltpu.VMEM((2, 3, 8, 128), f32),
            pltpu.VMEM((2, 3, 8, 128), f32),
            pltpu.VMEM((2, 4, 8, 128), f32),
            dma((6, 11)), dma((6, 11)), dma((8, 8)), dma((8, 8)), dma((2, 6)), dma((2, 6)), dma,
        ],
        compiler_params=pltpu.CompilerParams(
            collective_id=0, has_side_effects=True, vmem_limit_bytes=64 * 2**20
        ),
        cost_estimate=pl.CostEstimate(
            flops=67 * 10**9, bytes_accessed=10**7, transcendentals=10**7
        ),
    )(feat, nbr, edge, degree, counts, labels, live, win, pair, proj, head)


def update_kernel(*refs):
    inputs, outs = refs[:16], refs[16:]
    for at in range(4):
        weight, first, second, grad = (inputs[at + 4 * kind][...] for kind in range(4))
        new, first_new, second_new = adamw_update(weight, first, second, grad)
        outs[at][...] = new
        outs[4 + at][...] = first_new
        outs[8 + at][...] = second_new
        outs[12 + at][...] = new.astype(bf16)


def update(weights, firsts, seconds, grads):
    shapes = [jax.ShapeDtypeStruct(w.shape, f32) for w in weights]
    vmem = pl.BlockSpec(memory_space=pltpu.VMEM)
    return pl.pallas_call(
        update_kernel,
        out_shape=shapes * 3 + [jax.ShapeDtypeStruct(w.shape, bf16) for w in weights],
        in_specs=[vmem] * 16,
        out_specs=[vmem] * 16,
    )(*weights, *firsts, *seconds, *grads)


def turned_first(array):
    return jnp.swapaxes(array, -1, -2)


def body(
    features, labels, neighbors, degree, node_counts, edge_counts, live_nodes,
    input_weight, pair_weight, proj_weight, head_weight,
    input_first, pair_first, proj_first, head_first,
    input_second, pair_second, proj_second, head_second,
):
    def owned(input_w, pair_w, proj_w, head_w):
        return (turned_first(input_w), turned_first(pair_w), proj_w, head_w)

    weights = owned(input_weight, pair_weight, proj_weight, head_weight)
    *grads, scalars = train(
        turned_first(features), turned_first(neighbors), turned_first(edge_counts),
        degree[None, :], node_counts[None, :], labels[None, :], live_nodes[None, :], *weights,
    )
    results = update(
        weights,
        owned(input_first, pair_first, proj_first, head_first),
        owned(input_second, pair_second, proj_second, head_second),
        grads,
    )
    placed = []
    for kind in range(4):
        placed += owned(*results[4 * kind : 4 * kind + 4])
    return (scalars[0, 0], scalars[1, 0], *placed)


def normalize(preact):
    active = jax.nn.gelu(preact)
    return active * lax.rsqrt(jnp.mean(active * active, axis=-1, keepdims=True) + norm_eps)


def slot_terms(neighbors, degree, live_count):
    count_nodes, fanout = neighbors.shape
    node_live = jnp.arange(count_nodes, dtype=jnp.int32) < live_count
    used = (
        (jnp.arange(fanout, dtype=jnp.int32)[None, :] < degree[:, None])
        & (neighbors < live_count)
        & node_live[:, None]
    )
    return (node_live, used)


def coefficients(used, node_counts, edge_counts, total_node, total_edge):
    node_float = node_counts.astype(jnp.float32)
    edge_float = edge_counts.astype(jnp.float32)
    spread = jnp.maximum(jnp.sum(used.astype(jnp.float32), axis=1), 1.0)
    value = node_float[:, None] * total_edge / (edge_float * total_node * spread[:, None])
    return jnp.where(used, value, 0.0)


def contract_rows(left, right):
    return lax.dot_general(
        left, right, (((0,), (0,)), ((), ())), preferred_element_type=jnp.float32
    )


def contract_cols(left, right):
    return lax.dot_general(
        left, right, (((1,), (1,)), ((), ())), preferred_element_type=jnp.float32
    )


def coef_matrix(neighbors, coefs):
    count_nodes = neighbors.shape[0]
    columns = lax.iota(jnp.int32, count_nodes)[None, :]
    matrix = jnp.zeros((count_nodes, count_nodes), jnp.float32)
    for neighbor_slot in range(neighbors.shape[1]):
        matrix = matrix + jnp.where(
            neighbors[:, neighbor_slot : neighbor_slot + 1] == columns,
            coefs[:, neighbor_slot : neighbor_slot + 1],
            0.0,
        )
    return matrix


def layer_forward(hidden, pair_w, proj_w, matrix):
    width = pair_w.shape[0]
    pooled = jnp.dot(
        matrix,
        hidden.astype(jnp.float32),
        precision=lax.Precision.HIGHEST,
        preferred_element_type=jnp.float32,
    ).astype(jnp.bfloat16)
    self_part = jnp.dot(hidden, pair_w[:, :width], preferred_element_type=jnp.float32)
    nbr_part = jnp.dot(pooled, pair_w[:, width:], preferred_element_type=jnp.float32)
    joined = jnp.concatenate([self_part, nbr_part], axis=1).astype(jnp.bfloat16)
    preact = jnp.dot(joined, proj_w, preferred_element_type=jnp.float32)
    return (normalize(preact).astype(jnp.bfloat16), (hidden, pooled, joined, preact))


def layer_backward(grad_out, saved, pair_w, proj_w, matrix):
    hidden, pooled, joined, preact = saved
    width = pair_w.shape[0]
    _, pullback = jax.vjp(normalize, preact)
    grad_preact = pullback(grad_out)[0].astype(jnp.bfloat16)
    grad_proj = contract_rows(joined, grad_preact)
    grad_joined = contract_cols(grad_preact, proj_w).astype(jnp.bfloat16)
    grad_pair = jnp.concatenate(
        [
            contract_rows(hidden, grad_joined[:, :width]),
            contract_rows(pooled, grad_joined[:, width:]),
        ],
        axis=1,
    )
    grad_hidden = contract_cols(grad_joined[:, :width], pair_w[:, :width])
    grad_pooled = contract_cols(grad_joined[:, width:], pair_w[:, width:])
    grad_hidden = grad_hidden + lax.dot_general(
        matrix,
        grad_pooled,
        (((0,), (0,)), ((), ())),
        precision=lax.Precision.HIGHEST,
        preferred_element_type=jnp.float32,
    )
    return (grad_hidden, grad_pair, grad_proj)


def plain_body(
    features,
    labels,
    neighbors,
    degree,
    node_counts,
    edge_counts,
    live_nodes,
    input_weight,
    pair_weight,
    proj_weight,
    head_weight,
    input_first,
    pair_first,
    proj_first,
    head_first,
    input_second,
    pair_second,
    proj_second,
    head_second,
):
    count_nodes = features.shape[0]
    all_nodes = jnp.float32(count_nodes * lax.axis_size(("dp", "group")))
    node_live, used = slot_terms(neighbors, degree, live_nodes[0])
    node_float = node_counts.astype(jnp.float32)
    node_local = jnp.sum(jnp.where(node_live, node_float, 0.0))
    edge_local = jnp.sum(jnp.where(used, edge_counts.astype(jnp.float32), 0.0))
    total_node, total_edge = lax.psum((node_local, edge_local), ("dp", "group"))
    weights = jnp.where(node_live, total_node / (node_float * all_nodes), 0.0)
    coefs = coefficients(used, node_counts, edge_counts, total_node, total_edge)
    matrix = coef_matrix(neighbors, coefs)
    input_b, pair_b, proj_b, head_b = (
        lax.all_gather(input_weight.astype(jnp.bfloat16), ("dp", "group"), axis=1, tiled=True),
        lax.all_gather(pair_weight.astype(jnp.bfloat16), ("dp", "group"), axis=2, tiled=True),
        lax.all_gather(proj_weight.astype(jnp.bfloat16), ("dp", "group"), axis=1, tiled=True),
        lax.all_gather(head_weight.astype(jnp.bfloat16), ("dp", "group"), axis=0, tiled=True),
    )
    hidden = jnp.dot(features, input_b, preferred_element_type=jnp.float32).astype(jnp.bfloat16)
    kept = []
    for layer_index in range(LAYERS):
        hidden, saved = layer_forward(hidden, pair_b[layer_index], proj_b[layer_index], matrix)
        kept.append(saved)
    logits = jnp.dot(hidden, head_b, preferred_element_type=jnp.float32)
    log_total = jax.nn.logsumexp(logits, axis=1)
    targets = (labels[:, None] == lax.iota(jnp.int32, logits.shape[1])[None, :]).astype(jnp.float32)
    loss_local = jnp.sum(weights * (log_total - jnp.sum(logits * targets, axis=1)))
    loss_sum, weight_sum = lax.psum((loss_local, jnp.sum(weights)), ("dp", "group"))
    grad_logits = (
        (weights / weight_sum)[:, None] * (jnp.exp(logits - log_total[:, None]) - targets)
    ).astype(jnp.bfloat16)
    grad_head = contract_rows(hidden, grad_logits)
    grad_hidden = contract_cols(grad_logits, head_b)
    pair_grads = [None] * LAYERS
    proj_grads = [None] * LAYERS
    for layer_index in reversed(range(LAYERS)):
        grad_hidden, grad_pair, grad_proj = layer_backward(
            grad_hidden, kept[layer_index], pair_b[layer_index], proj_b[layer_index], matrix
        )
        pair_grads[layer_index] = grad_pair
        proj_grads[layer_index] = grad_proj
    grad_input = contract_rows(features, grad_hidden.astype(jnp.bfloat16))
    grad_input, grad_pairs, grad_projs, grad_head = (
        lax.psum_scatter(grad_input, ("dp", "group"), scatter_dimension=1, tiled=True),
        lax.psum_scatter(jnp.stack(pair_grads), ("dp", "group"), scatter_dimension=2, tiled=True),
        lax.psum_scatter(jnp.stack(proj_grads), ("dp", "group"), scatter_dimension=1, tiled=True),
        lax.psum_scatter(grad_head, ("dp", "group"), scatter_dimension=0, tiled=True),
    )
    input_new, input_first_new, input_second_new = adamw_update(
        input_weight, input_first, input_second, grad_input
    )
    pair_new, pair_first_new, pair_second_new = adamw_update(
        pair_weight, pair_first, pair_second, grad_pairs
    )
    proj_new, proj_first_new, proj_second_new = adamw_update(
        proj_weight, proj_first, proj_second, grad_projs
    )
    head_new, head_first_new, head_second_new = adamw_update(
        head_weight, head_first, head_second, grad_head
    )
    return (
        loss_sum / weight_sum,
        weight_sum / all_nodes,
        input_new,
        pair_new,
        proj_new,
        head_new,
        input_first_new,
        pair_first_new,
        proj_first_new,
        head_first_new,
        input_second_new,
        pair_second_new,
        proj_second_new,
        head_second_new,
        input_new.astype(jnp.bfloat16),
        pair_new.astype(jnp.bfloat16),
        proj_new.astype(jnp.bfloat16),
        head_new.astype(jnp.bfloat16),
    )


def solution(mesh):
    placed = (
        P(("dp", "group"), None),
        P(("dp", "group")),
        P(("dp", "group"), None),
        P(("dp", "group")),
        P(("dp", "group")),
        P(("dp", "group"), None),
        P(("dp", "group")),
        P(None, ("dp", "group")),
        P(None, None, ("dp", "group")),
        P(None, ("dp", "group"), None),
        P(("dp", "group"), None),
        P(None, ("dp", "group")),
        P(None, None, ("dp", "group")),
        P(None, ("dp", "group"), None),
        P(("dp", "group"), None),
        P(None, ("dp", "group")),
        P(None, None, ("dp", "group")),
        P(None, ("dp", "group"), None),
        P(("dp", "group"), None),
    )
    fits = dict(mesh.shape) == {"dp": 8, "group": 4}
    return jax.shard_map(
        body if fits else plain_body,
        mesh=mesh,
        in_specs=placed,
        out_specs=(
            P(),
            P(),
            P(None, ("dp", "group")),
            P(None, None, ("dp", "group")),
            P(None, ("dp", "group"), None),
            P(("dp", "group"), None),
            P(None, ("dp", "group")),
            P(None, None, ("dp", "group")),
            P(None, ("dp", "group"), None),
            P(("dp", "group"), None),
            P(None, ("dp", "group")),
            P(None, None, ("dp", "group")),
            P(None, ("dp", "group"), None),
            P(("dp", "group"), None),
            P(None, ("dp", "group")),
            P(None, None, ("dp", "group")),
            P(None, ("dp", "group"), None),
            P(("dp", "group"), None),
        ),
        check_vma=False,
    )
```

```python
import jax
import jax.numpy as jnp
from jax import lax
from jax.experimental import pallas as pl
from jax.experimental.pallas import tpu as pltpu
from jax.sharding import PartitionSpec as P

LAYERS = 3
STEP = 5
COMMON = 840.0

learn_rate = 0.03
beta_first = 0.5
beta_second = 0.5
adam_eps = 1e-08
decay_rate = 0.01
norm_eps = 1e-06

AXES = ("dp", "group")
MESH = pl.DeviceIdType.MESH
f32 = jnp.float32
bf16 = jnp.bfloat16
TILE = 512
WIDE = 1024
ROWS = 64
GATE_IN = 0.7978845608028654
GATE_CUBE = GATE_IN * 0.044715


def dot_nn(left, right):
    return jnp.dot(left, right, preferred_element_type=f32)


def dot_nt(left, right):
    return lax.dot_general(left, right, (((1,), (1,)), ((), ())), preferred_element_type=f32)


def adamw_update(weight, first, second, grad):
    first_new = beta_first * first + (1.0 - beta_first) * grad
    second_new = beta_second * second + (1.0 - beta_second) * grad * grad
    first_hat = first_new / (1.0 - beta_first**STEP)
    second_hat = second_new / (1.0 - beta_second**STEP)
    weight_new = weight - learn_rate * (
        first_hat / (jnp.sqrt(second_hat) + adam_eps) + decay_rate * weight
    )
    return (weight_new, first_new, second_new)


class Place:
    def __init__(self):
        dp, group = lax.axis_index("dp"), lax.axis_index("group")
        self.z, self.y = dp // 2, dp % 2
        self.x, self.c = group // 2, group % 2
        self.far_y, self.far_x, self.far_c = 1 - self.y, 1 - self.x, 1 - self.c
        self.sibling = (dp, group + 1 - 2 * self.c)
        self.beside_x = (dp, group + 2 - 4 * self.x)
        self.beside_y = (dp + 1 - 2 * self.y, group)
        self.later_z = [(self.z + step) % 4 for step in (1, 2, 3)]
        self.earlier_z = [(self.z + 4 - step) % 4 for step in (1, 2, 3)]
        self.to_z = [(at * 2 + self.y, group) for at in self.later_z]
        self.from_z = [(at * 2 + self.y, group) for at in self.earlier_z]

    def partners(self):
        return [self.sibling, self.beside_x, self.beside_y] + self.to_z


class Wire:
    def __init__(self, send_sems, recv_sems):
        self.send_sems, self.recv_sems = send_sems, recv_sems
        self.sent = []

    def copy(self, at, source, target, device):
        return pltpu.make_async_remote_copy(
            src_ref=source(),
            dst_ref=target(),
            send_sem=self.send_sems.at[at],
            recv_sem=self.recv_sems.at[at],
            device_id=device,
            device_id_type=MESH,
        )

    def send(self, at, source, target, device):
        self.copy(at, source, target, device).start()
        self.sent.append((at, source, target, device))

    def arrived(self, at, target, device):
        self.copy(at, target, target, device).wait_recv()

    def finish(self, below=100):
        for sent in self.sent:
            if sent[0] < below:
                self.copy(*sent).wait_send()
        self.sent = [sent for sent in self.sent if sent[0] >= below]


def gather_steps(place, wire, region):
    z, y, x, c = place.z, place.y, place.x, place.c
    fy, fx, fc = place.far_y, place.far_x, place.far_c
    whole, low, high = slice(0, 4), slice(0, 2), slice(2, 4)

    def at(*index):
        return lambda: region(*index)

    def send(sem, index, device):
        wire.send(sem, at(*index), at(*index), device)

    for step in range(3):
        send(step, (z, y, x, c), place.to_z[step])
    yield
    for step in range(3):
        wire.arrived(step, at(place.earlier_z[step], y, x, c), place.from_z[step])
    send(3, (whole, y, x, c), place.beside_x)
    send(4, (whole, y, x, c), place.beside_y)
    send(5, (whole, y, x, c), place.sibling)
    yield
    wire.arrived(3, at(whole, y, fx, c), place.beside_x)
    send(6, (low, y, fx, c), place.beside_y)
    send(8, (whole, y, fx, c), place.sibling)
    wire.arrived(4, at(whole, fy, x, c), place.beside_y)
    send(7, (high, fy, x, c), place.beside_x)
    send(9, (whole, fy, x, c), place.sibling)
    yield
    wire.arrived(6, at(low, fy, fx, c), place.beside_y)
    wire.arrived(7, at(high, fy, fx, c), place.beside_x)
    send(10, (whole, fy, fx, c), place.sibling)
    yield
    wire.arrived(5, at(whole, y, x, fc), place.sibling)
    wire.arrived(8, at(whole, y, fx, fc), place.sibling)
    wire.arrived(9, at(whole, fy, x, fc), place.sibling)
    wire.arrived(10, at(whole, fy, fx, fc), place.sibling)
    yield


def scatter_steps(place, wire, bufs, slot, store, free=None, reuses=False, reused=False):
    grads, from_core, out_half, in_half, out_col, in_col, out_z, in_z, own = bufs
    z, y, x, c = place.z, place.y, place.x, place.c
    fy, fx, fc = place.far_y, place.far_x, place.far_c
    low, high = slice(0, 2), slice(2, 4)

    def at(buf, *index):
        return lambda: buf.at[(slot, *index)]

    def both(zs, yy, xx):
        return grads[slot, zs, yy, xx, c].astype(f32) + from_core[slot, zs, yy, xx].astype(f32)

    def until_free(*partners):
        if reuses:
            for partner in partners:
                pl.semaphore_wait(free.at[slot, partner], 1)

    def set_free(*partners):
        for partner, device in partners:
            pl.semaphore_signal(free.at[slot, partner], inc=1, device_id=device, device_id_type=MESH)

    until_free(0)
    wire.send(0, at(grads, slice(0, 4), slice(0, 2), slice(0, 2), fc), at(from_core), place.sibling)
    yield
    wire.arrived(0, at(from_core), place.sibling)
    until_free(1, 2)
    out_half[slot, 0] = both(low, fy, fx).astype(bf16)
    wire.send(1, at(out_half, 0), at(in_half, 0), place.beside_x)
    out_half[slot, 1] = both(high, fy, fx).astype(bf16)
    wire.send(2, at(out_half, 1), at(in_half, 1), place.beside_y)
    yield
    wire.arrived(1, at(in_half, 0), place.beside_x)
    out_col[slot, 1, low] = (both(low, fy, x) + in_half[slot, 0].astype(f32)).astype(bf16)
    out_col[slot, 1, high] = both(high, fy, x).astype(bf16)
    wire.send(4, at(out_col, 1), at(in_col, 1), place.beside_y)
    wire.arrived(2, at(in_half, 1), place.beside_y)
    out_col[slot, 0, low] = both(low, y, fx).astype(bf16)
    out_col[slot, 0, high] = (both(high, y, fx) + in_half[slot, 1].astype(f32)).astype(bf16)
    wire.send(3, at(out_col, 0), at(in_col, 0), place.beside_x)
    yield
    wire.arrived(3, at(in_col, 0), place.beside_x)
    wire.arrived(4, at(in_col, 1), place.beside_y)

    def column(zz):
        beside = in_col[slot, 0, zz].astype(f32) + in_col[slot, 1, zz].astype(f32)
        return both(zz, y, x) + beside

    until_free(3, 4, 5)
    own[slot] = column(z)
    for step in range(3):
        out_z[slot, step] = column(place.later_z[step]).astype(bf16)
        wire.send(5 + step, at(out_z, step), at(in_z, step), place.to_z[step])
    wire.finish(5)
    if reused:
        set_free((0, place.sibling))
    yield
    for step in range(3):
        wire.arrived(5 + step, at(in_z, step), place.from_z[step])
    others = in_z[slot, 0].astype(f32) + in_z[slot, 1].astype(f32) + in_z[slot, 2].astype(f32)
    store(own[slot] + others)
    wire.finish()
    if reused:
        set_free(*enumerate([place.beside_x, place.beside_y] + place.from_z, 1))
    yield


def sum_steps(place, wire, bufs, slot, store):
    out, arrive, line = bufs

    def at(buf, *index):
        return lambda: buf.at[(slot, *index)]

    for stage, device in enumerate((place.sibling, place.beside_x, place.beside_y)):
        wire.send(stage, at(out, stage), at(arrive, stage), device)
        yield
        wire.arrived(stage, at(arrive, stage), device)
        if stage < 2:
            out[slot, stage + 1] = out[slot, stage] + arrive[slot, stage]
        else:
            line[slot, place.z] = out[slot, stage] + arrive[slot, stage]
    for step in range(3):
        wire.send(3 + step, at(line, place.z), at(line, place.z), place.to_z[step])
    yield
    for step in range(3):
        wire.arrived(3 + step, at(line, place.earlier_z[step]), place.from_z[step])
    store((line[slot, 0] + line[slot, 1]) + (line[slot, 2] + line[slot, 3]))
    wire.finish()
    yield


def step(*generators):
    for generator in generators:
        next(generator)


def row_of_scalars(values):
    rows = lax.broadcasted_iota(jnp.int32, (8, 128), 0)
    block = jnp.zeros((8, 128), f32)
    for at, value in enumerate(values):
        block = jnp.where(rows == at, value, block)
    return block


def gelu(pre):
    square = pre * pre
    gate = 0.5 * jnp.tanh(pre * (GATE_CUBE * square + GATE_IN)) + 0.5
    return pre * gate, gate, square


def row_chunks():
    return [slice(at, at + ROWS) for at in range(0, 512, ROWS)]


def norm_forward(pre, active, scales, out, lanes, scale_lanes):
    square = jnp.zeros((ROWS, 128), f32)
    for row in row_chunks():
        value, _, _ = gelu(pre[row, lanes])
        active[row, :] = value
        square = square + value * value
    scale = lax.rsqrt(jnp.sum(square, axis=0, keepdims=True) * (1.0 / 512) + norm_eps)
    scales[:, scale_lanes] = scale
    for row in row_chunks():
        out[row, lanes] = (active[row, :] * scale).astype(bf16)


def norm_backward(grad, pre, active, slope, scales, out, grad_lanes, pre_lanes, lanes):
    scale = scales[:, lanes]
    along = jnp.zeros((ROWS, 128), f32)
    for row in row_chunks():
        value, gate, square = gelu(pre[row, pre_lanes])
        active[row, :] = value
        slope[row, :] = gate + value * (
            (1.0 - gate) * ((6.0 * GATE_CUBE) * square + 2.0 * GATE_IN)
        )
        along = along + value * grad[row, grad_lanes]
    pull = scale * scale * scale * (jnp.sum(along, axis=0, keepdims=True) * (1.0 / 512))
    for row in row_chunks():
        out[row, lanes] = (
            slope[row, :] * (scale * grad[row, grad_lanes] - active[row, :] * pull)
        ).astype(bf16)


def ticks(at, plan):
    for when, generators in plan.items():

        @pl.when(at == when)
        def _(generators=generators):
            step(*generators)


def train_kernel(
    feat_hbm, nbr, edge, degree, counts, labels, live, win_own, pair_own, proj_own, head_own,
    gin_out, gpair_out, gproj_out, ghead_out, scal_out,
    matrix, feat, hid_0, hid_1, hid_2, pool_0, pool_1, pool_2, join_0, join_1, join_2, pre_0, pre_1,
    win, weights, head, turned, head_grad, scale, inverse, terms, totals, losses, scales,
    back, top_pre, last, active, slope,
    big_g, big_rc, big_oh, big_ih, big_ocol, big_icol, big_oz, big_iz, big_own,
    in_g, in_rc, in_oh, in_ih, in_ocol, in_icol, in_oz, in_iz, in_own,
    hd_g, hd_rc, hd_oh, hd_ih, hd_ocol, hd_icol, hd_oz, hd_iz, hd_own,
    sum_out, sum_in, sum_line,
    gather_send, gather_recv, scatter_send, scatter_recv, sum_send, sum_recv, feat_sem, free,
):
    place = Place()
    z, y, x, c = place.z, place.y, place.x, place.c
    nodes, width, classes = nbr.shape[1], hid_0.shape[0], head_own.shape[1]
    steps, wide_steps, chunks = nodes // TILE, nodes // WIDE, nodes // 128
    hidden, pooled, joined, pre = (
        [hid_0, hid_1, hid_2], [pool_0, pool_1, pool_2], [join_0, join_1, join_2], [pre_0, pre_1],
    )
    top = LAYERS - 1

    barrier = pltpu.get_barrier_semaphore()
    for partner in place.partners():
        pl.semaphore_signal(barrier, inc=1, device_id=partner, device_id_type=MESH)

    feat_copy = pltpu.make_async_copy(feat_hbm, feat, feat_sem)
    feat_copy.start()
    win[z, y, x, c] = win_own[...].astype(bf16)
    for layer in range(LAYERS):
        weights[layer, 0, z, y, x, c] = pair_own[layer].astype(bf16)
        weights[layer, 1, z, y, x, c] = proj_own[layer].astype(bf16)
    head[z, y, x, c] = jnp.zeros(head.shape[4:], bf16)
    head[z, y, x, c, :, 0:classes] = head_own[...].astype(bf16)

    pl.semaphore_wait(barrier, 6)

    def region_of(layer, kind):
        return lambda zz, yy, xx, cc: weights.at[layer, kind, zz, yy, xx, cc]

    regions = (
        [lambda zz, yy, xx, cc: win.at[zz, yy, xx, cc]]
        + [region_of(layer, kind) for layer in range(LAYERS) for kind in range(2)]
        + [lambda zz, yy, xx, cc: head.at[zz, yy, xx, cc]]
    )
    gather_wires = [Wire(gather_send.at[at], gather_recv.at[at]) for at in range(len(regions))]
    ga = [gather_steps(place, wire, region) for wire, region in zip(gather_wires, regions)]
    to_in, to_pair_0, to_proj_0, to_pair_1, to_proj_1, to_pair_2, to_proj_2, to_head = ga
    step(to_in, to_pair_0, to_proj_0, to_pair_1)

    node_live = lax.broadcasted_iota(jnp.int32, (1, nodes), 1) < live[...]
    slot = lax.broadcasted_iota(jnp.int32, nbr.shape, 0)
    used = (slot < degree[...]) & (nbr[...] < live[...]) & node_live
    edge_float = edge[...].astype(f32)
    count_float = counts[...].astype(f32)
    spread = jnp.maximum(jnp.sum(used.astype(f32), axis=0, keepdims=True), 1.0)
    inverse[...] = jnp.where(node_live, 1.0 / count_float, 0.0)
    scale[...] = count_float / (spread * COMMON)
    sum_out[0, 0] = row_of_scalars(
        [
            jnp.sum(jnp.where(node_live, count_float, 0.0)),
            jnp.sum(jnp.where(used, edge_float, 0.0)),
            jnp.sum(inverse[...]),
        ]
    )

    def keep_totals(block):
        totals[...] = block

    total_steps = sum_steps(
        place, Wire(sum_send.at[0], sum_recv.at[0]), (sum_out, sum_in, sum_line), 0, keep_totals
    )
    step(total_steps)

    term = jnp.where(used, COMMON / edge_float, 0.0)
    summed = jnp.zeros(nbr.shape, f32)
    for k in range(nbr.shape[0]):
        summed = summed + jnp.where(nbr[k : k + 1, :] == nbr[...], term[k : k + 1, :], 0.0)
    terms[...] = summed

    @pl.loop(0, nodes // 256)
    def _(block_at):
        lanes = pl.ds(pl.multiple_of(block_at * 256, 256), 256)
        ids = [jnp.broadcast_to(nbr[k : k + 1, lanes], (16, 256)).astype(jnp.int16) for k in range(8)]
        values = [jnp.broadcast_to(terms[k : k + 1, lanes], (16, 256)).astype(bf16) for k in range(8)]

        @pl.loop(0, nodes // 64)
        def _(at):
            for part in range(4):
                row = pl.multiple_of(at * 64 + part * 16, 16)
                own = (lax.broadcasted_iota(jnp.int32, (16, 256), 0) + row).astype(jnp.int16)
                block = jnp.zeros((16, 256), bf16)
                for k in range(8):
                    block = jnp.where(ids[k] == own, values[k], block)
                matrix[pl.ds(row, 16), lanes] = block

        ticks(
            block_at,
            {
                0: [total_steps],
                1: [to_proj_1],
                2: [to_in, total_steps],
                3: [to_pair_2],
                4: [to_proj_2, to_head, total_steps],
                5: [to_pair_0],
                6: [to_in],
                7: [to_proj_0, to_pair_0, to_in, to_pair_1, total_steps, to_in],
            },
        )

    scale[...] = scale[...] * (totals[1:2, 0:1] / totals[0:1, 0:1])
    feat_copy.wait()

    def tile_at(at):
        return pl.multiple_of(at * TILE, TILE)

    def wide(at):
        return pl.ds(pl.multiple_of(at * WIDE, WIDE), WIDE)

    def chunk_at(at, start=0):
        return pl.ds(pl.multiple_of(start + at * 128, 128), 128)

    @pl.loop(0, wide_steps)
    def _(at):
        tile = wide(at)
        hid_0[:, tile] = dot_nn(win[...].reshape(width, -1), feat[:, tile]).astype(bf16)
        ticks(at, {0: [to_proj_0], 1: [to_proj_1, to_pair_0]})

    def pair_of(layer):
        return weights[layer, 0].reshape(2 * width, width)

    def proj_of(layer):
        return weights[layer, 1].reshape(2 * width, width)

    def pool_tile(layer, tile):
        pooled[layer][:, tile] = (
            dot_nn(hidden[layer][...], matrix[:, tile]) * scale[:, tile]
        ).astype(bf16)

    def join_tile(layer, tile):
        pair = pair_of(layer)
        joined[layer][0:width, tile] = dot_nn(pair[:width], hidden[layer][:, tile]).astype(bf16)
        joined[layer][width:, tile] = dot_nn(pair[width:], pooled[layer][:, tile]).astype(bf16)

    pool_ticks = [
        {0: [to_pair_1, to_proj_0, to_pair_2], 1: [to_proj_1, to_pair_0, to_proj_0, to_proj_2]},
        {0: [to_pair_1, to_proj_1], 1: [to_proj_2, to_head]},
        {},
    ]
    join_ticks = [
        {0: [to_pair_1], 1: [to_head]},
        {1: [to_head]},
        {},
    ]
    pre_ticks = [
        {0: [to_proj_1, to_pair_2]},
        {},
    ]
    norm_ticks = [
        {chunks // 2 - 1: [to_pair_2, to_proj_2, to_head]},
        {chunks // 2 - 1: [to_pair_2, to_proj_2]},
    ]

    def pool_and_join(layer):
        @pl.loop(0, wide_steps)
        def _(at):
            pool_tile(layer, wide(at))
            ticks(at, pool_ticks[layer])

        @pl.loop(0, wide_steps)
        def _(at):
            join_tile(layer, wide(at))
            ticks(at, join_ticks[layer])

        turned[...] = proj_of(layer).T

    for layer in range(LAYERS - 1):
        pool_and_join(layer)

        @pl.loop(0, wide_steps)
        def _(at, layer=layer):
            pre[layer][:, wide(at)] = dot_nn(turned[...], joined[layer][:, wide(at)])
            ticks(at, pre_ticks[layer])

        @pl.loop(0, chunks // 2)
        def _(at, layer=layer):
            for part in range(2):
                lanes = chunk_at(at * 2 + part)
                norm_forward(pre[layer], active, scales.at[layer], hidden[layer + 1], lanes, lanes)
            ticks(at, norm_ticks[layer])

    pool_and_join(top)
    head_grad[...] = jnp.zeros_like(head_grad)
    losses[...] = jnp.zeros_like(losses)
    class_row = lax.broadcasted_iota(jnp.int32, (48, TILE), 0)

    def loss_tile(at):
        start = tile_at(at)
        tile = pl.ds(start, TILE)
        head_rows = head[...].reshape(width, 128)
        for part in range(TILE // 128):
            inside = slice(part * 128, part * 128 + 128)
            norm_forward(top_pre, active, scales.at[top], last, inside, chunk_at(part, start))
        logits = jnp.where(class_row < classes, dot_nn(head_rows.T[0:48], last[...]), -1e30)
        most = jnp.max(logits, axis=0, keepdims=True)
        log_total = jnp.log(jnp.sum(jnp.exp(logits - most), axis=0, keepdims=True)) + most
        target = class_row == labels[:, tile]
        picked = jnp.sum(jnp.where(target, logits, 0.0), axis=0, keepdims=True)
        loss = jnp.sum(inverse[:, tile] * (log_total - picked), axis=1, keepdims=True)
        losses[...] = losses[...] + loss
        weight = inverse[:, tile] / totals[2:3, 0:1]
        grad_logits = (weight * (jnp.exp(logits - log_total) - target.astype(f32))).astype(bf16)
        grad_logits = jnp.concatenate([grad_logits, jnp.zeros((80, TILE), bf16)], axis=0)
        head_grad[...] = head_grad[...] + dot_nt(last[...], grad_logits)
        back[...] = dot_nn(head_rows, grad_logits)
        for part in range(TILE // 128):
            inside = slice(part * 128, part * 128 + 128)
            norm_backward(
                back, top_pre, active, slope, scales.at[top], feat.at[0:width], inside, inside, chunk_at(part, start)
            )

    @pl.loop(0, steps)
    def _(at):
        top_pre[...] = dot_nn(turned[...], joined[top][:, pl.ds(tile_at(at), TILE)])
        loss_tile(at)

    hd_g[0] = head_grad[...].astype(bf16).reshape(hd_g.shape[1:])
    sum_out[1, 0] = jnp.broadcast_to(losses[0:1, 0:1], (8, 128))

    def keep_loss(block):
        rows = lax.broadcasted_iota(jnp.int32, (8, 128), 0)
        all_nodes = float(nodes * 32)
        weight_mean = (totals[0:1, :] * totals[2:3, :]) / (all_nodes * all_nodes)
        scal_out[...] = jnp.where(rows == 0, block / totals[2:3, :], weight_mean)

    loss_steps = sum_steps(
        place, Wire(sum_send.at[1], sum_recv.at[1]), (sum_out, sum_in, sum_line), 1, keep_loss
    )

    def keep_head(value):
        ghead_out[...] = value[:, 0:classes]

    head_steps = scatter_steps(
        place, Wire(scatter_send.at[0], scatter_recv.at[0]),
        (hd_g, hd_rc, hd_oh, hd_ih, hd_ocol, hd_icol, hd_oz, hd_iz, hd_own), 0, keep_head,
    )
    step(loss_steps, head_steps)

    def big_steps(chunk, slot, target, layer):
        def keep(value):
            target[layer] = value

        return scatter_steps(
            place, Wire(scatter_send.at[chunk], scatter_recv.at[chunk]),
            (big_g, big_rc, big_oh, big_ih, big_ocol, big_icol, big_oz, big_iz, big_own), slot, keep,
            free=free, reuses=layer < top, reused=layer > 0,
        )

    def grad_block(slot, at, left, right):
        rows = pl.ds(pl.multiple_of(at * 512, 512), 512)
        grad = dot_nt(left[rows, :], right).astype(bf16)
        big_g[slot, pl.ds(at * 2, 2)] = grad.reshape(2, *big_g.shape[2:])

    proj_before, pair_before = [], []
    for layer in reversed(range(LAYERS)):
        chunk = 1 + 2 * (top - layer)
        grad = feat.at[0:width] if layer == top else hidden[layer + 1]
        loss_beside = [loss_steps] if layer == top else []
        head_beside = [head_steps] if layer == top else []

        @pl.loop(0, 2)
        def _(at, layer=layer, grad=grad, plan={0: proj_before + pair_before + loss_beside}):
            grad_block(0, at, joined[layer], grad[...])
            ticks(at, plan)

        proj_steps = big_steps(chunk, 0, gproj_out, layer)
        step(proj_steps, *loss_beside, *head_beside)

        @pl.loop(0, wide_steps)
        def _(at, layer=layer, grad=grad, plan={1: [proj_steps] + pair_before + loss_beside + head_beside}):
            joined[layer][:, wide(at)] = dot_nn(proj_of(layer), grad[:, wide(at)]).astype(bf16)
            ticks(at, plan)

        if layer == top:
            feat_copy = pltpu.make_async_copy(feat_hbm, feat, feat_sem)
            feat_copy.start()

        grad_block(1, 0, joined[layer], hidden[layer][...])
        grad_block(1, 1, joined[layer], pooled[layer][...])
        pair_steps = big_steps(chunk + 1, 1, gpair_out, layer)
        step(pair_steps, proj_steps, *loss_beside, *head_beside)
        turned[...] = pair_of(layer).T

        @pl.loop(0, wide_steps)
        def _(at, layer=layer):
            tile = wide(at)
            pooled[layer][:, tile] = (
                dot_nn(turned[:, width:], joined[layer][width:, tile]) * scale[:, tile]
            ).astype(bf16)

        @pl.loop(0, steps)
        def _(at, layer=layer, plan={0: [pair_steps], 1: [proj_steps] + head_beside, 2: [pair_steps]}):
            tile = pl.ds(tile_at(at), TILE)
            back[...] = dot_nn(turned[:, :width], joined[layer][:width, tile])
            back[...] += dot_nt(pooled[layer][...], matrix[tile, :])
            if layer == 0:
                hidden[layer][:, tile] = back[...].astype(bf16)
            else:

                @pl.loop(0, TILE // 256)
                def _(part_at):
                    for part in range(2):
                        inside = chunk_at(part_at * 2 + part)
                        lanes = chunk_at(part_at * 2 + part, at * TILE)
                        norm_backward(
                            back, pre[layer - 1], active, slope, scales.at[layer - 1], hidden[layer], inside, lanes, lanes
                        )

            ticks(at, plan)

        proj_before, pair_before = [proj_steps], [pair_steps]

    feat_copy.wait()
    @pl.loop(0, 2)
    def _(at):
        rows = pl.ds(pl.multiple_of(at * 256, 256), 256)
        in_g[0, pl.ds(at * 2, 2)] = dot_nt(hid_0[rows, :], feat[...]).astype(bf16).reshape(2, *in_g.shape[2:])

    def keep_in(value):
        gin_out[...] = value

    in_steps = scatter_steps(
        place, Wire(scatter_send.at[7], scatter_recv.at[7]),
        (in_g, in_rc, in_oh, in_ih, in_ocol, in_icol, in_oz, in_iz, in_own), 0, keep_in,
    )
    step(in_steps, *proj_before)
    step(in_steps, *pair_before)
    step(in_steps)
    step(in_steps, *pair_before)
    step(in_steps)
    for wire in gather_wires:
        wire.finish()


def scatter_buffers(rows, columns, slots):
    def buf(*shape):
        return pltpu.VMEM((slots, *shape, rows, columns), bf16)

    return [
        buf(4, 2, 2, 2), buf(4, 2, 2), buf(2, 2), buf(2, 2), buf(2, 4), buf(2, 4), buf(3), buf(3),
        pltpu.VMEM((slots, rows, columns), f32),
    ]


def train(feat, nbr, edge, degree, counts, labels, live, win, pair, proj, head):
    features, nodes = feat.shape
    width = pair.shape[2]
    classes = head.shape[1]
    vmem = pl.BlockSpec(memory_space=pltpu.VMEM)
    dma = pltpu.SemaphoreType.DMA
    return pl.pallas_call(
        train_kernel,
        out_shape=[
            jax.ShapeDtypeStruct(win.shape, f32),
            jax.ShapeDtypeStruct(pair.shape, f32),
            jax.ShapeDtypeStruct(proj.shape, f32),
            jax.ShapeDtypeStruct(head.shape, f32),
            jax.ShapeDtypeStruct((8, 128), f32),
        ],
        in_specs=[pl.BlockSpec(memory_space=pl.ANY)] + [vmem] * 10,
        out_specs=[vmem] * 5,
        scratch_shapes=[
            pltpu.VMEM((nodes, nodes), bf16),
            pltpu.VMEM((features, nodes), bf16),
        ]
        + [pltpu.VMEM((width, nodes), bf16)] * 3
        + [pltpu.VMEM((width, nodes), bf16)] * 3
        + [pltpu.VMEM((2 * width, nodes), bf16)] * 3
        + [pltpu.VMEM((width, nodes), f32)] * 2
        + [
            pltpu.VMEM((4, 2, 2, 2, 16, features), bf16),
            pltpu.VMEM((LAYERS, 2, 4, 2, 2, 2, 32, width), bf16),
            pltpu.VMEM((4, 2, 2, 2, 16, 128), bf16),
            pltpu.VMEM((width, 2 * width), bf16),
            pltpu.VMEM((width, 128), f32),
            pltpu.VMEM((1, nodes), f32),
            pltpu.VMEM((1, nodes), f32),
            pltpu.VMEM((8, nodes), f32),
            pltpu.VMEM((8, 128), f32),
            pltpu.VMEM((8, 128), f32),
            pltpu.VMEM((LAYERS, 1, nodes), f32),
            pltpu.VMEM((width, TILE), f32),
            pltpu.VMEM((width, TILE), f32),
            pltpu.VMEM((width, TILE), bf16),
            pltpu.VMEM((width, 128), f32),
            pltpu.VMEM((width, 128), f32),
        ]
        + scatter_buffers(32, width, 2)
        + scatter_buffers(16, features, 1)
        + scatter_buffers(16, 128, 1)
        + [
            pltpu.VMEM((2, 3, 8, 128), f32),
            pltpu.VMEM((2, 3, 8, 128), f32),
            pltpu.VMEM((2, 4, 8, 128), f32),
            dma((8, 11)), dma((8, 11)), dma((8, 8)), dma((8, 8)), dma((2, 6)), dma((2, 6)), dma,
            pltpu.SemaphoreType.REGULAR((2, 6)),
        ],
        compiler_params=pltpu.CompilerParams(
            collective_id=0, has_side_effects=True, vmem_limit_bytes=64 * 2**20
        ),
        cost_estimate=pl.CostEstimate(
            flops=67 * 10**9, bytes_accessed=10**7, transcendentals=10**7
        ),
    )(feat, nbr, edge, degree, counts, labels, live, win, pair, proj, head)


def update_kernel(*refs):
    inputs, outs = refs[:16], refs[16:]
    for at in range(4):
        weight, first, second, grad = (inputs[at + 4 * kind][...] for kind in range(4))
        new, first_new, second_new = adamw_update(weight, first, second, grad)
        outs[at][...] = new
        outs[4 + at][...] = first_new
        outs[8 + at][...] = second_new
        outs[12 + at][...] = new.astype(bf16)


def update(weights, firsts, seconds, grads):
    shapes = [jax.ShapeDtypeStruct(w.shape, f32) for w in weights]
    vmem = pl.BlockSpec(memory_space=pltpu.VMEM)
    return pl.pallas_call(
        update_kernel,
        out_shape=shapes * 3 + [jax.ShapeDtypeStruct(w.shape, bf16) for w in weights],
        in_specs=[vmem] * 16,
        out_specs=[vmem] * 16,
    )(*weights, *firsts, *seconds, *grads)


def turned_first(array):
    return jnp.swapaxes(array, -1, -2)


def body(
    features, labels, neighbors, degree, node_counts, edge_counts, live_nodes,
    input_weight, pair_weight, proj_weight, head_weight,
    input_first, pair_first, proj_first, head_first,
    input_second, pair_second, proj_second, head_second,
):
    def owned(input_w, pair_w, proj_w, head_w):
        return (turned_first(input_w), turned_first(pair_w), proj_w, head_w)

    weights = owned(input_weight, pair_weight, proj_weight, head_weight)
    *grads, scalars = train(
        turned_first(features), turned_first(neighbors), turned_first(edge_counts),
        degree[None, :], node_counts[None, :], labels[None, :], live_nodes[None, :], *weights,
    )
    results = update(
        weights,
        owned(input_first, pair_first, proj_first, head_first),
        owned(input_second, pair_second, proj_second, head_second),
        grads,
    )
    placed = []
    for kind in range(4):
        placed += owned(*results[4 * kind : 4 * kind + 4])
    return (scalars[0, 0], scalars[1, 0], *placed)


def normalize(preact):
    active = jax.nn.gelu(preact)
    return active * lax.rsqrt(jnp.mean(active * active, axis=-1, keepdims=True) + norm_eps)


def slot_terms(neighbors, degree, live_count):
    count_nodes, fanout = neighbors.shape
    node_live = jnp.arange(count_nodes, dtype=jnp.int32) < live_count
    used = (
        (jnp.arange(fanout, dtype=jnp.int32)[None, :] < degree[:, None])
        & (neighbors < live_count)
        & node_live[:, None]
    )
    return (node_live, used)


def coefficients(used, node_counts, edge_counts, total_node, total_edge):
    node_float = node_counts.astype(jnp.float32)
    edge_float = edge_counts.astype(jnp.float32)
    spread = jnp.maximum(jnp.sum(used.astype(jnp.float32), axis=1), 1.0)
    value = node_float[:, None] * total_edge / (edge_float * total_node * spread[:, None])
    return jnp.where(used, value, 0.0)


def contract_rows(left, right):
    return lax.dot_general(
        left, right, (((0,), (0,)), ((), ())), preferred_element_type=jnp.float32
    )


def contract_cols(left, right):
    return lax.dot_general(
        left, right, (((1,), (1,)), ((), ())), preferred_element_type=jnp.float32
    )


def coef_matrix(neighbors, coefs):
    count_nodes = neighbors.shape[0]
    columns = lax.iota(jnp.int32, count_nodes)[None, :]
    matrix = jnp.zeros((count_nodes, count_nodes), jnp.float32)
    for neighbor_slot in range(neighbors.shape[1]):
        matrix = matrix + jnp.where(
            neighbors[:, neighbor_slot : neighbor_slot + 1] == columns,
            coefs[:, neighbor_slot : neighbor_slot + 1],
            0.0,
        )
    return matrix


def layer_forward(hidden, pair_w, proj_w, matrix):
    width = pair_w.shape[0]
    pooled = jnp.dot(
        matrix,
        hidden.astype(jnp.float32),
        precision=lax.Precision.HIGHEST,
        preferred_element_type=jnp.float32,
    ).astype(jnp.bfloat16)
    self_part = jnp.dot(hidden, pair_w[:, :width], preferred_element_type=jnp.float32)
    nbr_part = jnp.dot(pooled, pair_w[:, width:], preferred_element_type=jnp.float32)
    joined = jnp.concatenate([self_part, nbr_part], axis=1).astype(jnp.bfloat16)
    preact = jnp.dot(joined, proj_w, preferred_element_type=jnp.float32)
    return (normalize(preact).astype(jnp.bfloat16), (hidden, pooled, joined, preact))


def layer_backward(grad_out, saved, pair_w, proj_w, matrix):
    hidden, pooled, joined, preact = saved
    width = pair_w.shape[0]
    _, pullback = jax.vjp(normalize, preact)
    grad_preact = pullback(grad_out)[0].astype(jnp.bfloat16)
    grad_proj = contract_rows(joined, grad_preact)
    grad_joined = contract_cols(grad_preact, proj_w).astype(jnp.bfloat16)
    grad_pair = jnp.concatenate(
        [
            contract_rows(hidden, grad_joined[:, :width]),
            contract_rows(pooled, grad_joined[:, width:]),
        ],
        axis=1,
    )
    grad_hidden = contract_cols(grad_joined[:, :width], pair_w[:, :width])
    grad_pooled = contract_cols(grad_joined[:, width:], pair_w[:, width:])
    grad_hidden = grad_hidden + lax.dot_general(
        matrix,
        grad_pooled,
        (((0,), (0,)), ((), ())),
        precision=lax.Precision.HIGHEST,
        preferred_element_type=jnp.float32,
    )
    return (grad_hidden, grad_pair, grad_proj)


def plain_body(
    features,
    labels,
    neighbors,
    degree,
    node_counts,
    edge_counts,
    live_nodes,
    input_weight,
    pair_weight,
    proj_weight,
    head_weight,
    input_first,
    pair_first,
    proj_first,
    head_first,
    input_second,
    pair_second,
    proj_second,
    head_second,
):
    count_nodes = features.shape[0]
    all_nodes = jnp.float32(count_nodes * lax.axis_size(("dp", "group")))
    node_live, used = slot_terms(neighbors, degree, live_nodes[0])
    node_float = node_counts.astype(jnp.float32)
    node_local = jnp.sum(jnp.where(node_live, node_float, 0.0))
    edge_local = jnp.sum(jnp.where(used, edge_counts.astype(jnp.float32), 0.0))
    total_node, total_edge = lax.psum((node_local, edge_local), ("dp", "group"))
    weights = jnp.where(node_live, total_node / (node_float * all_nodes), 0.0)
    coefs = coefficients(used, node_counts, edge_counts, total_node, total_edge)
    matrix = coef_matrix(neighbors, coefs)
    input_b, pair_b, proj_b, head_b = (
        lax.all_gather(input_weight.astype(jnp.bfloat16), ("dp", "group"), axis=1, tiled=True),
        lax.all_gather(pair_weight.astype(jnp.bfloat16), ("dp", "group"), axis=2, tiled=True),
        lax.all_gather(proj_weight.astype(jnp.bfloat16), ("dp", "group"), axis=1, tiled=True),
        lax.all_gather(head_weight.astype(jnp.bfloat16), ("dp", "group"), axis=0, tiled=True),
    )
    hidden = jnp.dot(features, input_b, preferred_element_type=jnp.float32).astype(jnp.bfloat16)
    kept = []
    for layer_index in range(LAYERS):
        hidden, saved = layer_forward(hidden, pair_b[layer_index], proj_b[layer_index], matrix)
        kept.append(saved)
    logits = jnp.dot(hidden, head_b, preferred_element_type=jnp.float32)
    log_total = jax.nn.logsumexp(logits, axis=1)
    targets = (labels[:, None] == lax.iota(jnp.int32, logits.shape[1])[None, :]).astype(jnp.float32)
    loss_local = jnp.sum(weights * (log_total - jnp.sum(logits * targets, axis=1)))
    loss_sum, weight_sum = lax.psum((loss_local, jnp.sum(weights)), ("dp", "group"))
    grad_logits = (
        (weights / weight_sum)[:, None] * (jnp.exp(logits - log_total[:, None]) - targets)
    ).astype(jnp.bfloat16)
    grad_head = contract_rows(hidden, grad_logits)
    grad_hidden = contract_cols(grad_logits, head_b)
    pair_grads = [None] * LAYERS
    proj_grads = [None] * LAYERS
    for layer_index in reversed(range(LAYERS)):
        grad_hidden, grad_pair, grad_proj = layer_backward(
            grad_hidden, kept[layer_index], pair_b[layer_index], proj_b[layer_index], matrix
        )
        pair_grads[layer_index] = grad_pair
        proj_grads[layer_index] = grad_proj
    grad_input = contract_rows(features, grad_hidden.astype(jnp.bfloat16))
    grad_input, grad_pairs, grad_projs, grad_head = (
        lax.psum_scatter(grad_input, ("dp", "group"), scatter_dimension=1, tiled=True),
        lax.psum_scatter(jnp.stack(pair_grads), ("dp", "group"), scatter_dimension=2, tiled=True),
        lax.psum_scatter(jnp.stack(proj_grads), ("dp", "group"), scatter_dimension=1, tiled=True),
        lax.psum_scatter(grad_head, ("dp", "group"), scatter_dimension=0, tiled=True),
    )
    input_new, input_first_new, input_second_new = adamw_update(
        input_weight, input_first, input_second, grad_input
    )
    pair_new, pair_first_new, pair_second_new = adamw_update(
        pair_weight, pair_first, pair_second, grad_pairs
    )
    proj_new, proj_first_new, proj_second_new = adamw_update(
        proj_weight, proj_first, proj_second, grad_projs
    )
    head_new, head_first_new, head_second_new = adamw_update(
        head_weight, head_first, head_second, grad_head
    )
    return (
        loss_sum / weight_sum,
        weight_sum / all_nodes,
        input_new,
        pair_new,
        proj_new,
        head_new,
        input_first_new,
        pair_first_new,
        proj_first_new,
        head_first_new,
        input_second_new,
        pair_second_new,
        proj_second_new,
        head_second_new,
        input_new.astype(jnp.bfloat16),
        pair_new.astype(jnp.bfloat16),
        proj_new.astype(jnp.bfloat16),
        head_new.astype(jnp.bfloat16),
    )


def solution(mesh):
    placed = (
        P(("dp", "group"), None),
        P(("dp", "group")),
        P(("dp", "group"), None),
        P(("dp", "group")),
        P(("dp", "group")),
        P(("dp", "group"), None),
        P(("dp", "group")),
        P(None, ("dp", "group")),
        P(None, None, ("dp", "group")),
        P(None, ("dp", "group"), None),
        P(("dp", "group"), None),
        P(None, ("dp", "group")),
        P(None, None, ("dp", "group")),
        P(None, ("dp", "group"), None),
        P(("dp", "group"), None),
        P(None, ("dp", "group")),
        P(None, None, ("dp", "group")),
        P(None, ("dp", "group"), None),
        P(("dp", "group"), None),
    )
    fits = dict(mesh.shape) == {"dp": 8, "group": 4}
    return jax.shard_map(
        body if fits else plain_body,
        mesh=mesh,
        in_specs=placed,
        out_specs=(
            P(),
            P(),
            P(None, ("dp", "group")),
            P(None, None, ("dp", "group")),
            P(None, ("dp", "group"), None),
            P(("dp", "group"), None),
            P(None, ("dp", "group")),
            P(None, None, ("dp", "group")),
            P(None, ("dp", "group"), None),
            P(("dp", "group"), None),
            P(None, ("dp", "group")),
            P(None, None, ("dp", "group")),
            P(None, ("dp", "group"), None),
            P(("dp", "group"), None),
            P(None, ("dp", "group")),
            P(None, None, ("dp", "group")),
            P(None, ("dp", "group"), None),
            P(("dp", "group"), None),
        ),
        check_vma=False,
    )
```

```python
import functools

import jax
import jax.numpy as jnp
from jax import lax
from jax.experimental import pallas as pl
from jax.experimental.pallas import tpu as pltpu
from jax.sharding import PartitionSpec as P

LAYERS = 3
STEP = 5
COMMON = 840.0

learn_rate = 0.03
beta_first = 0.5
beta_second = 0.5
adam_eps = 1e-08
decay_rate = 0.01
norm_eps = 1e-06

AXES = ("dp", "group")
MESH = pl.DeviceIdType.MESH
f32 = jnp.float32
bf16 = jnp.bfloat16
TILE = 512
WIDE = 1024
SPLIT = 384
ROWS = 16
GATE_IN = 0.7978845608028654
GATE_CUBE = GATE_IN * 0.044715


def dot_nn(left, right):
    return jnp.dot(left, right, preferred_element_type=f32)


def dot_nt(left, right):
    return lax.dot_general(left, right, (((1,), (1,)), ((), ())), preferred_element_type=f32)


def adamw_update(weight, first, second, grad):
    first_new = beta_first * first + (1.0 - beta_first) * grad
    second_new = beta_second * second + (1.0 - beta_second) * grad * grad
    first_hat = first_new / (1.0 - beta_first**STEP)
    second_hat = second_new / (1.0 - beta_second**STEP)
    weight_new = weight - learn_rate * (
        first_hat / (jnp.sqrt(second_hat) + adam_eps) + decay_rate * weight
    )
    return (weight_new, first_new, second_new)


class Place:
    def __init__(self):
        dp, group = lax.axis_index("dp"), lax.axis_index("group")
        self.z, self.y = dp // 2, dp % 2
        self.x, self.c = group // 2, group % 2
        self.far_y, self.far_x, self.far_c = 1 - self.y, 1 - self.x, 1 - self.c
        self.sibling = (dp, group + 1 - 2 * self.c)
        self.beside_x = (dp, group + 2 - 4 * self.x)
        self.beside_y = (dp + 1 - 2 * self.y, group)
        self.across = (dp + 1 - 2 * self.y, group + 2 - 4 * self.x)
        self.later_z = [(self.z + step) % 4 for step in (1, 2, 3)]
        self.earlier_z = [(self.z + 4 - step) % 4 for step in (1, 2, 3)]
        self.to_z = [(at * 2 + self.y, group) for at in self.later_z]
        self.from_z = [(at * 2 + self.y, group) for at in self.earlier_z]

    def partners(self):
        return [self.sibling] + self.plane() + self.to_z

    def plane(self):
        return [self.beside_x, self.beside_y, self.across]

    def columns(self):
        return [(self.y, self.far_x), (self.far_y, self.x), (self.far_y, self.far_x)]


class Wire:
    def __init__(self, send_sems, recv_sems):
        self.send_sems, self.recv_sems = send_sems, recv_sems
        self.sent = []

    def copy(self, at, source, target, device):
        return pltpu.make_async_remote_copy(
            src_ref=source(),
            dst_ref=target(),
            send_sem=self.send_sems.at[at],
            recv_sem=self.recv_sems.at[at],
            device_id=device,
            device_id_type=MESH,
        )

    def send(self, at, source, target, device):
        self.copy(at, source, target, device).start()
        self.sent.append((at, source, target, device))

    def arrived(self, at, target, device):
        self.copy(at, target, target, device).wait_recv()

    def finish(self, below=100):
        for sent in self.sent:
            if sent[0] < below:
                self.copy(*sent).wait_send()
        self.sent = [sent for sent in self.sent if sent[0] >= below]


def gather_steps(place, wire, region):
    z, y, x, c = place.z, place.y, place.x, place.c
    fy, fx, fc = place.far_y, place.far_x, place.far_c
    whole, low, high = slice(0, 4), slice(0, 2), slice(2, 4)

    def at(*index):
        return lambda: region(*index)

    def send(sem, index, device):
        wire.send(sem, at(*index), at(*index), device)

    for step in range(3):
        send(step, (z, y, x, c), place.to_z[step])
    yield
    for step in range(3):
        wire.arrived(step, at(place.earlier_z[step], y, x, c), place.from_z[step])
    send(3, (whole, y, x, c), place.beside_x)
    send(4, (whole, y, x, c), place.beside_y)
    send(5, (whole, y, x, c), place.sibling)
    yield
    wire.arrived(3, at(whole, y, fx, c), place.beside_x)
    send(6, (low, y, fx, c), place.beside_y)
    send(8, (whole, y, fx, c), place.sibling)
    wire.arrived(4, at(whole, fy, x, c), place.beside_y)
    send(7, (high, fy, x, c), place.beside_x)
    send(9, (whole, fy, x, c), place.sibling)
    yield
    wire.arrived(6, at(low, fy, fx, c), place.beside_y)
    wire.arrived(7, at(high, fy, fx, c), place.beside_x)
    send(10, (whole, fy, fx, c), place.sibling)
    yield
    wire.arrived(5, at(whole, y, x, fc), place.sibling)
    wire.arrived(8, at(whole, y, fx, fc), place.sibling)
    wire.arrived(9, at(whole, fy, x, fc), place.sibling)
    wire.arrived(10, at(whole, fy, fx, fc), place.sibling)
    yield


def small_gather_steps(place, wire, region):
    z, y, x, c = place.z, place.y, place.x, place.c
    whole = slice(0, 4)

    def at(*index):
        return lambda: region(*index)

    def send(sem, index, device):
        wire.send(sem, at(*index), at(*index), device)

    for step in range(3):
        send(step, (z, y, x, c), place.to_z[step])
    yield
    for step in range(3):
        wire.arrived(step, at(place.earlier_z[step], y, x, c), place.from_z[step])
    for step, device in enumerate(place.plane()):
        send(3 + step, (whole, y, x, c), device)
    send(6, (whole, y, x, c), place.sibling)
    yield
    for step, (yy, xx) in enumerate(place.columns()):
        wire.arrived(3 + step, at(whole, yy, xx, c), place.plane()[step])
        send(7 + step, (whole, yy, xx, c), place.sibling)
    yield
    for step, (yy, xx) in enumerate([(y, x)] + place.columns()):
        wire.arrived(6 + step, at(whole, yy, xx, place.far_c), place.sibling)
    yield


def small_scatter_steps(place, wire, bufs, store):
    grads, from_core, out_col, in_col, out_z, in_z, own = bufs
    z, y, x, c, fc = place.z, place.y, place.x, place.c, place.far_c
    whole = slice(0, 4)

    def at(buf, *index):
        return lambda: buf.at[index]

    def both(zs, yy, xx):
        return grads[zs, yy, xx, c].astype(f32) + from_core[zs, yy, xx].astype(f32)

    wire.send(
        0, at(grads, whole, slice(0, 2), slice(0, 2), fc), at(from_core, whole), place.sibling
    )
    yield
    wire.arrived(0, at(from_core, whole), place.sibling)
    for step, (yy, xx) in enumerate(place.columns()):
        out_col[step] = both(whole, yy, xx).astype(bf16)
        wire.send(1 + step, at(out_col, step), at(in_col, step), place.plane()[step])
    yield
    for step, device in enumerate(place.plane()):
        wire.arrived(1 + step, at(in_col, step), device)

    def column(zz):
        beside = in_col[0, zz].astype(f32) + in_col[1, zz].astype(f32)
        return both(zz, y, x) + (beside + in_col[2, zz].astype(f32))

    for step in range(3):
        out_z[step] = column(place.later_z[step]).astype(bf16)
        wire.send(4 + step, at(out_z, step), at(in_z, step), place.to_z[step])
    own[...] = column(z)
    yield
    for step in range(3):
        wire.arrived(4 + step, at(in_z, step), place.from_z[step])
    store(own[...] + (in_z[0].astype(f32) + in_z[1].astype(f32) + in_z[2].astype(f32)))
    wire.finish()
    yield


def scatter_steps(place, wire, bufs, slot, store, free=None, reuses=False, reused=False):
    grads, from_core, out_half, in_half, out_col, in_col, out_z, in_z, own = bufs
    z, y, x, c = place.z, place.y, place.x, place.c
    fy, fx, fc = place.far_y, place.far_x, place.far_c
    low, high = slice(0, 2), slice(2, 4)

    def at(buf, *index):
        return lambda: buf.at[(slot, *index)]

    def both(zs, yy, xx):
        return grads[slot, zs, yy, xx, c].astype(f32) + from_core[slot, zs, yy, xx].astype(f32)

    def until_free(*partners):
        if reuses:
            for partner in partners:
                pl.semaphore_wait(free.at[slot, partner], 1)

    def set_free(*partners):
        for partner, device in partners:
            pl.semaphore_signal(free.at[slot, partner], inc=1, device_id=device, device_id_type=MESH)

    until_free(0)
    wire.send(0, at(grads, slice(0, 4), slice(0, 2), slice(0, 2), fc), at(from_core), place.sibling)
    yield
    wire.arrived(0, at(from_core), place.sibling)
    until_free(1, 2)
    out_half[slot, 0] = both(low, fy, fx).astype(bf16)
    wire.send(1, at(out_half, 0), at(in_half, 0), place.beside_x)
    out_half[slot, 1] = both(high, fy, fx).astype(bf16)
    wire.send(2, at(out_half, 1), at(in_half, 1), place.beside_y)
    yield
    wire.arrived(1, at(in_half, 0), place.beside_x)
    out_col[slot, 1, low] = (both(low, fy, x) + in_half[slot, 0].astype(f32)).astype(bf16)
    out_col[slot, 1, high] = both(high, fy, x).astype(bf16)
    wire.send(4, at(out_col, 1), at(in_col, 1), place.beside_y)
    wire.arrived(2, at(in_half, 1), place.beside_y)
    out_col[slot, 0, low] = both(low, y, fx).astype(bf16)
    out_col[slot, 0, high] = (both(high, y, fx) + in_half[slot, 1].astype(f32)).astype(bf16)
    wire.send(3, at(out_col, 0), at(in_col, 0), place.beside_x)
    yield
    wire.arrived(3, at(in_col, 0), place.beside_x)
    wire.arrived(4, at(in_col, 1), place.beside_y)

    def column(zz):
        beside = in_col[slot, 0, zz].astype(f32) + in_col[slot, 1, zz].astype(f32)
        return both(zz, y, x) + beside

    until_free(3, 4, 5)
    own[slot] = column(z)
    for step in range(3):
        out_z[slot, step] = column(place.later_z[step]).astype(bf16)
        wire.send(5 + step, at(out_z, step), at(in_z, step), place.to_z[step])
    wire.finish(5)
    if reused:
        set_free((0, place.sibling))
    yield
    for step in range(3):
        wire.arrived(5 + step, at(in_z, step), place.from_z[step])
    others = in_z[slot, 0].astype(f32) + in_z[slot, 1].astype(f32) + in_z[slot, 2].astype(f32)
    store(own[slot] + others)
    wire.finish()
    if reused:
        set_free(*enumerate([place.beside_x, place.beside_y] + place.from_z, 1))
    yield


def sum_steps(place, wire, bufs, slot, store):
    out, arrive, plane, line = bufs
    z, y, x = place.z, place.y, place.x

    def at(buf, *index):
        return lambda: buf.at[(slot, *index)]

    wire.send(0, at(out), at(arrive), place.sibling)
    yield
    wire.arrived(0, at(arrive), place.sibling)
    plane[slot, y, x] = out[slot] + arrive[slot]
    for step, device in enumerate(place.plane()):
        wire.send(1 + step, at(plane, y, x), at(plane, y, x), device)
    yield
    for step, (yy, xx) in enumerate(place.columns()):
        wire.arrived(1 + step, at(plane, yy, xx), place.plane()[step])
    line[slot, z] = (plane[slot, 0, 0] + plane[slot, 0, 1]) + (plane[slot, 1, 0] + plane[slot, 1, 1])
    for step in range(3):
        wire.send(4 + step, at(line, z), at(line, z), place.to_z[step])
    yield
    for step in range(3):
        wire.arrived(4 + step, at(line, place.earlier_z[step]), place.from_z[step])
    store((line[slot, 0] + line[slot, 1]) + (line[slot, 2] + line[slot, 3]))
    wire.finish()
    yield


PLAN = {
    ("start", 0): ("ia", "ib",),
    ("slots", 0): ("tot",),
    ("build", 0): ("tot",),
    ("build", 1): ("ia", "p0",),
    ("build", 2): ("ib", "q0",),
    ("build", 3): ("tot",),
    ("build", 7): ("ia", "tot", "p0", "p1", "ib", "ia", "ib",),
    ("first", 1): ("q0", "q1",),
    ("pool0", 0): ("p0", "p1", "p2",),
    ("pool0", 1): ("q0", "q1", "q2", "p0", "p0",),
    ("join0", 0): ("p1", "p2", "wh",),
    ("join0", 1): ("q0", "q2", "wh", "q0",),
    ("pre0", 0): ("q1",),
    ("pre0", 2): ("p1",),
    ("pool1", 0): ("p2",),
    ("pool1", 1): ("q2", "wh", "p1",),
    ("join1", 0): ("q1",),
    ("join1", 1): ("p2", "q1",),
    ("pre1", 0): ("q2",),
    ("pool2", 1): ("p2",),
    ("join2", 1): ("q2", "wh",),
    ("loss", 0): ("rh", "los",),
    ("A2", 0): ("rh", "los",),
    ("A2", 1): ("P2",),
    ("B2", 0): ("los", "rh",),
    ("B2", 1): ("P2",),
    ("C2", 0): ("rh", "los",),
    ("C2", 1): ("Q2",),
    ("D2", 0): ("P2",),
    ("E2", 0): ("Q2",),
    ("E2", 1): ("P2",),
    ("E2", 2): ("Q2",),
    ("A1", 0): ("P2",),
    ("A1", 1): ("P1",),
    ("B1", 0): ("Q2",),
    ("B1", 1): ("P1",),
    ("C1", 1): ("Q1",),
    ("D1", 0): ("Q2", "P1",),
    ("E1", 0): ("Q1",),
    ("E1", 1): ("P1",),
    ("E1", 2): ("Q1",),
    ("A0", 0): ("P1",),
    ("A0", 1): ("P0",),
    ("B0", 0): ("Q1",),
    ("B0", 1): ("P0",),
    ("C0", 1): ("Q0",),
    ("D0", 0): ("Q1", "P0",),
    ("E0", 0): ("Q0",),
    ("E0", 2): ("P0",),
    ("E0", 3): ("Q0",),
    ("inputs", 0): ("ra",),
    ("inputs", 1): ("rb", "ra", "P0", "rb", "Q0", "ra", "rb", "Q0", "ra", "rb",),
}


class Moves:
    def __init__(self):
        self.under_way = {}

    def play(self, label, at=0):
        for name in PLAN.get((label, at), ()):
            next(self.under_way[name])

    def after(self, label, at, count, part=0, parts=1):
        for when in range(count):
            if (label, when * parts + part) in PLAN:

                @pl.when(at == when)
                def _(when=when):
                    self.play(label, when * parts + part)


def row_of_scalars(values):
    rows = lax.broadcasted_iota(jnp.int32, (8, 128), 0)
    block = jnp.zeros((8, 128), f32)
    for at, value in enumerate(values):
        block = jnp.where(rows == at, value, block)
    return block


def gelu(pre):
    square = pre * pre
    gate = 0.5 * jnp.tanh(pre * (GATE_CUBE * square + GATE_IN)) + 0.5
    return pre * gate, gate, square


def weave(dots, vectors):
    done = 0
    for at, piece in enumerate(dots):
        piece()
        upto = (at + 1) * len(vectors) // len(dots)
        for vector in vectors[done:upto]:
            vector()
        done = upto


def dot_pieces(terms, store):
    pieces = []
    for block in range(TILE // 256):
        for rows in (slice(0, 256), slice(256, 512)):
            held = {}
            for at, term in enumerate(terms):

                def piece(at=at, term=term, block=block, rows=rows, held=held):
                    value = term(rows, block)
                    held["sum"] = value if at == 0 else held["sum"] + value
                    if at == len(terms) - 1:
                        store(rows, block, held["sum"])

                pieces.append(piece)
    return pieces


def staggered(firsts, seconds):
    pieces = []
    for at in range(len(firsts) + 1):
        first = firsts[at] if at < len(firsts) else []
        second = seconds[at - 1] if at > 0 else []
        for pick in range(max(len(first), len(second))):
            pieces += first[pick : pick + 1] + second[pick : pick + 1]
    return pieces


def row_chunks():
    return [slice(at, at + ROWS) for at in range(0, 512, ROWS)]


def forward_pieces(pre, active, scales, out, inside, lanes):
    firsts, seconds = [], []
    for at in range(TILE // 128):
        held = {"square": jnp.zeros((ROWS, 128), f32)}
        slot = active.at[at % 2]

        def first(row, at=at, held=held, slot=slot):
            value, _, _ = gelu(pre[row, inside(at)])
            slot[row, :] = value
            held["square"] = held["square"] + value * value

        def finish(at=at, held=held):
            mean = jnp.sum(held["square"], axis=0, keepdims=True) * (1.0 / 512)
            held["scale"] = lax.rsqrt(mean + norm_eps)
            scales[:, lanes(at)] = held["scale"]

        def second(row, at=at, held=held, slot=slot):
            out[row, lanes(at)] = (slot[row, :] * held["scale"]).astype(bf16)

        firsts.append([functools.partial(first, row) for row in row_chunks()] + [finish])
        seconds.append([functools.partial(second, row) for row in row_chunks()])
    return staggered(firsts, seconds)


def backward_pieces(grad, pre, active, slope, scales, out, inside, pre_lanes, lanes):
    firsts, seconds = [], []
    for at in range(TILE // 128):
        held = {"along": jnp.zeros((ROWS, 128), f32)}
        values, slopes = active.at[at % 2], slope.at[at % 2]

        def first(row, at=at, held=held, values=values, slopes=slopes):
            value, gate, square = gelu(pre[row, pre_lanes(at)])
            values[row, :] = value
            slopes[row, :] = gate + value * (
                (1.0 - gate) * ((6.0 * GATE_CUBE) * square + 2.0 * GATE_IN)
            )
            held["along"] = held["along"] + value * grad[row, inside(at)]

        def finish(at=at, held=held):
            scale = scales[:, lanes(at)]
            mean = jnp.sum(held["along"], axis=0, keepdims=True) * (1.0 / 512)
            held["scale"], held["pull"] = scale, scale * scale * scale * mean

        def second(row, at=at, held=held, values=values, slopes=slopes):
            push = held["scale"] * grad[row, inside(at)] - values[row, :] * held["pull"]
            out[row, lanes(at)] = (slopes[row, :] * push).astype(bf16)

        firsts.append([functools.partial(first, row) for row in row_chunks()] + [finish])
        seconds.append([functools.partial(second, row) for row in row_chunks()])
    return staggered(firsts, seconds)


def train_kernel(
    feat_hbm, nbr, edge, degree, counts, labels, live, win_own, pair_own, proj_own, head_own,
    gin_out, gpair_out, gproj_out, ghead_out, scal_out,
    matrix, feat, hid_0, hid_1, hid_2, pool_0, pool_1, pool_2, join_0, join_1, join_2, pre_0, pre_1,
    win, weights, head, turned, head_grad, scale, inverse, terms, totals, losses, scales,
    back, top_pre, last, active, slope, top_scale,
    big_g, big_rc, big_oh, big_ih, big_ocol, big_icol, big_oz, big_iz, big_own,
    ina_g, ina_rc, ina_ocol, ina_icol, ina_oz, ina_iz, ina_own,
    inb_g, inb_rc, inb_ocol, inb_icol, inb_oz, inb_iz, inb_own,
    hd_g, hd_rc, hd_ocol, hd_icol, hd_oz, hd_iz, hd_own,
    sum_out, sum_in, sum_plane, sum_line,
    gather_send, gather_recv, scatter_send, scatter_recv, sum_send, sum_recv, feat_sem, free,
):
    place = Place()
    z, y, x, c = place.z, place.y, place.x, place.c
    nodes, width, classes = nbr.shape[1], hid_0.shape[0], head_own.shape[1]
    steps, wide_steps = nodes // TILE, nodes // WIDE
    hidden, pooled, joined, pre = (
        [hid_0, hid_1, hid_2], [pool_0, pool_1, pool_2], [join_0, join_1, join_2], [pre_0, pre_1],
    )
    top, features = LAYERS - 1, feat.shape[0]

    barrier = pltpu.get_barrier_semaphore()
    for partner in place.partners():
        pl.semaphore_signal(barrier, inc=1, device_id=partner, device_id_type=MESH)

    feat_copy = pltpu.make_async_copy(feat_hbm, feat, feat_sem)
    feat_copy.start()
    win[z, y, x, c] = win_own[...].astype(bf16)
    for layer in range(LAYERS):
        weights[layer, 0, z, y, x, c] = pair_own[layer].astype(bf16)
        weights[layer, 1, z, y, x, c] = proj_own[layer].astype(bf16)
    head[z, y, x, c] = jnp.zeros(head.shape[4:], bf16)
    head[z, y, x, c, :, 0:classes] = head_own[...].astype(bf16)

    pl.semaphore_wait(barrier, 7)

    def region_of(layer, kind):
        return lambda zz, yy, xx, cc: weights.at[layer, kind, zz, yy, xx, cc]

    def region_of_input(columns):
        return lambda zz, yy, xx, cc: win.at[zz, yy, xx, cc, :, columns]

    regions = {
        "ia": region_of_input(slice(0, SPLIT)),
        "ib": region_of_input(slice(SPLIT, features)),
        "wh": lambda zz, yy, xx, cc: head.at[zz, yy, xx, cc],
    }
    for layer in range(LAYERS):
        regions[f"p{layer}"] = region_of(layer, 0)
        regions[f"q{layer}"] = region_of(layer, 1)
    moves = Moves()
    gather_wires = []
    for at, (name, region) in enumerate(regions.items()):
        gather_wires.append(Wire(gather_send.at[at], gather_recv.at[at]))
        steps_of = gather_steps if name[0] in "pq" else small_gather_steps
        moves.under_way[name] = steps_of(place, gather_wires[-1], region)
    moves.play("start")

    node_live = lax.broadcasted_iota(jnp.int32, (1, nodes), 1) < live[...]
    slot = lax.broadcasted_iota(jnp.int32, nbr.shape, 0)
    used = (slot < degree[...]) & (nbr[...] < live[...]) & node_live
    edge_float = edge[...].astype(f32)
    count_float = counts[...].astype(f32)
    spread = jnp.maximum(jnp.sum(used.astype(f32), axis=0, keepdims=True), 1.0)
    inverse[...] = jnp.where(node_live, 1.0 / count_float, 0.0)
    scale[...] = count_float / (spread * COMMON)
    sum_out[0] = row_of_scalars(
        [
            jnp.sum(jnp.where(node_live, count_float, 0.0)),
            jnp.sum(jnp.where(used, edge_float, 0.0)),
            jnp.sum(inverse[...]),
        ]
    )

    def keep_totals(block):
        totals[...] = block

    moves.under_way["tot"] = sum_steps(
        place, Wire(sum_send.at[0], sum_recv.at[0]), (sum_out, sum_in, sum_plane, sum_line), 0, keep_totals
    )
    moves.play("slots")

    term = jnp.where(used, COMMON / edge_float, 0.0)
    summed = jnp.zeros(nbr.shape, f32)
    for k in range(nbr.shape[0]):
        summed = summed + jnp.where(nbr[k : k + 1, :] == nbr[...], term[k : k + 1, :], 0.0)
    terms[...] = summed

    @pl.loop(0, nodes // 256)
    def _(block_at):
        lanes = pl.ds(pl.multiple_of(block_at * 256, 256), 256)
        ids = [jnp.broadcast_to(nbr[k : k + 1, lanes], (16, 256)).astype(jnp.int16) for k in range(8)]
        values = [jnp.broadcast_to(terms[k : k + 1, lanes], (16, 256)).astype(bf16) for k in range(8)]

        @pl.loop(0, nodes // 64)
        def _(at):
            for part in range(4):
                row = pl.multiple_of(at * 64 + part * 16, 16)
                own = (lax.broadcasted_iota(jnp.int32, (16, 256), 0) + row).astype(jnp.int16)
                block = jnp.zeros((16, 256), bf16)
                for k in range(8):
                    block = jnp.where(ids[k] == own, values[k], block)
                matrix[pl.ds(row, 16), lanes] = block

        moves.after("build", block_at, nodes // 256)

    scale[...] = scale[...] * (totals[1:2, 0:1] / totals[0:1, 0:1])
    feat_copy.wait()

    def tile_at(at):
        return pl.multiple_of(at * TILE, TILE)

    def wide(at):
        return pl.ds(pl.multiple_of(at * WIDE, WIDE), WIDE)

    def inside(at):
        return slice(at * 128, at * 128 + 128)

    def lanes_of(start):
        return lambda at: pl.ds(pl.multiple_of(start + at * 128, 128), 128)

    def block_of(at, block):
        return pl.ds(pl.multiple_of(at * TILE + block * 256, 256), 256)

    def parts_of(depth):
        return [slice(at, at + 256) for at in range(0, depth, 256)]

    @pl.loop(0, wide_steps)
    def _(at):
        tile = wide(at)
        hid_0[:, tile] = dot_nn(win[...].reshape(width, -1), feat[:, tile]).astype(bf16)
        moves.after("first", at, wide_steps)

    def pair_of(layer):
        return weights[layer, 0].reshape(2 * width, width)

    def proj_of(layer):
        return weights[layer, 1].reshape(2 * width, width)

    def pool_tile(layer, tile):
        pooled[layer][:, tile] = (
            dot_nn(hidden[layer][...], matrix[:, tile]) * scale[:, tile]
        ).astype(bf16)

    def join_tile(layer, tile):
        pair = pair_of(layer)
        joined[layer][0:width, tile] = dot_nn(pair[:width], hidden[layer][:, tile]).astype(bf16)
        joined[layer][width:, tile] = dot_nn(pair[width:], pooled[layer][:, tile]).astype(bf16)

    def pool_and_join(layer):
        @pl.loop(0, wide_steps)
        def _(at):
            pool_tile(layer, wide(at))
            moves.after(f"pool{layer}", at, wide_steps)

        @pl.loop(0, wide_steps)
        def _(at):
            join_tile(layer, wide(at))
            moves.after(f"join{layer}", at, wide_steps)

        turned[...] = proj_of(layer).T

    for layer in range(LAYERS - 1):
        pool_and_join(layer)

        def normed(source, at, layer=layer):
            return forward_pieces(
                source, active, scales.at[layer], hidden[layer + 1], inside, lanes_of(tile_at(at))
            )

        @pl.loop(0, steps // 2)
        def _(pair, layer=layer):
            for odd in range(2):
                at = pair * 2 + odd
                here, there = (back, top_pre) if odd == 0 else (top_pre, back)

                def store(rows, block, value, at=at, here=here):
                    here[rows, block * 256 : block * 256 + 256] = value
                    pre[layer][rows, block_of(at, block)] = value

                terms = [
                    lambda rows, block, at=at, part=part: dot_nn(
                        turned[rows, part], joined[layer][part, block_of(at, block)]
                    )
                    for part in parts_of(2 * width)
                ]
                weave(dot_pieces(terms, store), normed(there, jnp.maximum(at - 1, 0)))
                moves.after(f"pre{layer}", pair, steps // 2, odd, 2)

        for piece in normed(top_pre, steps - 1):
            piece()
        moves.play(f"norm{layer}")

    pool_and_join(top)
    head_grad[...] = jnp.zeros_like(head_grad)
    losses[...] = jnp.zeros_like(losses)
    class_row = lax.broadcasted_iota(jnp.int32, (48, TILE), 0)

    def loss_tile(at):
        start = tile_at(at)
        tile = pl.ds(start, TILE)
        head_rows = head[...].reshape(width, 128)
        for piece in forward_pieces(top_pre, active, top_scale, last, inside, inside):
            piece()
        logits = jnp.where(class_row < classes, dot_nn(head_rows.T[0:48], last[...]), -1e30)
        most = jnp.max(logits, axis=0, keepdims=True)
        log_total = jnp.log(jnp.sum(jnp.exp(logits - most), axis=0, keepdims=True)) + most
        target = class_row == labels[:, tile]
        picked = jnp.sum(jnp.where(target, logits, 0.0), axis=0, keepdims=True)
        loss = jnp.sum(inverse[:, tile] * (log_total - picked), axis=1, keepdims=True)
        losses[...] = losses[...] + loss
        weight = inverse[:, tile] / totals[2:3, 0:1]
        grad_logits = (weight * (jnp.exp(logits - log_total) - target.astype(f32))).astype(bf16)
        grad_logits = jnp.concatenate([grad_logits, jnp.zeros((80, TILE), bf16)], axis=0)
        head_grad[...] = head_grad[...] + dot_nt(last[...], grad_logits)
        back[...] = dot_nn(head_rows, grad_logits)
        to_feat = feat.at[:, tile]
        for piece in backward_pieces(back, top_pre, active, slope, top_scale, to_feat, inside, inside, inside):
            piece()

    @pl.loop(0, steps)
    def _(at):
        top_pre[...] = dot_nn(turned[...], joined[top][:, pl.ds(tile_at(at), TILE)])
        loss_tile(at)

    hd_g[...] = head_grad[...].astype(bf16).reshape(hd_g.shape)
    sum_out[1] = jnp.broadcast_to(losses[0:1, 0:1], (8, 128))

    def keep_loss(block):
        rows = lax.broadcasted_iota(jnp.int32, (8, 128), 0)
        all_nodes = float(nodes * 32)
        weight_mean = (totals[0:1, :] * totals[2:3, :]) / (all_nodes * all_nodes)
        scal_out[...] = jnp.where(rows == 0, block / totals[2:3, :], weight_mean)

    moves.under_way["los"] = sum_steps(
        place, Wire(sum_send.at[1], sum_recv.at[1]), (sum_out, sum_in, sum_plane, sum_line), 1, keep_loss
    )

    def keep_head(value):
        ghead_out[...] = value[:, 0:classes]

    moves.under_way["rh"] = small_scatter_steps(
        place, Wire(scatter_send.at[0], scatter_recv.at[0]),
        (hd_g, hd_rc, hd_ocol, hd_icol, hd_oz, hd_iz, hd_own), keep_head,
    )
    moves.play("loss")

    def big_steps(chunk, slot, target, layer):
        def keep(value):
            target[layer] = value

        return scatter_steps(
            place, Wire(scatter_send.at[chunk], scatter_recv.at[chunk]),
            (big_g, big_rc, big_oh, big_ih, big_ocol, big_icol, big_oz, big_iz, big_own), slot, keep,
            free=free, reuses=layer < top, reused=layer > 0,
        )

    def grad_block(slot, at, left, right):
        rows = pl.ds(pl.multiple_of(at * 512, 512), 512)
        grad = dot_nt(left[rows, :], right).astype(bf16)
        big_g[slot, pl.ds(at * 2, 2)] = grad.reshape(2, *big_g.shape[2:])

    for layer in reversed(range(LAYERS)):
        chunk = 1 + 2 * (top - layer)
        grad = feat.at[0:width] if layer == top else hidden[layer + 1]

        moves.under_way[f"P{layer}"] = big_steps(chunk, 0, gproj_out, layer)
        moves.under_way[f"Q{layer}"] = big_steps(chunk + 1, 1, gpair_out, layer)

        @pl.loop(0, 2)
        def _(at, layer=layer, grad=grad):
            grad_block(0, at, joined[layer], grad[...])
            moves.after(f"A{layer}", at, 2)

        @pl.loop(0, wide_steps)
        def _(at, layer=layer, grad=grad):
            joined[layer][:, wide(at)] = dot_nn(proj_of(layer), grad[:, wide(at)]).astype(bf16)
            moves.after(f"B{layer}", at, wide_steps)

        if layer == top:
            feat_copy = pltpu.make_async_copy(feat_hbm, feat, feat_sem)
            feat_copy.start()

        grad_block(1, 0, joined[layer], hidden[layer][...])
        moves.play(f"C{layer}", 0)
        grad_block(1, 1, joined[layer], pooled[layer][...])
        moves.play(f"C{layer}", 1)
        turned[...] = pair_of(layer).T

        @pl.loop(0, wide_steps)
        def _(at, layer=layer):
            tile = wide(at)
            pooled[layer][:, tile] = (
                dot_nn(turned[:, width:], joined[layer][width:, tile]) * scale[:, tile]
            ).astype(bf16)
            moves.after(f"D{layer}", at, wide_steps)

        def product(at, layer=layer):
            return [
                lambda rows, block, part=part: dot_nn(
                    turned[rows, part], joined[layer][part, block_of(at, block)]
                )
                for part in parts_of(width)
            ] + [
                lambda rows, block, part=part: dot_nt(
                    pooled[layer][rows, part], matrix[block_of(at, block), part]
                )
                for part in parts_of(nodes)
            ]

        if layer == 0:

            @pl.loop(0, steps)
            def _(at):
                def store(rows, block, value):
                    hid_0[rows, block_of(at, block)] = value.astype(bf16)

                weave(dot_pieces(product(at), store), [])
                moves.after("E0", at, steps)

            continue

        def pulled(source, at, layer=layer):
            lanes = lanes_of(tile_at(at))
            return backward_pieces(
                source, pre[layer - 1], active, slope, scales.at[layer - 1], hidden[layer], inside, lanes, lanes
            )

        @pl.loop(0, steps // 2)
        def _(pair, layer=layer):
            for odd in range(2):
                at = pair * 2 + odd
                here, there = (back, top_pre) if odd == 0 else (top_pre, back)

                def store(rows, block, value, here=here):
                    here[rows, block * 256 : block * 256 + 256] = value

                weave(dot_pieces(product(at), store), pulled(there, jnp.maximum(at - 1, 0)))
                moves.after(f"E{layer}", pair, steps // 2, odd, 2)

        for piece in pulled(top_pre, steps - 1):
            piece()

    def keep_in(columns):
        def keep(value):
            gin_out[:, columns] = value

        return keep

    feat_copy.wait()
    for at, (name, bufs, columns) in enumerate(
        [
            ("ra", (ina_g, ina_rc, ina_ocol, ina_icol, ina_oz, ina_iz, ina_own), slice(0, SPLIT)),
            ("rb", (inb_g, inb_rc, inb_ocol, inb_icol, inb_oz, inb_iz, inb_own), slice(SPLIT, features)),
        ]
    ):

        @pl.loop(0, 2)
        def _(half, bufs=bufs, columns=columns):
            rows = pl.ds(pl.multiple_of(half * 256, 256), 256)
            grad = dot_nt(hid_0[rows, :], feat[columns, :]).astype(bf16)
            bufs[0][pl.ds(half * 2, 2)] = grad.reshape(2, *bufs[0].shape[1:])

        moves.under_way[name] = small_scatter_steps(
            place, Wire(scatter_send.at[7 + at], scatter_recv.at[7 + at]), bufs, keep_in(columns)
        )
        moves.play("inputs", at)
    for wire in gather_wires:
        wire.finish()


def scatter_buffers(rows, columns, slots):
    def buf(*shape):
        return pltpu.VMEM((slots, *shape, rows, columns), bf16)

    return [
        buf(4, 2, 2, 2), buf(4, 2, 2), buf(2, 2), buf(2, 2), buf(2, 4), buf(2, 4), buf(3), buf(3),
        pltpu.VMEM((slots, rows, columns), f32),
    ]


def small_scatter_buffers(rows, columns):
    def buf(*shape):
        return pltpu.VMEM((*shape, rows, columns), bf16)

    return [
        buf(4, 2, 2, 2), buf(4, 2, 2), buf(3, 4), buf(3, 4), buf(3), buf(3),
        pltpu.VMEM((rows, columns), f32),
    ]


def train(feat, nbr, edge, degree, counts, labels, live, win, pair, proj, head):
    features, nodes = feat.shape
    width = pair.shape[2]
    classes = head.shape[1]
    vmem = pl.BlockSpec(memory_space=pltpu.VMEM)
    dma = pltpu.SemaphoreType.DMA
    return pl.pallas_call(
        train_kernel,
        out_shape=[
            jax.ShapeDtypeStruct(win.shape, f32),
            jax.ShapeDtypeStruct(pair.shape, f32),
            jax.ShapeDtypeStruct(proj.shape, f32),
            jax.ShapeDtypeStruct(head.shape, f32),
            jax.ShapeDtypeStruct((8, 128), f32),
        ],
        in_specs=[pl.BlockSpec(memory_space=pl.ANY)] + [vmem] * 10,
        out_specs=[vmem] * 5,
        scratch_shapes=[
            pltpu.VMEM((nodes, nodes), bf16),
            pltpu.VMEM((features, nodes), bf16),
        ]
        + [pltpu.VMEM((width, nodes), bf16)] * 3
        + [pltpu.VMEM((width, nodes), bf16)] * 3
        + [pltpu.VMEM((2 * width, nodes), bf16)] * 3
        + [pltpu.VMEM((width, nodes), f32)] * 2
        + [
            pltpu.VMEM((4, 2, 2, 2, 16, features), bf16),
            pltpu.VMEM((LAYERS, 2, 4, 2, 2, 2, 32, width), bf16),
            pltpu.VMEM((4, 2, 2, 2, 16, 128), bf16),
            pltpu.VMEM((width, 2 * width), bf16),
            pltpu.VMEM((width, 128), f32),
            pltpu.VMEM((1, nodes), f32),
            pltpu.VMEM((1, nodes), f32),
            pltpu.VMEM((8, nodes), f32),
            pltpu.VMEM((8, 128), f32),
            pltpu.VMEM((8, 128), f32),
            pltpu.VMEM((LAYERS, 1, nodes), f32),
            pltpu.VMEM((width, TILE), f32),
            pltpu.VMEM((width, TILE), f32),
            pltpu.VMEM((width, TILE), bf16),
            pltpu.VMEM((2, width, 128), f32),
            pltpu.VMEM((2, width, 128), f32),
            pltpu.VMEM((1, TILE), f32),
        ]
        + scatter_buffers(32, width, 2)
        + small_scatter_buffers(16, SPLIT)
        + small_scatter_buffers(16, features - SPLIT)
        + small_scatter_buffers(16, 128)
        + [
            pltpu.VMEM((2, 8, 128), f32),
            pltpu.VMEM((2, 8, 128), f32),
            pltpu.VMEM((2, 2, 2, 8, 128), f32),
            pltpu.VMEM((2, 4, 8, 128), f32),
            dma((9, 11)), dma((9, 11)), dma((9, 8)), dma((9, 8)), dma((2, 7)), dma((2, 7)), dma,
            pltpu.SemaphoreType.REGULAR((2, 6)),
        ],
        compiler_params=pltpu.CompilerParams(
            collective_id=0, has_side_effects=True, vmem_limit_bytes=64 * 2**20
        ),
        cost_estimate=pl.CostEstimate(
            flops=67 * 10**9, bytes_accessed=10**7, transcendentals=10**7
        ),
    )(feat, nbr, edge, degree, counts, labels, live, win, pair, proj, head)


def update_kernel(scalars, *refs):
    inputs, outs = refs[:16], refs[16:]
    outs[16][0, 0] = scalars[0, 0]
    outs[17][0, 0] = scalars[1, 0]
    for at in range(4):
        weight, first, second, grad = (inputs[at + 4 * kind][...] for kind in range(4))
        new, first_new, second_new = adamw_update(weight, first, second, grad)
        outs[at][...] = new
        outs[4 + at][...] = first_new
        outs[8 + at][...] = second_new
        outs[12 + at][...] = new.astype(bf16)


def update(scalars, weights, firsts, seconds, grads):
    shapes = [jax.ShapeDtypeStruct(w.shape, f32) for w in weights]
    vmem = pl.BlockSpec(memory_space=pltpu.VMEM)
    smem = pl.BlockSpec(memory_space=pltpu.SMEM)
    return pl.pallas_call(
        update_kernel,
        out_shape=shapes * 3
        + [jax.ShapeDtypeStruct(w.shape, bf16) for w in weights]
        + [jax.ShapeDtypeStruct((1, 1), f32)] * 2,
        in_specs=[smem] + [vmem] * 16,
        out_specs=[vmem] * 16 + [smem] * 2,
    )(scalars, *weights, *firsts, *seconds, *grads)


def turned_first(array):
    return jnp.swapaxes(array, -1, -2)


def body(
    features, labels, neighbors, degree, node_counts, edge_counts, live_nodes,
    input_weight, pair_weight, proj_weight, head_weight,
    input_first, pair_first, proj_first, head_first,
    input_second, pair_second, proj_second, head_second,
):
    def owned(input_w, pair_w, proj_w, head_w):
        return (turned_first(input_w), turned_first(pair_w), proj_w, head_w)

    weights = owned(input_weight, pair_weight, proj_weight, head_weight)
    *grads, scalars = train(
        turned_first(features), turned_first(neighbors), turned_first(edge_counts),
        degree[None, :], node_counts[None, :], labels[None, :], live_nodes[None, :], *weights,
    )
    *results, mean_loss, weight_mean = update(
        scalars,
        weights,
        owned(input_first, pair_first, proj_first, head_first),
        owned(input_second, pair_second, proj_second, head_second),
        grads,
    )
    placed = []
    for kind in range(4):
        placed += owned(*results[4 * kind : 4 * kind + 4])
    return (mean_loss.reshape(()), weight_mean.reshape(()), *placed)


def normalize(preact):
    active = jax.nn.gelu(preact)
    return active * lax.rsqrt(jnp.mean(active * active, axis=-1, keepdims=True) + norm_eps)


def slot_terms(neighbors, degree, live_count):
    count_nodes, fanout = neighbors.shape
    node_live = jnp.arange(count_nodes, dtype=jnp.int32) < live_count
    used = (
        (jnp.arange(fanout, dtype=jnp.int32)[None, :] < degree[:, None])
        & (neighbors < live_count)
        & node_live[:, None]
    )
    return (node_live, used)


def coefficients(used, node_counts, edge_counts, total_node, total_edge):
    node_float = node_counts.astype(jnp.float32)
    edge_float = edge_counts.astype(jnp.float32)
    spread = jnp.maximum(jnp.sum(used.astype(jnp.float32), axis=1), 1.0)
    value = node_float[:, None] * total_edge / (edge_float * total_node * spread[:, None])
    return jnp.where(used, value, 0.0)


def contract_rows(left, right):
    return lax.dot_general(
        left, right, (((0,), (0,)), ((), ())), preferred_element_type=jnp.float32
    )


def contract_cols(left, right):
    return lax.dot_general(
        left, right, (((1,), (1,)), ((), ())), preferred_element_type=jnp.float32
    )


def coef_matrix(neighbors, coefs):
    count_nodes = neighbors.shape[0]
    columns = lax.iota(jnp.int32, count_nodes)[None, :]
    matrix = jnp.zeros((count_nodes, count_nodes), jnp.float32)
    for neighbor_slot in range(neighbors.shape[1]):
        matrix = matrix + jnp.where(
            neighbors[:, neighbor_slot : neighbor_slot + 1] == columns,
            coefs[:, neighbor_slot : neighbor_slot + 1],
            0.0,
        )
    return matrix


def layer_forward(hidden, pair_w, proj_w, matrix):
    width = pair_w.shape[0]
    pooled = jnp.dot(
        matrix,
        hidden.astype(jnp.float32),
        precision=lax.Precision.HIGHEST,
        preferred_element_type=jnp.float32,
    ).astype(jnp.bfloat16)
    self_part = jnp.dot(hidden, pair_w[:, :width], preferred_element_type=jnp.float32)
    nbr_part = jnp.dot(pooled, pair_w[:, width:], preferred_element_type=jnp.float32)
    joined = jnp.concatenate([self_part, nbr_part], axis=1).astype(jnp.bfloat16)
    preact = jnp.dot(joined, proj_w, preferred_element_type=jnp.float32)
    return (normalize(preact).astype(jnp.bfloat16), (hidden, pooled, joined, preact))


def layer_backward(grad_out, saved, pair_w, proj_w, matrix):
    hidden, pooled, joined, preact = saved
    width = pair_w.shape[0]
    _, pullback = jax.vjp(normalize, preact)
    grad_preact = pullback(grad_out)[0].astype(jnp.bfloat16)
    grad_proj = contract_rows(joined, grad_preact)
    grad_joined = contract_cols(grad_preact, proj_w).astype(jnp.bfloat16)
    grad_pair = jnp.concatenate(
        [
            contract_rows(hidden, grad_joined[:, :width]),
            contract_rows(pooled, grad_joined[:, width:]),
        ],
        axis=1,
    )
    grad_hidden = contract_cols(grad_joined[:, :width], pair_w[:, :width])
    grad_pooled = contract_cols(grad_joined[:, width:], pair_w[:, width:])
    grad_hidden = grad_hidden + lax.dot_general(
        matrix,
        grad_pooled,
        (((0,), (0,)), ((), ())),
        precision=lax.Precision.HIGHEST,
        preferred_element_type=jnp.float32,
    )
    return (grad_hidden, grad_pair, grad_proj)


def plain_body(
    features,
    labels,
    neighbors,
    degree,
    node_counts,
    edge_counts,
    live_nodes,
    input_weight,
    pair_weight,
    proj_weight,
    head_weight,
    input_first,
    pair_first,
    proj_first,
    head_first,
    input_second,
    pair_second,
    proj_second,
    head_second,
):
    count_nodes = features.shape[0]
    all_nodes = jnp.float32(count_nodes * lax.axis_size(("dp", "group")))
    node_live, used = slot_terms(neighbors, degree, live_nodes[0])
    node_float = node_counts.astype(jnp.float32)
    node_local = jnp.sum(jnp.where(node_live, node_float, 0.0))
    edge_local = jnp.sum(jnp.where(used, edge_counts.astype(jnp.float32), 0.0))
    total_node, total_edge = lax.psum((node_local, edge_local), ("dp", "group"))
    weights = jnp.where(node_live, total_node / (node_float * all_nodes), 0.0)
    coefs = coefficients(used, node_counts, edge_counts, total_node, total_edge)
    matrix = coef_matrix(neighbors, coefs)
    input_b, pair_b, proj_b, head_b = (
        lax.all_gather(input_weight.astype(jnp.bfloat16), ("dp", "group"), axis=1, tiled=True),
        lax.all_gather(pair_weight.astype(jnp.bfloat16), ("dp", "group"), axis=2, tiled=True),
        lax.all_gather(proj_weight.astype(jnp.bfloat16), ("dp", "group"), axis=1, tiled=True),
        lax.all_gather(head_weight.astype(jnp.bfloat16), ("dp", "group"), axis=0, tiled=True),
    )
    hidden = jnp.dot(features, input_b, preferred_element_type=jnp.float32).astype(jnp.bfloat16)
    kept = []
    for layer_index in range(LAYERS):
        hidden, saved = layer_forward(hidden, pair_b[layer_index], proj_b[layer_index], matrix)
        kept.append(saved)
    logits = jnp.dot(hidden, head_b, preferred_element_type=jnp.float32)
    log_total = jax.nn.logsumexp(logits, axis=1)
    targets = (labels[:, None] == lax.iota(jnp.int32, logits.shape[1])[None, :]).astype(jnp.float32)
    loss_local = jnp.sum(weights * (log_total - jnp.sum(logits * targets, axis=1)))
    loss_sum, weight_sum = lax.psum((loss_local, jnp.sum(weights)), ("dp", "group"))
    grad_logits = (
        (weights / weight_sum)[:, None] * (jnp.exp(logits - log_total[:, None]) - targets)
    ).astype(jnp.bfloat16)
    grad_head = contract_rows(hidden, grad_logits)
    grad_hidden = contract_cols(grad_logits, head_b)
    pair_grads = [None] * LAYERS
    proj_grads = [None] * LAYERS
    for layer_index in reversed(range(LAYERS)):
        grad_hidden, grad_pair, grad_proj = layer_backward(
            grad_hidden, kept[layer_index], pair_b[layer_index], proj_b[layer_index], matrix
        )
        pair_grads[layer_index] = grad_pair
        proj_grads[layer_index] = grad_proj
    grad_input = contract_rows(features, grad_hidden.astype(jnp.bfloat16))
    grad_input, grad_pairs, grad_projs, grad_head = (
        lax.psum_scatter(grad_input, ("dp", "group"), scatter_dimension=1, tiled=True),
        lax.psum_scatter(jnp.stack(pair_grads), ("dp", "group"), scatter_dimension=2, tiled=True),
        lax.psum_scatter(jnp.stack(proj_grads), ("dp", "group"), scatter_dimension=1, tiled=True),
        lax.psum_scatter(grad_head, ("dp", "group"), scatter_dimension=0, tiled=True),
    )
    input_new, input_first_new, input_second_new = adamw_update(
        input_weight, input_first, input_second, grad_input
    )
    pair_new, pair_first_new, pair_second_new = adamw_update(
        pair_weight, pair_first, pair_second, grad_pairs
    )
    proj_new, proj_first_new, proj_second_new = adamw_update(
        proj_weight, proj_first, proj_second, grad_projs
    )
    head_new, head_first_new, head_second_new = adamw_update(
        head_weight, head_first, head_second, grad_head
    )
    return (
        loss_sum / weight_sum,
        weight_sum / all_nodes,
        input_new,
        pair_new,
        proj_new,
        head_new,
        input_first_new,
        pair_first_new,
        proj_first_new,
        head_first_new,
        input_second_new,
        pair_second_new,
        proj_second_new,
        head_second_new,
        input_new.astype(jnp.bfloat16),
        pair_new.astype(jnp.bfloat16),
        proj_new.astype(jnp.bfloat16),
        head_new.astype(jnp.bfloat16),
    )


def solution(mesh):
    placed = (
        P(("dp", "group"), None),
        P(("dp", "group")),
        P(("dp", "group"), None),
        P(("dp", "group")),
        P(("dp", "group")),
        P(("dp", "group"), None),
        P(("dp", "group")),
        P(None, ("dp", "group")),
        P(None, None, ("dp", "group")),
        P(None, ("dp", "group"), None),
        P(("dp", "group"), None),
        P(None, ("dp", "group")),
        P(None, None, ("dp", "group")),
        P(None, ("dp", "group"), None),
        P(("dp", "group"), None),
        P(None, ("dp", "group")),
        P(None, None, ("dp", "group")),
        P(None, ("dp", "group"), None),
        P(("dp", "group"), None),
    )
    fits = dict(mesh.shape) == {"dp": 8, "group": 4}
    return jax.shard_map(
        body if fits else plain_body,
        mesh=mesh,
        in_specs=placed,
        out_specs=(
            P(),
            P(),
            P(None, ("dp", "group")),
            P(None, None, ("dp", "group")),
            P(None, ("dp", "group"), None),
            P(("dp", "group"), None),
            P(None, ("dp", "group")),
            P(None, None, ("dp", "group")),
            P(None, ("dp", "group"), None),
            P(("dp", "group"), None),
            P(None, ("dp", "group")),
            P(None, None, ("dp", "group")),
            P(None, ("dp", "group"), None),
            P(("dp", "group"), None),
            P(None, ("dp", "group")),
            P(None, None, ("dp", "group")),
            P(None, ("dp", "group"), None),
            P(("dp", "group"), None),
        ),
        check_vma=False,
    )
```

```python
import jax
import jax.numpy as jnp
from jax import lax
from jax.experimental import pallas as pl
from jax.experimental.pallas import tpu as pltpu
from jax.sharding import PartitionSpec as P

LAYERS = 3
STEP = 5
COMMON = 840.0

learn_rate = 0.03
beta_first = 0.5
beta_second = 0.5
adam_eps = 1e-08
decay_rate = 0.01
norm_eps = 1e-06

AXES = ("dp", "group")
MESH = pl.DeviceIdType.MESH
f32 = jnp.float32
bf16 = jnp.bfloat16
TILE = 512
WIDE = 1024
SPLIT = 384
ROWS = 64
GATE_IN = 0.7978845608028654
GATE_CUBE = GATE_IN * 0.044715


def dot_nn(left, right):
    return jnp.dot(left, right, preferred_element_type=f32)


def dot_nt(left, right):
    return lax.dot_general(left, right, (((1,), (1,)), ((), ())), preferred_element_type=f32)


def adamw_update(weight, first, second, grad):
    first_new = beta_first * first + (1.0 - beta_first) * grad
    second_new = beta_second * second + (1.0 - beta_second) * grad * grad
    first_hat = first_new / (1.0 - beta_first**STEP)
    second_hat = second_new / (1.0 - beta_second**STEP)
    weight_new = weight - learn_rate * (
        first_hat / (jnp.sqrt(second_hat) + adam_eps) + decay_rate * weight
    )
    return (weight_new, first_new, second_new)


class Place:
    def __init__(self):
        dp, group = lax.axis_index("dp"), lax.axis_index("group")
        self.z, self.y = dp // 2, dp % 2
        self.x, self.c = group // 2, group % 2
        self.far_y, self.far_x, self.far_c = 1 - self.y, 1 - self.x, 1 - self.c
        self.sibling = (dp, group + 1 - 2 * self.c)
        self.beside_x = (dp, group + 2 - 4 * self.x)
        self.beside_y = (dp + 1 - 2 * self.y, group)
        self.later_z = [(self.z + step) % 4 for step in (1, 2, 3)]
        self.earlier_z = [(self.z + 4 - step) % 4 for step in (1, 2, 3)]
        self.to_z = [(at * 2 + self.y, group) for at in self.later_z]
        self.from_z = [(at * 2 + self.y, group) for at in self.earlier_z]

    def partners(self):
        return [self.sibling, self.beside_x, self.beside_y] + self.to_z


class Wire:
    def __init__(self, send_sems, recv_sems):
        self.send_sems, self.recv_sems = send_sems, recv_sems
        self.sent = []

    def copy(self, at, source, target, device):
        return pltpu.make_async_remote_copy(
            src_ref=source(),
            dst_ref=target(),
            send_sem=self.send_sems.at[at],
            recv_sem=self.recv_sems.at[at],
            device_id=device,
            device_id_type=MESH,
        )

    def send(self, at, source, target, device):
        self.copy(at, source, target, device).start()
        self.sent.append((at, source, target, device))

    def arrived(self, at, target, device):
        self.copy(at, target, target, device).wait_recv()

    def finish(self, below=100):
        for sent in self.sent:
            if sent[0] < below:
                self.copy(*sent).wait_send()
        self.sent = [sent for sent in self.sent if sent[0] >= below]


def gather_steps(place, wire, region):
    z, y, x, c = place.z, place.y, place.x, place.c
    fy, fx, fc = place.far_y, place.far_x, place.far_c
    whole, low, high = slice(0, 4), slice(0, 2), slice(2, 4)

    def at(*index):
        return lambda: region(*index)

    def send(sem, index, device):
        wire.send(sem, at(*index), at(*index), device)

    for step in range(3):
        send(step, (z, y, x, c), place.to_z[step])
    yield
    for step in range(3):
        wire.arrived(step, at(place.earlier_z[step], y, x, c), place.from_z[step])
    send(3, (whole, y, x, c), place.beside_x)
    send(4, (whole, y, x, c), place.beside_y)
    send(5, (whole, y, x, c), place.sibling)
    yield
    wire.arrived(3, at(whole, y, fx, c), place.beside_x)
    send(6, (low, y, fx, c), place.beside_y)
    send(8, (whole, y, fx, c), place.sibling)
    wire.arrived(4, at(whole, fy, x, c), place.beside_y)
    send(7, (high, fy, x, c), place.beside_x)
    send(9, (whole, fy, x, c), place.sibling)
    yield
    wire.arrived(6, at(low, fy, fx, c), place.beside_y)
    wire.arrived(7, at(high, fy, fx, c), place.beside_x)
    send(10, (whole, fy, fx, c), place.sibling)
    yield
    wire.arrived(5, at(whole, y, x, fc), place.sibling)
    wire.arrived(8, at(whole, y, fx, fc), place.sibling)
    wire.arrived(9, at(whole, fy, x, fc), place.sibling)
    wire.arrived(10, at(whole, fy, fx, fc), place.sibling)
    yield


def scatter_steps(place, wire, bufs, slot, store, free=None, reuses=False, reused=False):
    grads, from_core, out_half, in_half, out_col, in_col, out_z, in_z, own = bufs
    z, y, x, c = place.z, place.y, place.x, place.c
    fy, fx, fc = place.far_y, place.far_x, place.far_c
    low, high = slice(0, 2), slice(2, 4)

    def at(buf, *index):
        return lambda: buf.at[(slot, *index)]

    def both(zs, yy, xx):
        return grads[slot, zs, yy, xx, c].astype(f32) + from_core[slot, zs, yy, xx].astype(f32)

    def until_free(*partners):
        if reuses:
            for partner in partners:
                pl.semaphore_wait(free.at[slot, partner], 1)

    def set_free(*partners):
        for partner, device in partners:
            pl.semaphore_signal(free.at[slot, partner], inc=1, device_id=device, device_id_type=MESH)

    until_free(0)
    wire.send(0, at(grads, slice(0, 4), slice(0, 2), slice(0, 2), fc), at(from_core), place.sibling)
    yield
    wire.arrived(0, at(from_core), place.sibling)
    until_free(1, 2)
    out_half[slot, 0] = both(low, fy, fx).astype(bf16)
    wire.send(1, at(out_half, 0), at(in_half, 0), place.beside_x)
    out_half[slot, 1] = both(high, fy, fx).astype(bf16)
    wire.send(2, at(out_half, 1), at(in_half, 1), place.beside_y)
    yield
    wire.arrived(1, at(in_half, 0), place.beside_x)
    out_col[slot, 1, low] = (both(low, fy, x) + in_half[slot, 0].astype(f32)).astype(bf16)
    out_col[slot, 1, high] = both(high, fy, x).astype(bf16)
    wire.send(4, at(out_col, 1), at(in_col, 1), place.beside_y)
    wire.arrived(2, at(in_half, 1), place.beside_y)
    out_col[slot, 0, low] = both(low, y, fx).astype(bf16)
    out_col[slot, 0, high] = (both(high, y, fx) + in_half[slot, 1].astype(f32)).astype(bf16)
    wire.send(3, at(out_col, 0), at(in_col, 0), place.beside_x)
    yield
    wire.arrived(3, at(in_col, 0), place.beside_x)
    wire.arrived(4, at(in_col, 1), place.beside_y)

    def column(zz):
        beside = in_col[slot, 0, zz].astype(f32) + in_col[slot, 1, zz].astype(f32)
        return both(zz, y, x) + beside

    until_free(3, 4, 5)
    own[slot] = column(z)
    for step in range(3):
        out_z[slot, step] = column(place.later_z[step]).astype(bf16)
        wire.send(5 + step, at(out_z, step), at(in_z, step), place.to_z[step])
    wire.finish(5)
    if reused:
        set_free((0, place.sibling))
    yield
    for step in range(3):
        wire.arrived(5 + step, at(in_z, step), place.from_z[step])
    others = in_z[slot, 0].astype(f32) + in_z[slot, 1].astype(f32) + in_z[slot, 2].astype(f32)
    store(own[slot] + others)
    wire.finish()
    if reused:
        set_free(*enumerate([place.beside_x, place.beside_y] + place.from_z, 1))
    yield


def sum_steps(place, wire, bufs, slot, store):
    out, arrive, line = bufs

    def at(buf, *index):
        return lambda: buf.at[(slot, *index)]

    for stage, device in enumerate((place.sibling, place.beside_x, place.beside_y)):
        wire.send(stage, at(out, stage), at(arrive, stage), device)
        yield
        wire.arrived(stage, at(arrive, stage), device)
        if stage < 2:
            out[slot, stage + 1] = out[slot, stage] + arrive[slot, stage]
        else:
            line[slot, place.z] = out[slot, stage] + arrive[slot, stage]
    for step in range(3):
        wire.send(3 + step, at(line, place.z), at(line, place.z), place.to_z[step])
    yield
    for step in range(3):
        wire.arrived(3 + step, at(line, place.earlier_z[step]), place.from_z[step])
    store((line[slot, 0] + line[slot, 1]) + (line[slot, 2] + line[slot, 3]))
    wire.finish()
    yield


PLAN = {
    ("start", 0): ("ia", "ib",),
    ("slots", 0): ("tot",),
    ("build", 0): ("tot",),
    ("build", 1): ("ia", "p0",),
    ("build", 2): ("ib", "q0",),
    ("build", 3): ("tot",),
    ("build", 5): ("ia",),
    ("build", 6): ("ib", "tot",),
    ("build", 7): ("p0", "p1", "ia", "ib", "ia", "tot", "ib",),
    ("first", 0): ("q0", "q1",),
    ("first", 1): ("p0",),
    ("pool0", 0): ("p1", "p2",),
    ("pool0", 1): ("p0", "q0", "q1", "q2", "p0",),
    ("join0", 0): ("p1", "p2", "wh",),
    ("join0", 1): ("q0", "q0",),
    ("pre0", 0): ("q1", "q2", "wh",),
    ("pre0", 1): ("p1",),
    ("norm0", 6): ("p2",),
    ("pool1", 0): ("q1",),
    ("pool1", 1): ("q2", "wh", "p1",),
    ("join1", 0): ("p2",),
    ("join1", 1): ("q1",),
    ("pre1", 0): ("q2", "wh",),
    ("pool2", 1): ("p2",),
    ("join2", 1): ("q2", "wh",),
    ("loss", 0): ("rh", "los",),
    ("A2", 0): ("rh", "los",),
    ("A2", 1): ("P2",),
    ("B2", 0): ("rh", "los",),
    ("B2", 1): ("P2",),
    ("C2", 0): ("rh", "los",),
    ("C2", 1): ("Q2",),
    ("D2", 0): ("P2", "rh", "los",),
    ("D2", 1): ("Q2",),
    ("E2", 1): ("P2", "Q2",),
    ("E2", 3): ("P2", "Q2",),
    ("A1", 1): ("P1",),
    ("B1", 1): ("Q2", "P1",),
    ("C1", 1): ("Q1",),
    ("D1", 0): ("P1",),
    ("E1", 0): ("Q1",),
    ("E1", 1): ("P1",),
    ("E1", 2): ("Q1",),
    ("E1", 3): ("P1",),
    ("A0", 1): ("Q1", "P0",),
    ("B0", 1): ("P0",),
    ("C0", 1): ("Q1", "Q0",),
    ("D0", 0): ("P0",),
    ("E0", 0): ("Q0",),
    ("E0", 2): ("P0",),
    ("E0", 3): ("Q0",),
    ("inputs", 0): ("ra",),
    ("inputs", 1): ("rb", "ra", "P0", "rb", "Q0", "ra", "rb", "ra", "rb", "Q0", "ra", "rb",),
}


class Moves:
    def __init__(self):
        self.under_way = {}

    def play(self, label, at=0):
        for name in PLAN.get((label, at), ()):
            next(self.under_way[name])

    def after(self, label, at, count):
        for when in range(count):
            if (label, when) in PLAN:

                @pl.when(at == when)
                def _(when=when):
                    self.play(label, when)


def row_of_scalars(values):
    rows = lax.broadcasted_iota(jnp.int32, (8, 128), 0)
    block = jnp.zeros((8, 128), f32)
    for at, value in enumerate(values):
        block = jnp.where(rows == at, value, block)
    return block


def gelu(pre):
    square = pre * pre
    gate = 0.5 * jnp.tanh(pre * (GATE_CUBE * square + GATE_IN)) + 0.5
    return pre * gate, gate, square


def row_chunks():
    return [slice(at, at + ROWS) for at in range(0, 512, ROWS)]


def norm_forward(pre, active, scales, out, lanes, scale_lanes):
    square = jnp.zeros((ROWS, 128), f32)
    for row in row_chunks():
        value, _, _ = gelu(pre[row, lanes])
        active[row, :] = value
        square = square + value * value
    scale = lax.rsqrt(jnp.sum(square, axis=0, keepdims=True) * (1.0 / 512) + norm_eps)
    scales[:, scale_lanes] = scale
    for row in row_chunks():
        out[row, lanes] = (active[row, :] * scale).astype(bf16)


def norm_backward(grad, pre, active, slope, scales, out, grad_lanes, pre_lanes, lanes):
    scale = scales[:, lanes]
    along = jnp.zeros((ROWS, 128), f32)
    for row in row_chunks():
        value, gate, square = gelu(pre[row, pre_lanes])
        active[row, :] = value
        slope[row, :] = gate + value * (
            (1.0 - gate) * ((6.0 * GATE_CUBE) * square + 2.0 * GATE_IN)
        )
        along = along + value * grad[row, grad_lanes]
    pull = scale * scale * scale * (jnp.sum(along, axis=0, keepdims=True) * (1.0 / 512))
    for row in row_chunks():
        out[row, lanes] = (
            slope[row, :] * (scale * grad[row, grad_lanes] - active[row, :] * pull)
        ).astype(bf16)


def train_kernel(
    feat_hbm, nbr, edge, degree, counts, labels, live, win_own, pair_own, proj_own, head_own,
    gin_out, gpair_out, gproj_out, ghead_out, scal_out,
    matrix, feat, hid_0, hid_1, hid_2, pool_0, pool_1, pool_2, join_0, join_1, join_2, pre_0, pre_1,
    win, weights, head, turned, head_grad, scale, inverse, terms, totals, losses, scales,
    back, top_pre, last, active, slope,
    big_g, big_rc, big_oh, big_ih, big_ocol, big_icol, big_oz, big_iz, big_own,
    ina_g, ina_rc, ina_oh, ina_ih, ina_ocol, ina_icol, ina_oz, ina_iz, ina_own,
    inb_g, inb_rc, inb_oh, inb_ih, inb_ocol, inb_icol, inb_oz, inb_iz, inb_own,
    hd_g, hd_rc, hd_oh, hd_ih, hd_ocol, hd_icol, hd_oz, hd_iz, hd_own,
    sum_out, sum_in, sum_line,
    gather_send, gather_recv, scatter_send, scatter_recv, sum_send, sum_recv, feat_sem, free,
):
    place = Place()
    z, y, x, c = place.z, place.y, place.x, place.c
    nodes, width, classes = nbr.shape[1], hid_0.shape[0], head_own.shape[1]
    steps, wide_steps, chunks = nodes // TILE, nodes // WIDE, nodes // 128
    hidden, pooled, joined, pre = (
        [hid_0, hid_1, hid_2], [pool_0, pool_1, pool_2], [join_0, join_1, join_2], [pre_0, pre_1],
    )
    top, features = LAYERS - 1, feat.shape[0]

    barrier = pltpu.get_barrier_semaphore()
    for partner in place.partners():
        pl.semaphore_signal(barrier, inc=1, device_id=partner, device_id_type=MESH)

    feat_copy = pltpu.make_async_copy(feat_hbm, feat, feat_sem)
    feat_copy.start()
    win[z, y, x, c] = win_own[...].astype(bf16)
    for layer in range(LAYERS):
        weights[layer, 0, z, y, x, c] = pair_own[layer].astype(bf16)
        weights[layer, 1, z, y, x, c] = proj_own[layer].astype(bf16)
    head[z, y, x, c] = jnp.zeros(head.shape[4:], bf16)
    head[z, y, x, c, :, 0:classes] = head_own[...].astype(bf16)

    pl.semaphore_wait(barrier, 6)

    def region_of(layer, kind):
        return lambda zz, yy, xx, cc: weights.at[layer, kind, zz, yy, xx, cc]

    def region_of_input(columns):
        return lambda zz, yy, xx, cc: win.at[zz, yy, xx, cc, :, columns]

    regions = {
        "ia": region_of_input(slice(0, SPLIT)),
        "ib": region_of_input(slice(SPLIT, features)),
        "wh": lambda zz, yy, xx, cc: head.at[zz, yy, xx, cc],
    }
    for layer in range(LAYERS):
        regions[f"p{layer}"] = region_of(layer, 0)
        regions[f"q{layer}"] = region_of(layer, 1)
    moves = Moves()
    gather_wires = []
    for at, (name, region) in enumerate(regions.items()):
        gather_wires.append(Wire(gather_send.at[at], gather_recv.at[at]))
        moves.under_way[name] = gather_steps(place, gather_wires[-1], region)
    moves.play("start")

    node_live = lax.broadcasted_iota(jnp.int32, (1, nodes), 1) < live[...]
    slot = lax.broadcasted_iota(jnp.int32, nbr.shape, 0)
    used = (slot < degree[...]) & (nbr[...] < live[...]) & node_live
    edge_float = edge[...].astype(f32)
    count_float = counts[...].astype(f32)
    spread = jnp.maximum(jnp.sum(used.astype(f32), axis=0, keepdims=True), 1.0)
    inverse[...] = jnp.where(node_live, 1.0 / count_float, 0.0)
    scale[...] = count_float / (spread * COMMON)
    sum_out[0, 0] = row_of_scalars(
        [
            jnp.sum(jnp.where(node_live, count_float, 0.0)),
            jnp.sum(jnp.where(used, edge_float, 0.0)),
            jnp.sum(inverse[...]),
        ]
    )

    def keep_totals(block):
        totals[...] = block

    moves.under_way["tot"] = sum_steps(
        place, Wire(sum_send.at[0], sum_recv.at[0]), (sum_out, sum_in, sum_line), 0, keep_totals
    )
    moves.play("slots")

    term = jnp.where(used, COMMON / edge_float, 0.0)
    summed = jnp.zeros(nbr.shape, f32)
    for k in range(nbr.shape[0]):
        summed = summed + jnp.where(nbr[k : k + 1, :] == nbr[...], term[k : k + 1, :], 0.0)
    terms[...] = summed

    @pl.loop(0, nodes // 256)
    def _(block_at):
        lanes = pl.ds(pl.multiple_of(block_at * 256, 256), 256)
        ids = [jnp.broadcast_to(nbr[k : k + 1, lanes], (16, 256)).astype(jnp.int16) for k in range(8)]
        values = [jnp.broadcast_to(terms[k : k + 1, lanes], (16, 256)).astype(bf16) for k in range(8)]

        @pl.loop(0, nodes // 64)
        def _(at):
            for part in range(4):
                row = pl.multiple_of(at * 64 + part * 16, 16)
                own = (lax.broadcasted_iota(jnp.int32, (16, 256), 0) + row).astype(jnp.int16)
                block = jnp.zeros((16, 256), bf16)
                for k in range(8):
                    block = jnp.where(ids[k] == own, values[k], block)
                matrix[pl.ds(row, 16), lanes] = block

        moves.after("build", block_at, nodes // 256)

    scale[...] = scale[...] * (totals[1:2, 0:1] / totals[0:1, 0:1])
    feat_copy.wait()

    def tile_at(at):
        return pl.multiple_of(at * TILE, TILE)

    def wide(at):
        return pl.ds(pl.multiple_of(at * WIDE, WIDE), WIDE)

    def chunk_at(at, start=0):
        return pl.ds(pl.multiple_of(start + at * 128, 128), 128)

    @pl.loop(0, wide_steps)
    def _(at):
        tile = wide(at)
        hid_0[:, tile] = dot_nn(win[...].reshape(width, -1), feat[:, tile]).astype(bf16)
        moves.after("first", at, wide_steps)

    def pair_of(layer):
        return weights[layer, 0].reshape(2 * width, width)

    def proj_of(layer):
        return weights[layer, 1].reshape(2 * width, width)

    def pool_tile(layer, tile):
        pooled[layer][:, tile] = (
            dot_nn(hidden[layer][...], matrix[:, tile]) * scale[:, tile]
        ).astype(bf16)

    def join_tile(layer, tile):
        pair = pair_of(layer)
        joined[layer][0:width, tile] = dot_nn(pair[:width], hidden[layer][:, tile]).astype(bf16)
        joined[layer][width:, tile] = dot_nn(pair[width:], pooled[layer][:, tile]).astype(bf16)

    def pool_and_join(layer):
        @pl.loop(0, wide_steps)
        def _(at):
            pool_tile(layer, wide(at))
            moves.after(f"pool{layer}", at, wide_steps)

        @pl.loop(0, wide_steps)
        def _(at):
            join_tile(layer, wide(at))
            moves.after(f"join{layer}", at, wide_steps)

        turned[...] = proj_of(layer).T

    for layer in range(LAYERS - 1):
        pool_and_join(layer)

        @pl.loop(0, wide_steps)
        def _(at, layer=layer):
            pre[layer][:, wide(at)] = dot_nn(turned[...], joined[layer][:, wide(at)])
            moves.after(f"pre{layer}", at, wide_steps)

        @pl.loop(0, chunks // 2)
        def _(at, layer=layer):
            for part in range(2):
                lanes = chunk_at(at * 2 + part)
                norm_forward(pre[layer], active, scales.at[layer], hidden[layer + 1], lanes, lanes)
            moves.after(f"norm{layer}", at, chunks // 2)

    pool_and_join(top)
    head_grad[...] = jnp.zeros_like(head_grad)
    losses[...] = jnp.zeros_like(losses)
    class_row = lax.broadcasted_iota(jnp.int32, (48, TILE), 0)

    def loss_tile(at):
        start = tile_at(at)
        tile = pl.ds(start, TILE)
        head_rows = head[...].reshape(width, 128)
        for part in range(TILE // 128):
            inside = slice(part * 128, part * 128 + 128)
            norm_forward(top_pre, active, scales.at[top], last, inside, chunk_at(part, start))
        logits = jnp.where(class_row < classes, dot_nn(head_rows.T[0:48], last[...]), -1e30)
        most = jnp.max(logits, axis=0, keepdims=True)
        log_total = jnp.log(jnp.sum(jnp.exp(logits - most), axis=0, keepdims=True)) + most
        target = class_row == labels[:, tile]
        picked = jnp.sum(jnp.where(target, logits, 0.0), axis=0, keepdims=True)
        loss = jnp.sum(inverse[:, tile] * (log_total - picked), axis=1, keepdims=True)
        losses[...] = losses[...] + loss
        weight = inverse[:, tile] / totals[2:3, 0:1]
        grad_logits = (weight * (jnp.exp(logits - log_total) - target.astype(f32))).astype(bf16)
        grad_logits = jnp.concatenate([grad_logits, jnp.zeros((80, TILE), bf16)], axis=0)
        head_grad[...] = head_grad[...] + dot_nt(last[...], grad_logits)
        back[...] = dot_nn(head_rows, grad_logits)
        for part in range(TILE // 128):
            inside = slice(part * 128, part * 128 + 128)
            norm_backward(
                back, top_pre, active, slope, scales.at[top], feat.at[0:width], inside, inside, chunk_at(part, start)
            )

    @pl.loop(0, steps)
    def _(at):
        top_pre[...] = dot_nn(turned[...], joined[top][:, pl.ds(tile_at(at), TILE)])
        loss_tile(at)

    hd_g[0] = head_grad[...].astype(bf16).reshape(hd_g.shape[1:])
    sum_out[1, 0] = jnp.broadcast_to(losses[0:1, 0:1], (8, 128))

    def keep_loss(block):
        rows = lax.broadcasted_iota(jnp.int32, (8, 128), 0)
        all_nodes = float(nodes * 32)
        weight_mean = (totals[0:1, :] * totals[2:3, :]) / (all_nodes * all_nodes)
        scal_out[...] = jnp.where(rows == 0, block / totals[2:3, :], weight_mean)

    moves.under_way["los"] = sum_steps(
        place, Wire(sum_send.at[1], sum_recv.at[1]), (sum_out, sum_in, sum_line), 1, keep_loss
    )

    def keep_head(value):
        ghead_out[...] = value[:, 0:classes]

    moves.under_way["rh"] = scatter_steps(
        place, Wire(scatter_send.at[0], scatter_recv.at[0]),
        (hd_g, hd_rc, hd_oh, hd_ih, hd_ocol, hd_icol, hd_oz, hd_iz, hd_own), 0, keep_head,
    )
    moves.play("loss")

    def big_steps(chunk, slot, target, layer):
        def keep(value):
            target[layer] = value

        return scatter_steps(
            place, Wire(scatter_send.at[chunk], scatter_recv.at[chunk]),
            (big_g, big_rc, big_oh, big_ih, big_ocol, big_icol, big_oz, big_iz, big_own), slot, keep,
            free=free, reuses=layer < top, reused=layer > 0,
        )

    def grad_block(slot, at, left, right):
        rows = pl.ds(pl.multiple_of(at * 512, 512), 512)
        grad = dot_nt(left[rows, :], right).astype(bf16)
        big_g[slot, pl.ds(at * 2, 2)] = grad.reshape(2, *big_g.shape[2:])

    for layer in reversed(range(LAYERS)):
        chunk = 1 + 2 * (top - layer)
        grad = feat.at[0:width] if layer == top else hidden[layer + 1]

        moves.under_way[f"P{layer}"] = big_steps(chunk, 0, gproj_out, layer)
        moves.under_way[f"Q{layer}"] = big_steps(chunk + 1, 1, gpair_out, layer)

        @pl.loop(0, 2)
        def _(at, layer=layer, grad=grad):
            grad_block(0, at, joined[layer], grad[...])
            moves.after(f"A{layer}", at, 2)

        @pl.loop(0, wide_steps)
        def _(at, layer=layer, grad=grad):
            joined[layer][:, wide(at)] = dot_nn(proj_of(layer), grad[:, wide(at)]).astype(bf16)
            moves.after(f"B{layer}", at, wide_steps)

        if layer == top:
            feat_copy = pltpu.make_async_copy(feat_hbm, feat, feat_sem)
            feat_copy.start()

        grad_block(1, 0, joined[layer], hidden[layer][...])
        moves.play(f"C{layer}", 0)
        grad_block(1, 1, joined[layer], pooled[layer][...])
        moves.play(f"C{layer}", 1)
        turned[...] = pair_of(layer).T

        @pl.loop(0, wide_steps)
        def _(at, layer=layer):
            tile = wide(at)
            pooled[layer][:, tile] = (
                dot_nn(turned[:, width:], joined[layer][width:, tile]) * scale[:, tile]
            ).astype(bf16)
            moves.after(f"D{layer}", at, wide_steps)

        @pl.loop(0, steps)
        def _(at, layer=layer):
            tile = pl.ds(tile_at(at), TILE)
            back[...] = dot_nn(turned[:, :width], joined[layer][:width, tile])
            back[...] += dot_nt(pooled[layer][...], matrix[tile, :])
            if layer == 0:
                hidden[layer][:, tile] = back[...].astype(bf16)
            else:

                @pl.loop(0, TILE // 256)
                def _(part_at):
                    for part in range(2):
                        inside = chunk_at(part_at * 2 + part)
                        lanes = chunk_at(part_at * 2 + part, at * TILE)
                        norm_backward(
                            back, pre[layer - 1], active, slope, scales.at[layer - 1], hidden[layer], inside, lanes, lanes
                        )

            moves.after(f"E{layer}", at, steps)

    def keep_in(columns):
        def keep(value):
            gin_out[:, columns] = value

        return keep

    feat_copy.wait()
    for at, (name, bufs, columns) in enumerate(
        [
            ("ra", (ina_g, ina_rc, ina_oh, ina_ih, ina_ocol, ina_icol, ina_oz, ina_iz, ina_own), slice(0, SPLIT)),
            ("rb", (inb_g, inb_rc, inb_oh, inb_ih, inb_ocol, inb_icol, inb_oz, inb_iz, inb_own), slice(SPLIT, features)),
        ]
    ):

        @pl.loop(0, 2)
        def _(half, bufs=bufs, columns=columns):
            rows = pl.ds(pl.multiple_of(half * 256, 256), 256)
            grad = dot_nt(hid_0[rows, :], feat[columns, :]).astype(bf16)
            bufs[0][0, pl.ds(half * 2, 2)] = grad.reshape(2, *bufs[0].shape[2:])

        moves.under_way[name] = scatter_steps(
            place, Wire(scatter_send.at[7 + at], scatter_recv.at[7 + at]), bufs, 0, keep_in(columns)
        )
        moves.play("inputs", at)
    for wire in gather_wires:
        wire.finish()


def scatter_buffers(rows, columns, slots):
    def buf(*shape):
        return pltpu.VMEM((slots, *shape, rows, columns), bf16)

    return [
        buf(4, 2, 2, 2), buf(4, 2, 2), buf(2, 2), buf(2, 2), buf(2, 4), buf(2, 4), buf(3), buf(3),
        pltpu.VMEM((slots, rows, columns), f32),
    ]


def train(feat, nbr, edge, degree, counts, labels, live, win, pair, proj, head):
    features, nodes = feat.shape
    width = pair.shape[2]
    classes = head.shape[1]
    vmem = pl.BlockSpec(memory_space=pltpu.VMEM)
    dma = pltpu.SemaphoreType.DMA
    return pl.pallas_call(
        train_kernel,
        out_shape=[
            jax.ShapeDtypeStruct(win.shape, f32),
            jax.ShapeDtypeStruct(pair.shape, f32),
            jax.ShapeDtypeStruct(proj.shape, f32),
            jax.ShapeDtypeStruct(head.shape, f32),
            jax.ShapeDtypeStruct((8, 128), f32),
        ],
        in_specs=[pl.BlockSpec(memory_space=pl.ANY)] + [vmem] * 10,
        out_specs=[vmem] * 5,
        scratch_shapes=[
            pltpu.VMEM((nodes, nodes), bf16),
            pltpu.VMEM((features, nodes), bf16),
        ]
        + [pltpu.VMEM((width, nodes), bf16)] * 3
        + [pltpu.VMEM((width, nodes), bf16)] * 3
        + [pltpu.VMEM((2 * width, nodes), bf16)] * 3
        + [pltpu.VMEM((width, nodes), f32)] * 2
        + [
            pltpu.VMEM((4, 2, 2, 2, 16, features), bf16),
            pltpu.VMEM((LAYERS, 2, 4, 2, 2, 2, 32, width), bf16),
            pltpu.VMEM((4, 2, 2, 2, 16, 128), bf16),
            pltpu.VMEM((width, 2 * width), bf16),
            pltpu.VMEM((width, 128), f32),
            pltpu.VMEM((1, nodes), f32),
            pltpu.VMEM((1, nodes), f32),
            pltpu.VMEM((8, nodes), f32),
            pltpu.VMEM((8, 128), f32),
            pltpu.VMEM((8, 128), f32),
            pltpu.VMEM((LAYERS, 1, nodes), f32),
            pltpu.VMEM((width, TILE), f32),
            pltpu.VMEM((width, TILE), f32),
            pltpu.VMEM((width, TILE), bf16),
            pltpu.VMEM((width, 128), f32),
            pltpu.VMEM((width, 128), f32),
        ]
        + scatter_buffers(32, width, 2)
        + scatter_buffers(16, SPLIT, 1)
        + scatter_buffers(16, features - SPLIT, 1)
        + scatter_buffers(16, 128, 1)
        + [
            pltpu.VMEM((2, 3, 8, 128), f32),
            pltpu.VMEM((2, 3, 8, 128), f32),
            pltpu.VMEM((2, 4, 8, 128), f32),
            dma((9, 11)), dma((9, 11)), dma((9, 8)), dma((9, 8)), dma((2, 6)), dma((2, 6)), dma,
            pltpu.SemaphoreType.REGULAR((2, 6)),
        ],
        compiler_params=pltpu.CompilerParams(
            collective_id=0, has_side_effects=True, vmem_limit_bytes=64 * 2**20
        ),
        cost_estimate=pl.CostEstimate(
            flops=67 * 10**9, bytes_accessed=10**7, transcendentals=10**7
        ),
    )(feat, nbr, edge, degree, counts, labels, live, win, pair, proj, head)


def update_kernel(scalars, *refs):
    inputs, outs = refs[:16], refs[16:]
    outs[16][0, 0] = scalars[0, 0]
    outs[17][0, 0] = scalars[1, 0]
    for at in range(4):
        weight, first, second, grad = (inputs[at + 4 * kind][...] for kind in range(4))
        new, first_new, second_new = adamw_update(weight, first, second, grad)
        outs[at][...] = new
        outs[4 + at][...] = first_new
        outs[8 + at][...] = second_new
        outs[12 + at][...] = new.astype(bf16)


def update(scalars, weights, firsts, seconds, grads):
    shapes = [jax.ShapeDtypeStruct(w.shape, f32) for w in weights]
    vmem = pl.BlockSpec(memory_space=pltpu.VMEM)
    smem = pl.BlockSpec(memory_space=pltpu.SMEM)
    return pl.pallas_call(
        update_kernel,
        out_shape=shapes * 3
        + [jax.ShapeDtypeStruct(w.shape, bf16) for w in weights]
        + [jax.ShapeDtypeStruct((1, 1), f32)] * 2,
        in_specs=[smem] + [vmem] * 16,
        out_specs=[vmem] * 16 + [smem] * 2,
    )(scalars, *weights, *firsts, *seconds, *grads)


def turned_first(array):
    return jnp.swapaxes(array, -1, -2)


def body(
    features, labels, neighbors, degree, node_counts, edge_counts, live_nodes,
    input_weight, pair_weight, proj_weight, head_weight,
    input_first, pair_first, proj_first, head_first,
    input_second, pair_second, proj_second, head_second,
):
    def owned(input_w, pair_w, proj_w, head_w):
        return (turned_first(input_w), turned_first(pair_w), proj_w, head_w)

    weights = owned(input_weight, pair_weight, proj_weight, head_weight)
    *grads, scalars = train(
        turned_first(features), turned_first(neighbors), turned_first(edge_counts),
        degree[None, :], node_counts[None, :], labels[None, :], live_nodes[None, :], *weights,
    )
    *results, mean_loss, weight_mean = update(
        scalars,
        weights,
        owned(input_first, pair_first, proj_first, head_first),
        owned(input_second, pair_second, proj_second, head_second),
        grads,
    )
    placed = []
    for kind in range(4):
        placed += owned(*results[4 * kind : 4 * kind + 4])
    return (mean_loss.reshape(()), weight_mean.reshape(()), *placed)


def normalize(preact):
    active = jax.nn.gelu(preact)
    return active * lax.rsqrt(jnp.mean(active * active, axis=-1, keepdims=True) + norm_eps)


def slot_terms(neighbors, degree, live_count):
    count_nodes, fanout = neighbors.shape
    node_live = jnp.arange(count_nodes, dtype=jnp.int32) < live_count
    used = (
        (jnp.arange(fanout, dtype=jnp.int32)[None, :] < degree[:, None])
        & (neighbors < live_count)
        & node_live[:, None]
    )
    return (node_live, used)


def coefficients(used, node_counts, edge_counts, total_node, total_edge):
    node_float = node_counts.astype(jnp.float32)
    edge_float = edge_counts.astype(jnp.float32)
    spread = jnp.maximum(jnp.sum(used.astype(jnp.float32), axis=1), 1.0)
    value = node_float[:, None] * total_edge / (edge_float * total_node * spread[:, None])
    return jnp.where(used, value, 0.0)


def contract_rows(left, right):
    return lax.dot_general(
        left, right, (((0,), (0,)), ((), ())), preferred_element_type=jnp.float32
    )


def contract_cols(left, right):
    return lax.dot_general(
        left, right, (((1,), (1,)), ((), ())), preferred_element_type=jnp.float32
    )


def coef_matrix(neighbors, coefs):
    count_nodes = neighbors.shape[0]
    columns = lax.iota(jnp.int32, count_nodes)[None, :]
    matrix = jnp.zeros((count_nodes, count_nodes), jnp.float32)
    for neighbor_slot in range(neighbors.shape[1]):
        matrix = matrix + jnp.where(
            neighbors[:, neighbor_slot : neighbor_slot + 1] == columns,
            coefs[:, neighbor_slot : neighbor_slot + 1],
            0.0,
        )
    return matrix


def layer_forward(hidden, pair_w, proj_w, matrix):
    width = pair_w.shape[0]
    pooled = jnp.dot(
        matrix,
        hidden.astype(jnp.float32),
        precision=lax.Precision.HIGHEST,
        preferred_element_type=jnp.float32,
    ).astype(jnp.bfloat16)
    self_part = jnp.dot(hidden, pair_w[:, :width], preferred_element_type=jnp.float32)
    nbr_part = jnp.dot(pooled, pair_w[:, width:], preferred_element_type=jnp.float32)
    joined = jnp.concatenate([self_part, nbr_part], axis=1).astype(jnp.bfloat16)
    preact = jnp.dot(joined, proj_w, preferred_element_type=jnp.float32)
    return (normalize(preact).astype(jnp.bfloat16), (hidden, pooled, joined, preact))


def layer_backward(grad_out, saved, pair_w, proj_w, matrix):
    hidden, pooled, joined, preact = saved
    width = pair_w.shape[0]
    _, pullback = jax.vjp(normalize, preact)
    grad_preact = pullback(grad_out)[0].astype(jnp.bfloat16)
    grad_proj = contract_rows(joined, grad_preact)
    grad_joined = contract_cols(grad_preact, proj_w).astype(jnp.bfloat16)
    grad_pair = jnp.concatenate(
        [
            contract_rows(hidden, grad_joined[:, :width]),
            contract_rows(pooled, grad_joined[:, width:]),
        ],
        axis=1,
    )
    grad_hidden = contract_cols(grad_joined[:, :width], pair_w[:, :width])
    grad_pooled = contract_cols(grad_joined[:, width:], pair_w[:, width:])
    grad_hidden = grad_hidden + lax.dot_general(
        matrix,
        grad_pooled,
        (((0,), (0,)), ((), ())),
        precision=lax.Precision.HIGHEST,
        preferred_element_type=jnp.float32,
    )
    return (grad_hidden, grad_pair, grad_proj)


def plain_body(
    features,
    labels,
    neighbors,
    degree,
    node_counts,
    edge_counts,
    live_nodes,
    input_weight,
    pair_weight,
    proj_weight,
    head_weight,
    input_first,
    pair_first,
    proj_first,
    head_first,
    input_second,
    pair_second,
    proj_second,
    head_second,
):
    count_nodes = features.shape[0]
    all_nodes = jnp.float32(count_nodes * lax.axis_size(("dp", "group")))
    node_live, used = slot_terms(neighbors, degree, live_nodes[0])
    node_float = node_counts.astype(jnp.float32)
    node_local = jnp.sum(jnp.where(node_live, node_float, 0.0))
    edge_local = jnp.sum(jnp.where(used, edge_counts.astype(jnp.float32), 0.0))
    total_node, total_edge = lax.psum((node_local, edge_local), ("dp", "group"))
    weights = jnp.where(node_live, total_node / (node_float * all_nodes), 0.0)
    coefs = coefficients(used, node_counts, edge_counts, total_node, total_edge)
    matrix = coef_matrix(neighbors, coefs)
    input_b, pair_b, proj_b, head_b = (
        lax.all_gather(input_weight.astype(jnp.bfloat16), ("dp", "group"), axis=1, tiled=True),
        lax.all_gather(pair_weight.astype(jnp.bfloat16), ("dp", "group"), axis=2, tiled=True),
        lax.all_gather(proj_weight.astype(jnp.bfloat16), ("dp", "group"), axis=1, tiled=True),
        lax.all_gather(head_weight.astype(jnp.bfloat16), ("dp", "group"), axis=0, tiled=True),
    )
    hidden = jnp.dot(features, input_b, preferred_element_type=jnp.float32).astype(jnp.bfloat16)
    kept = []
    for layer_index in range(LAYERS):
        hidden, saved = layer_forward(hidden, pair_b[layer_index], proj_b[layer_index], matrix)
        kept.append(saved)
    logits = jnp.dot(hidden, head_b, preferred_element_type=jnp.float32)
    log_total = jax.nn.logsumexp(logits, axis=1)
    targets = (labels[:, None] == lax.iota(jnp.int32, logits.shape[1])[None, :]).astype(jnp.float32)
    loss_local = jnp.sum(weights * (log_total - jnp.sum(logits * targets, axis=1)))
    loss_sum, weight_sum = lax.psum((loss_local, jnp.sum(weights)), ("dp", "group"))
    grad_logits = (
        (weights / weight_sum)[:, None] * (jnp.exp(logits - log_total[:, None]) - targets)
    ).astype(jnp.bfloat16)
    grad_head = contract_rows(hidden, grad_logits)
    grad_hidden = contract_cols(grad_logits, head_b)
    pair_grads = [None] * LAYERS
    proj_grads = [None] * LAYERS
    for layer_index in reversed(range(LAYERS)):
        grad_hidden, grad_pair, grad_proj = layer_backward(
            grad_hidden, kept[layer_index], pair_b[layer_index], proj_b[layer_index], matrix
        )
        pair_grads[layer_index] = grad_pair
        proj_grads[layer_index] = grad_proj
    grad_input = contract_rows(features, grad_hidden.astype(jnp.bfloat16))
    grad_input, grad_pairs, grad_projs, grad_head = (
        lax.psum_scatter(grad_input, ("dp", "group"), scatter_dimension=1, tiled=True),
        lax.psum_scatter(jnp.stack(pair_grads), ("dp", "group"), scatter_dimension=2, tiled=True),
        lax.psum_scatter(jnp.stack(proj_grads), ("dp", "group"), scatter_dimension=1, tiled=True),
        lax.psum_scatter(grad_head, ("dp", "group"), scatter_dimension=0, tiled=True),
    )
    input_new, input_first_new, input_second_new = adamw_update(
        input_weight, input_first, input_second, grad_input
    )
    pair_new, pair_first_new, pair_second_new = adamw_update(
        pair_weight, pair_first, pair_second, grad_pairs
    )
    proj_new, proj_first_new, proj_second_new = adamw_update(
        proj_weight, proj_first, proj_second, grad_projs
    )
    head_new, head_first_new, head_second_new = adamw_update(
        head_weight, head_first, head_second, grad_head
    )
    return (
        loss_sum / weight_sum,
        weight_sum / all_nodes,
        input_new,
        pair_new,
        proj_new,
        head_new,
        input_first_new,
        pair_first_new,
        proj_first_new,
        head_first_new,
        input_second_new,
        pair_second_new,
        proj_second_new,
        head_second_new,
        input_new.astype(jnp.bfloat16),
        pair_new.astype(jnp.bfloat16),
        proj_new.astype(jnp.bfloat16),
        head_new.astype(jnp.bfloat16),
    )


def solution(mesh):
    placed = (
        P(("dp", "group"), None),
        P(("dp", "group")),
        P(("dp", "group"), None),
        P(("dp", "group")),
        P(("dp", "group")),
        P(("dp", "group"), None),
        P(("dp", "group")),
        P(None, ("dp", "group")),
        P(None, None, ("dp", "group")),
        P(None, ("dp", "group"), None),
        P(("dp", "group"), None),
        P(None, ("dp", "group")),
        P(None, None, ("dp", "group")),
        P(None, ("dp", "group"), None),
        P(("dp", "group"), None),
        P(None, ("dp", "group")),
        P(None, None, ("dp", "group")),
        P(None, ("dp", "group"), None),
        P(("dp", "group"), None),
    )
    fits = dict(mesh.shape) == {"dp": 8, "group": 4}
    return jax.shard_map(
        body if fits else plain_body,
        mesh=mesh,
        in_specs=placed,
        out_specs=(
            P(),
            P(),
            P(None, ("dp", "group")),
            P(None, None, ("dp", "group")),
            P(None, ("dp", "group"), None),
            P(("dp", "group"), None),
            P(None, ("dp", "group")),
            P(None, None, ("dp", "group")),
            P(None, ("dp", "group"), None),
            P(("dp", "group"), None),
            P(None, ("dp", "group")),
            P(None, None, ("dp", "group")),
            P(None, ("dp", "group"), None),
            P(("dp", "group"), None),
            P(None, ("dp", "group")),
            P(None, None, ("dp", "group")),
            P(None, ("dp", "group"), None),
            P(("dp", "group"), None),
        ),
        check_vma=False,
    )
```

```python
import jax
import jax.numpy as jnp
from jax import lax
from jax.experimental import pallas as pl
from jax.experimental.pallas import tpu as pltpu
from jax.sharding import PartitionSpec as P

LAYERS = 3
STEP = 5
COMMON = 840.0

learn_rate = 0.03
beta_first = 0.5
beta_second = 0.5
adam_eps = 1e-08
decay_rate = 0.01
norm_eps = 1e-06

AXES = ("dp", "group")
MESH = pl.DeviceIdType.MESH
f32 = jnp.float32
bf16 = jnp.bfloat16
TILE = 512
WIDE = 1024
SPLIT = 384
ROWS = 64
GATE_IN = 0.7978845608028654
GATE_CUBE = GATE_IN * 0.044715


def dot_nn(left, right):
    return jnp.dot(left, right, preferred_element_type=f32)


def dot_nt(left, right):
    return lax.dot_general(left, right, (((1,), (1,)), ((), ())), preferred_element_type=f32)


def adamw_update(weight, first, second, grad):
    first_new = beta_first * first + (1.0 - beta_first) * grad
    second_new = beta_second * second + (1.0 - beta_second) * grad * grad
    first_hat = first_new / (1.0 - beta_first**STEP)
    second_hat = second_new / (1.0 - beta_second**STEP)
    weight_new = weight - learn_rate * (
        first_hat / (jnp.sqrt(second_hat) + adam_eps) + decay_rate * weight
    )
    return (weight_new, first_new, second_new)


class Place:
    def __init__(self):
        dp, group = lax.axis_index("dp"), lax.axis_index("group")
        self.z, self.y = dp // 2, dp % 2
        self.x, self.c = group // 2, group % 2
        self.far_y, self.far_x, self.far_c = 1 - self.y, 1 - self.x, 1 - self.c
        self.sibling = (dp, group + 1 - 2 * self.c)
        self.beside_x = (dp, group + 2 - 4 * self.x)
        self.beside_y = (dp + 1 - 2 * self.y, group)
        self.later_z = [(self.z + step) % 4 for step in (1, 2, 3)]
        self.earlier_z = [(self.z + 4 - step) % 4 for step in (1, 2, 3)]
        self.to_z = [(at * 2 + self.y, group) for at in self.later_z]
        self.from_z = [(at * 2 + self.y, group) for at in self.earlier_z]

    def partners(self):
        return [self.sibling, self.beside_x, self.beside_y] + self.to_z


class Wire:
    def __init__(self, send_sems, recv_sems):
        self.send_sems, self.recv_sems = send_sems, recv_sems
        self.sent = []

    def copy(self, at, source, target, device):
        return pltpu.make_async_remote_copy(
            src_ref=source(),
            dst_ref=target(),
            send_sem=self.send_sems.at[at],
            recv_sem=self.recv_sems.at[at],
            device_id=device,
            device_id_type=MESH,
        )

    def send(self, at, source, target, device):
        self.copy(at, source, target, device).start()
        self.sent.append((at, source, target, device))

    def arrived(self, at, target, device):
        self.copy(at, target, target, device).wait_recv()

    def finish(self, below=100):
        for sent in self.sent:
            if sent[0] < below:
                self.copy(*sent).wait_send()
        self.sent = [sent for sent in self.sent if sent[0] >= below]


def gather_steps(place, wire, region):
    z, y, x, c = place.z, place.y, place.x, place.c
    fy, fx, fc = place.far_y, place.far_x, place.far_c
    whole, low, high = slice(0, 4), slice(0, 2), slice(2, 4)

    def at(*index):
        return lambda: region(*index)

    def send(sem, index, device):
        wire.send(sem, at(*index), at(*index), device)

    for step in range(3):
        send(step, (z, y, x, c), place.to_z[step])
    yield
    for step in range(3):
        wire.arrived(step, at(place.earlier_z[step], y, x, c), place.from_z[step])
    send(3, (whole, y, x, c), place.beside_x)
    send(4, (whole, y, x, c), place.beside_y)
    send(5, (whole, y, x, c), place.sibling)
    yield
    wire.arrived(3, at(whole, y, fx, c), place.beside_x)
    send(6, (low, y, fx, c), place.beside_y)
    send(8, (whole, y, fx, c), place.sibling)
    wire.arrived(4, at(whole, fy, x, c), place.beside_y)
    send(7, (high, fy, x, c), place.beside_x)
    send(9, (whole, fy, x, c), place.sibling)
    yield
    wire.arrived(6, at(low, fy, fx, c), place.beside_y)
    wire.arrived(7, at(high, fy, fx, c), place.beside_x)
    send(10, (whole, fy, fx, c), place.sibling)
    yield
    wire.arrived(5, at(whole, y, x, fc), place.sibling)
    wire.arrived(8, at(whole, y, fx, fc), place.sibling)
    wire.arrived(9, at(whole, fy, x, fc), place.sibling)
    wire.arrived(10, at(whole, fy, fx, fc), place.sibling)
    yield


def scatter_steps(place, wire, bufs, slot, store, free=None, reuses=False, reused=False):
    grads, from_core, out_half, in_half, out_col, in_col, out_z, in_z, own = bufs
    z, y, x, c = place.z, place.y, place.x, place.c
    fy, fx, fc = place.far_y, place.far_x, place.far_c
    low, high = slice(0, 2), slice(2, 4)

    def at(buf, *index):
        return lambda: buf.at[(slot, *index)]

    def both(zs, yy, xx):
        return grads[slot, zs, yy, xx, c].astype(f32) + from_core[slot, zs, yy, xx].astype(f32)

    def until_free(*partners):
        if reuses:
            for partner in partners:
                pl.semaphore_wait(free.at[slot, partner], 1)

    def set_free(*partners):
        for partner, device in partners:
            pl.semaphore_signal(free.at[slot, partner], inc=1, device_id=device, device_id_type=MESH)

    until_free(0)
    wire.send(0, at(grads, slice(0, 4), slice(0, 2), slice(0, 2), fc), at(from_core), place.sibling)
    yield
    wire.arrived(0, at(from_core), place.sibling)
    until_free(1, 2)
    out_half[slot, 0] = both(low, fy, fx).astype(bf16)
    wire.send(1, at(out_half, 0), at(in_half, 0), place.beside_x)
    out_half[slot, 1] = both(high, fy, fx).astype(bf16)
    wire.send(2, at(out_half, 1), at(in_half, 1), place.beside_y)
    yield
    wire.arrived(1, at(in_half, 0), place.beside_x)
    out_col[slot, 1, low] = (both(low, fy, x) + in_half[slot, 0].astype(f32)).astype(bf16)
    out_col[slot, 1, high] = both(high, fy, x).astype(bf16)
    wire.send(4, at(out_col, 1), at(in_col, 1), place.beside_y)
    wire.arrived(2, at(in_half, 1), place.beside_y)
    out_col[slot, 0, low] = both(low, y, fx).astype(bf16)
    out_col[slot, 0, high] = (both(high, y, fx) + in_half[slot, 1].astype(f32)).astype(bf16)
    wire.send(3, at(out_col, 0), at(in_col, 0), place.beside_x)
    yield
    wire.arrived(3, at(in_col, 0), place.beside_x)
    wire.arrived(4, at(in_col, 1), place.beside_y)

    def column(zz):
        beside = in_col[slot, 0, zz].astype(f32) + in_col[slot, 1, zz].astype(f32)
        return both(zz, y, x) + beside

    until_free(3, 4, 5)
    own[slot] = column(z)
    for step in range(3):
        out_z[slot, step] = column(place.later_z[step]).astype(bf16)
        wire.send(5 + step, at(out_z, step), at(in_z, step), place.to_z[step])
    wire.finish(5)
    if reused:
        set_free((0, place.sibling))
    yield
    for step in range(3):
        wire.arrived(5 + step, at(in_z, step), place.from_z[step])
    others = in_z[slot, 0].astype(f32) + in_z[slot, 1].astype(f32) + in_z[slot, 2].astype(f32)
    store(own[slot] + others)
    wire.finish()
    if reused:
        set_free(*enumerate([place.beside_x, place.beside_y] + place.from_z, 1))
    yield


def sum_steps(place, wire, bufs, slot, store):
    out, arrive, line = bufs

    def at(buf, *index):
        return lambda: buf.at[(slot, *index)]

    for stage, device in enumerate((place.sibling, place.beside_x, place.beside_y)):
        wire.send(stage, at(out, stage), at(arrive, stage), device)
        yield
        wire.arrived(stage, at(arrive, stage), device)
        if stage < 2:
            out[slot, stage + 1] = out[slot, stage] + arrive[slot, stage]
        else:
            line[slot, place.z] = out[slot, stage] + arrive[slot, stage]
    for step in range(3):
        wire.send(3 + step, at(line, place.z), at(line, place.z), place.to_z[step])
    yield
    for step in range(3):
        wire.arrived(3 + step, at(line, place.earlier_z[step]), place.from_z[step])
    store((line[slot, 0] + line[slot, 1]) + (line[slot, 2] + line[slot, 3]))
    wire.finish()
    yield


PLAN = {
    ("start", 0): ("ia", "ib",),
    ("slots", 0): ("tot",),
    ("build", 0): ("tot",),
    ("build", 1): ("ia", "p0",),
    ("build", 2): ("ib", "q0",),
    ("build", 3): ("tot",),
    ("build", 5): ("ia",),
    ("build", 6): ("ib", "tot",),
    ("build", 7): ("p0", "p1", "ia", "ib", "ia", "tot", "ib",),
    ("first", 0): ("q0", "q1",),
    ("first", 1): ("p0",),
    ("pool0", 0): ("p1", "p2",),
    ("pool0", 1): ("p0", "q0", "q1", "q2", "p0",),
    ("join0", 0): ("p1", "p2", "wh",),
    ("join0", 1): ("q0", "q0",),
    ("pre0", 0): ("q1", "q2", "wh",),
    ("pre0", 1): ("p1",),
    ("norm0", 6): ("p2",),
    ("pool1", 0): ("q1",),
    ("pool1", 1): ("q2", "wh", "p1",),
    ("join1", 0): ("p2",),
    ("join1", 1): ("q1",),
    ("pre1", 0): ("q2", "wh",),
    ("pool2", 1): ("p2",),
    ("join2", 1): ("q2", "wh",),
    ("loss", 0): ("rh", "los",),
    ("A2", 0): ("rh", "los",),
    ("A2", 1): ("P2",),
    ("B2", 0): ("rh", "los",),
    ("B2", 1): ("P2",),
    ("C2", 0): ("rh", "los",),
    ("C2", 1): ("Q2",),
    ("D2", 0): ("P2", "rh", "los",),
    ("D2", 1): ("Q2",),
    ("E2", 1): ("P2", "Q2",),
    ("E2", 3): ("P2", "Q2",),
    ("A1", 1): ("P1",),
    ("B1", 1): ("Q2", "P1",),
    ("C1", 1): ("Q1",),
    ("D1", 0): ("P1",),
    ("E1", 0): ("Q1",),
    ("E1", 1): ("P1",),
    ("E1", 2): ("Q1",),
    ("E1", 3): ("P1",),
    ("A0", 1): ("Q1", "P0",),
    ("B0", 1): ("P0",),
    ("C0", 1): ("Q1", "Q0",),
    ("D0", 0): ("P0",),
    ("E0", 0): ("Q0",),
    ("E0", 2): ("P0",),
    ("E0", 3): ("Q0",),
    ("inputs", 0): ("ra",),
    ("inputs", 1): ("rb", "ra", "P0", "rb", "Q0", "ra", "rb", "ra", "rb", "Q0", "ra", "rb",),
}


class Moves:
    def __init__(self):
        self.under_way = {}

    def play(self, label, at=0):
        for name in PLAN.get((label, at), ()):
            next(self.under_way[name])

    def after(self, label, at, count):
        for when in range(count):
            if (label, when) in PLAN:

                @pl.when(at == when)
                def _(when=when):
                    self.play(label, when)


def row_of_scalars(values):
    rows = lax.broadcasted_iota(jnp.int32, (8, 128), 0)
    block = jnp.zeros((8, 128), f32)
    for at, value in enumerate(values):
        block = jnp.where(rows == at, value, block)
    return block


def gelu(pre):
    square = pre * pre
    gate = 0.5 * jnp.tanh(pre * (GATE_CUBE * square + GATE_IN)) + 0.5
    return pre * gate, gate, square


def row_chunks():
    return [slice(at, at + ROWS) for at in range(0, 512, ROWS)]


def norm_forward(pre, active, scales, out, lanes, scale_lanes):
    square = jnp.zeros((ROWS, 128), f32)
    for row in row_chunks():
        value, _, _ = gelu(pre[row, lanes])
        active[row, :] = value
        square = square + value * value
    scale = lax.rsqrt(jnp.sum(square, axis=0, keepdims=True) * (1.0 / 512) + norm_eps)
    scales[:, scale_lanes] = scale
    for row in row_chunks():
        out[row, lanes] = (active[row, :] * scale).astype(bf16)


def norm_backward(grad, pre, active, slope, scales, out, grad_lanes, pre_lanes, lanes):
    scale = scales[:, lanes]
    along = jnp.zeros((ROWS, 128), f32)
    for row in row_chunks():
        value, gate, square = gelu(pre[row, pre_lanes])
        active[row, :] = value
        slope[row, :] = gate + value * (
            (1.0 - gate) * ((6.0 * GATE_CUBE) * square + 2.0 * GATE_IN)
        )
        along = along + value * grad[row, grad_lanes]
    pull = scale * scale * scale * (jnp.sum(along, axis=0, keepdims=True) * (1.0 / 512))
    for row in row_chunks():
        out[row, lanes] = (
            slope[row, :] * (scale * grad[row, grad_lanes] - active[row, :] * pull)
        ).astype(bf16)


def train_kernel(
    feat_hbm, nbr, edge, degree, counts, labels, live, win_own, pair_own, proj_own, head_own,
    gin_out, gpair_out, gproj_out, ghead_out, scal_out,
    matrix, feat, hid_0, hid_1, hid_2, pool_0, pool_1, pool_2, join_0, join_1, join_2, pre_0, pre_1,
    win, weights, head, turned, head_grad, scale, inverse, terms, totals, losses, scales,
    back, top_pre, last, active, slope,
    big_g, big_rc, big_oh, big_ih, big_ocol, big_icol, big_oz, big_iz, big_own,
    ina_g, ina_rc, ina_oh, ina_ih, ina_ocol, ina_icol, ina_oz, ina_iz, ina_own,
    inb_g, inb_rc, inb_oh, inb_ih, inb_ocol, inb_icol, inb_oz, inb_iz, inb_own,
    hd_g, hd_rc, hd_oh, hd_ih, hd_ocol, hd_icol, hd_oz, hd_iz, hd_own,
    sum_out, sum_in, sum_line,
    gather_send, gather_recv, scatter_send, scatter_recv, sum_send, sum_recv, feat_sem, free,
):
    place = Place()
    z, y, x, c = place.z, place.y, place.x, place.c
    nodes, width, classes = nbr.shape[1], hid_0.shape[0], head_own.shape[1]
    steps, wide_steps, chunks = nodes // TILE, nodes // WIDE, nodes // 128
    hidden, pooled, joined, pre = (
        [hid_0, hid_1, hid_2], [pool_0, pool_1, pool_2], [join_0, join_1, join_2], [pre_0, pre_1],
    )
    top, features = LAYERS - 1, feat.shape[0]

    barrier = pltpu.get_barrier_semaphore()
    for partner in place.partners():
        pl.semaphore_signal(barrier, inc=1, device_id=partner, device_id_type=MESH)

    feat_copy = pltpu.make_async_copy(feat_hbm, feat, feat_sem)
    feat_copy.start()
    win[z, y, x, c] = win_own[...].astype(bf16)
    for layer in range(LAYERS):
        weights[layer, 0, z, y, x, c] = pair_own[layer].astype(bf16)
        weights[layer, 1, z, y, x, c] = proj_own[layer].astype(bf16)
    head[z, y, x, c] = jnp.zeros(head.shape[4:], bf16)
    head[z, y, x, c, :, 0:classes] = head_own[...].astype(bf16)

    pl.semaphore_wait(barrier, 6)

    def region_of(layer, kind):
        return lambda zz, yy, xx, cc: weights.at[layer, kind, zz, yy, xx, cc]

    def region_of_input(columns):
        return lambda zz, yy, xx, cc: win.at[zz, yy, xx, cc, :, columns]

    regions = {
        "ia": region_of_input(slice(0, SPLIT)),
        "ib": region_of_input(slice(SPLIT, features)),
        "wh": lambda zz, yy, xx, cc: head.at[zz, yy, xx, cc],
    }
    for layer in range(LAYERS):
        regions[f"p{layer}"] = region_of(layer, 0)
        regions[f"q{layer}"] = region_of(layer, 1)
    moves = Moves()
    gather_wires = []
    for at, (name, region) in enumerate(regions.items()):
        gather_wires.append(Wire(gather_send.at[at], gather_recv.at[at]))
        moves.under_way[name] = gather_steps(place, gather_wires[-1], region)
    moves.play("start")

    node_live = lax.broadcasted_iota(jnp.int32, (1, nodes), 1) < live[0]
    slot = lax.broadcasted_iota(jnp.int32, nbr.shape, 0)
    used = (slot < degree[...]) & (nbr[...] < live[0]) & node_live
    edge_float = edge[...].astype(f32)
    count_float = counts[...].astype(f32)
    spread = jnp.maximum(jnp.sum(used.astype(f32), axis=0, keepdims=True), 1.0)
    inverse[...] = jnp.where(node_live, 1.0 / count_float, 0.0)
    scale[...] = count_float / (spread * COMMON)
    sum_out[0, 0] = row_of_scalars(
        [
            jnp.sum(jnp.where(node_live, count_float, 0.0)),
            jnp.sum(jnp.where(used, edge_float, 0.0)),
            jnp.sum(inverse[...]),
        ]
    )

    def keep_totals(block):
        totals[...] = block

    moves.under_way["tot"] = sum_steps(
        place, Wire(sum_send.at[0], sum_recv.at[0]), (sum_out, sum_in, sum_line), 0, keep_totals
    )
    moves.play("slots")

    term = jnp.where(used, COMMON / edge_float, 0.0)
    summed = jnp.zeros(nbr.shape, f32)
    for k in range(nbr.shape[0]):
        summed = summed + jnp.where(nbr[k : k + 1, :] == nbr[...], term[k : k + 1, :], 0.0)
    terms[...] = summed

    @pl.loop(0, nodes // 256)
    def _(block_at):
        lanes = pl.ds(pl.multiple_of(block_at * 256, 256), 256)
        ids = [jnp.broadcast_to(nbr[k : k + 1, lanes], (16, 256)).astype(jnp.int16) for k in range(8)]
        values = [jnp.broadcast_to(terms[k : k + 1, lanes], (16, 256)).astype(bf16) for k in range(8)]

        @pl.loop(0, nodes // 64)
        def _(at):
            for part in range(4):
                row = pl.multiple_of(at * 64 + part * 16, 16)
                own = (lax.broadcasted_iota(jnp.int32, (16, 256), 0) + row).astype(jnp.int16)
                block = jnp.zeros((16, 256), bf16)
                for k in range(8):
                    block = jnp.where(ids[k] == own, values[k], block)
                matrix[pl.ds(row, 16), lanes] = block

        moves.after("build", block_at, nodes // 256)

    scale[...] = scale[...] * (totals[1:2, 0:1] / totals[0:1, 0:1])
    feat_copy.wait()

    def tile_at(at):
        return pl.multiple_of(at * TILE, TILE)

    def wide(at):
        return pl.ds(pl.multiple_of(at * WIDE, WIDE), WIDE)

    def chunk_at(at, start=0):
        return pl.ds(pl.multiple_of(start + at * 128, 128), 128)

    @pl.loop(0, wide_steps)
    def _(at):
        tile = wide(at)
        hid_0[:, tile] = dot_nn(win[...].reshape(width, -1), feat[:, tile]).astype(bf16)
        moves.after("first", at, wide_steps)

    def pair_of(layer):
        return weights[layer, 0].reshape(2 * width, width)

    def proj_of(layer):
        return weights[layer, 1].reshape(2 * width, width)

    def pool_tile(layer, tile):
        pooled[layer][:, tile] = (
            dot_nn(hidden[layer][...], matrix[:, tile]) * scale[:, tile]
        ).astype(bf16)

    def join_tile(layer, tile):
        pair = pair_of(layer)
        joined[layer][0:width, tile] = dot_nn(pair[:width], hidden[layer][:, tile]).astype(bf16)
        joined[layer][width:, tile] = dot_nn(pair[width:], pooled[layer][:, tile]).astype(bf16)

    def pool_and_join(layer):
        @pl.loop(0, wide_steps)
        def _(at):
            pool_tile(layer, wide(at))
            moves.after(f"pool{layer}", at, wide_steps)

        @pl.loop(0, wide_steps)
        def _(at):
            join_tile(layer, wide(at))
            moves.after(f"join{layer}", at, wide_steps)

        turned[...] = proj_of(layer).T

    for layer in range(LAYERS - 1):
        pool_and_join(layer)

        @pl.loop(0, wide_steps)
        def _(at, layer=layer):
            pre[layer][:, wide(at)] = dot_nn(turned[...], joined[layer][:, wide(at)])
            moves.after(f"pre{layer}", at, wide_steps)

        @pl.loop(0, chunks // 2)
        def _(at, layer=layer):
            for part in range(2):
                lanes = chunk_at(at * 2 + part)
                norm_forward(pre[layer], active, scales.at[layer], hidden[layer + 1], lanes, lanes)
            moves.after(f"norm{layer}", at, chunks // 2)

    pool_and_join(top)
    head_grad[...] = jnp.zeros_like(head_grad)
    losses[...] = jnp.zeros_like(losses)
    class_row = lax.broadcasted_iota(jnp.int32, (48, TILE), 0)

    def loss_tile(at):
        start = tile_at(at)
        tile = pl.ds(start, TILE)
        head_rows = head[...].reshape(width, 128)
        for part in range(TILE // 128):
            inside = slice(part * 128, part * 128 + 128)
            norm_forward(top_pre, active, scales.at[top], last, inside, chunk_at(part, start))
        logits = jnp.where(class_row < classes, dot_nn(head_rows.T[0:48], last[...]), -1e30)
        most = jnp.max(logits, axis=0, keepdims=True)
        log_total = jnp.log(jnp.sum(jnp.exp(logits - most), axis=0, keepdims=True)) + most
        target = class_row == labels[:, tile]
        picked = jnp.sum(jnp.where(target, logits, 0.0), axis=0, keepdims=True)
        loss = jnp.sum(inverse[:, tile] * (log_total - picked), axis=1, keepdims=True)
        losses[...] = losses[...] + loss
        weight = inverse[:, tile] / totals[2:3, 0:1]
        grad_logits = (weight * (jnp.exp(logits - log_total) - target.astype(f32))).astype(bf16)
        grad_logits = jnp.concatenate([grad_logits, jnp.zeros((80, TILE), bf16)], axis=0)
        head_grad[...] = head_grad[...] + dot_nt(last[...], grad_logits)
        back[...] = dot_nn(head_rows, grad_logits)
        for part in range(TILE // 128):
            inside = slice(part * 128, part * 128 + 128)
            norm_backward(
                back, top_pre, active, slope, scales.at[top], feat.at[0:width], inside, inside, chunk_at(part, start)
            )

    @pl.loop(0, steps)
    def _(at):
        top_pre[...] = dot_nn(turned[...], joined[top][:, pl.ds(tile_at(at), TILE)])
        loss_tile(at)

    hd_g[0] = head_grad[...].astype(bf16).reshape(hd_g.shape[1:])
    sum_out[1, 0] = jnp.broadcast_to(losses[0:1, 0:1], (8, 128))

    def keep_loss(block):
        rows = lax.broadcasted_iota(jnp.int32, (8, 128), 0)
        all_nodes = float(nodes * 32)
        weight_mean = (totals[0:1, :] * totals[2:3, :]) / (all_nodes * all_nodes)
        scal_out[...] = jnp.where(rows == 0, block / totals[2:3, :], weight_mean)

    moves.under_way["los"] = sum_steps(
        place, Wire(sum_send.at[1], sum_recv.at[1]), (sum_out, sum_in, sum_line), 1, keep_loss
    )

    def keep_head(value):
        ghead_out[...] = value[:, 0:classes]

    moves.under_way["rh"] = scatter_steps(
        place, Wire(scatter_send.at[0], scatter_recv.at[0]),
        (hd_g, hd_rc, hd_oh, hd_ih, hd_ocol, hd_icol, hd_oz, hd_iz, hd_own), 0, keep_head,
    )
    moves.play("loss")

    def big_steps(chunk, slot, target, layer):
        def keep(value):
            target[layer] = value

        return scatter_steps(
            place, Wire(scatter_send.at[chunk], scatter_recv.at[chunk]),
            (big_g, big_rc, big_oh, big_ih, big_ocol, big_icol, big_oz, big_iz, big_own), slot, keep,
            free=free, reuses=layer < top, reused=layer > 0,
        )

    def grad_block(slot, at, left, right):
        rows = pl.ds(pl.multiple_of(at * 512, 512), 512)
        grad = dot_nt(left[rows, :], right).astype(bf16)
        big_g[slot, pl.ds(at * 2, 2)] = grad.reshape(2, *big_g.shape[2:])

    for layer in reversed(range(LAYERS)):
        chunk = 1 + 2 * (top - layer)
        grad = feat.at[0:width] if layer == top else hidden[layer + 1]

        moves.under_way[f"P{layer}"] = big_steps(chunk, 0, gproj_out, layer)
        moves.under_way[f"Q{layer}"] = big_steps(chunk + 1, 1, gpair_out, layer)

        @pl.loop(0, 2)
        def _(at, layer=layer, grad=grad):
            grad_block(0, at, joined[layer], grad[...])
            moves.after(f"A{layer}", at, 2)

        @pl.loop(0, wide_steps)
        def _(at, layer=layer, grad=grad):
            joined[layer][:, wide(at)] = dot_nn(proj_of(layer), grad[:, wide(at)]).astype(bf16)
            moves.after(f"B{layer}", at, wide_steps)

        if layer == top:
            feat_copy = pltpu.make_async_copy(feat_hbm, feat, feat_sem)
            feat_copy.start()

        grad_block(1, 0, joined[layer], hidden[layer][...])
        moves.play(f"C{layer}", 0)
        grad_block(1, 1, joined[layer], pooled[layer][...])
        moves.play(f"C{layer}", 1)
        turned[...] = pair_of(layer).T

        @pl.loop(0, wide_steps)
        def _(at, layer=layer):
            tile = wide(at)
            pooled[layer][:, tile] = (
                dot_nn(turned[:, width:], joined[layer][width:, tile]) * scale[:, tile]
            ).astype(bf16)
            moves.after(f"D{layer}", at, wide_steps)

        @pl.loop(0, steps)
        def _(at, layer=layer):
            tile = pl.ds(tile_at(at), TILE)
            back[...] = dot_nn(turned[:, :width], joined[layer][:width, tile])
            back[...] += dot_nt(pooled[layer][...], matrix[tile, :])
            if layer == 0:
                hidden[layer][:, tile] = back[...].astype(bf16)
            else:

                @pl.loop(0, TILE // 256)
                def _(part_at):
                    for part in range(2):
                        inside = chunk_at(part_at * 2 + part)
                        lanes = chunk_at(part_at * 2 + part, at * TILE)
                        norm_backward(
                            back, pre[layer - 1], active, slope, scales.at[layer - 1], hidden[layer], inside, lanes, lanes
                        )

            moves.after(f"E{layer}", at, steps)

    def keep_in(columns):
        def keep(value):
            gin_out[:, columns] = value

        return keep

    feat_copy.wait()
    for at, (name, bufs, columns) in enumerate(
        [
            ("ra", (ina_g, ina_rc, ina_oh, ina_ih, ina_ocol, ina_icol, ina_oz, ina_iz, ina_own), slice(0, SPLIT)),
            ("rb", (inb_g, inb_rc, inb_oh, inb_ih, inb_ocol, inb_icol, inb_oz, inb_iz, inb_own), slice(SPLIT, features)),
        ]
    ):

        @pl.loop(0, 2)
        def _(half, bufs=bufs, columns=columns):
            rows = pl.ds(pl.multiple_of(half * 256, 256), 256)
            grad = dot_nt(hid_0[rows, :], feat[columns, :]).astype(bf16)
            bufs[0][0, pl.ds(half * 2, 2)] = grad.reshape(2, *bufs[0].shape[2:])

        moves.under_way[name] = scatter_steps(
            place, Wire(scatter_send.at[7 + at], scatter_recv.at[7 + at]), bufs, 0, keep_in(columns)
        )
        moves.play("inputs", at)
    for wire in gather_wires:
        wire.finish()


def scatter_buffers(rows, columns, slots):
    def buf(*shape):
        return pltpu.VMEM((slots, *shape, rows, columns), bf16)

    return [
        buf(4, 2, 2, 2), buf(4, 2, 2), buf(2, 2), buf(2, 2), buf(2, 4), buf(2, 4), buf(3), buf(3),
        pltpu.VMEM((slots, rows, columns), f32),
    ]


def train(feat, nbr, edge, degree, counts, labels, live, win, pair, proj, head):
    features, nodes = feat.shape
    width = pair.shape[2]
    classes = head.shape[1]
    vmem = pl.BlockSpec(memory_space=pltpu.VMEM)
    dma = pltpu.SemaphoreType.DMA
    return pl.pallas_call(
        train_kernel,
        out_shape=[
            jax.ShapeDtypeStruct(win.shape, f32),
            jax.ShapeDtypeStruct(pair.shape, f32),
            jax.ShapeDtypeStruct(proj.shape, f32),
            jax.ShapeDtypeStruct(head.shape, f32),
            jax.ShapeDtypeStruct((8, 128), f32),
        ],
        in_specs=[pl.BlockSpec(memory_space=pl.ANY)]
        + [vmem] * 5
        + [pl.BlockSpec(memory_space=pltpu.SMEM)]
        + [vmem] * 4,
        out_specs=[vmem] * 5,
        scratch_shapes=[
            pltpu.VMEM((nodes, nodes), bf16),
            pltpu.VMEM((features, nodes), bf16),
        ]
        + [pltpu.VMEM((width, nodes), bf16)] * 3
        + [pltpu.VMEM((width, nodes), bf16)] * 3
        + [pltpu.VMEM((2 * width, nodes), bf16)] * 3
        + [pltpu.VMEM((width, nodes), f32)] * 2
        + [
            pltpu.VMEM((4, 2, 2, 2, 16, features), bf16),
            pltpu.VMEM((LAYERS, 2, 4, 2, 2, 2, 32, width), bf16),
            pltpu.VMEM((4, 2, 2, 2, 16, 128), bf16),
            pltpu.VMEM((width, 2 * width), bf16),
            pltpu.VMEM((width, 128), f32),
            pltpu.VMEM((1, nodes), f32),
            pltpu.VMEM((1, nodes), f32),
            pltpu.VMEM((8, nodes), f32),
            pltpu.VMEM((8, 128), f32),
            pltpu.VMEM((8, 128), f32),
            pltpu.VMEM((LAYERS, 1, nodes), f32),
            pltpu.VMEM((width, TILE), f32),
            pltpu.VMEM((width, TILE), f32),
            pltpu.VMEM((width, TILE), bf16),
            pltpu.VMEM((width, 128), f32),
            pltpu.VMEM((width, 128), f32),
        ]
        + scatter_buffers(32, width, 2)
        + scatter_buffers(16, SPLIT, 1)
        + scatter_buffers(16, features - SPLIT, 1)
        + scatter_buffers(16, 128, 1)
        + [
            pltpu.VMEM((2, 3, 8, 128), f32),
            pltpu.VMEM((2, 3, 8, 128), f32),
            pltpu.VMEM((2, 4, 8, 128), f32),
            dma((9, 11)), dma((9, 11)), dma((9, 8)), dma((9, 8)), dma((2, 6)), dma((2, 6)), dma,
            pltpu.SemaphoreType.REGULAR((2, 6)),
        ],
        compiler_params=pltpu.CompilerParams(
            collective_id=0, has_side_effects=True, vmem_limit_bytes=64 * 2**20
        ),
        cost_estimate=pl.CostEstimate(
            flops=67 * 10**9, bytes_accessed=10**7, transcendentals=10**7
        ),
    )(feat, nbr, edge, degree, counts, labels, live, win, pair, proj, head)


def update_kernel(scalars, *refs):
    inputs, outs = refs[:16], refs[16:]
    outs[16][0, 0] = scalars[0, 0]
    outs[17][0, 0] = scalars[1, 0]
    for at in range(4):
        weight, first, second, grad = (inputs[at + 4 * kind][...] for kind in range(4))
        new, first_new, second_new = adamw_update(weight, first, second, grad)
        outs[at][...] = new
        outs[4 + at][...] = first_new
        outs[8 + at][...] = second_new
        outs[12 + at][...] = new.astype(bf16)


def update(scalars, weights, firsts, seconds, grads):
    shapes = [jax.ShapeDtypeStruct(w.shape, f32) for w in weights]
    smem = pl.BlockSpec(memory_space=pltpu.SMEM)
    blocks = [
        pl.BlockSpec((1, *w.shape[1:]), lambda layer: (layer, 0, 0))
        if w.ndim == 3
        else pl.BlockSpec(w.shape, lambda layer: (0, 0))
        for w in weights
    ]
    return pl.pallas_call(
        update_kernel,
        out_shape=shapes * 3
        + [jax.ShapeDtypeStruct(w.shape, bf16) for w in weights]
        + [jax.ShapeDtypeStruct((1, 1), f32)] * 2,
        grid=(LAYERS,),
        in_specs=[smem] + blocks * 4,
        out_specs=blocks * 4 + [smem] * 2,
    )(scalars, *weights, *firsts, *seconds, *grads)


def turned_first(array):
    return jnp.swapaxes(array, -1, -2)


def body(
    features, labels, neighbors, degree, node_counts, edge_counts, live_nodes,
    input_weight, pair_weight, proj_weight, head_weight,
    input_first, pair_first, proj_first, head_first,
    input_second, pair_second, proj_second, head_second,
):
    def owned(input_w, pair_w, proj_w, head_w):
        return (turned_first(input_w), turned_first(pair_w), proj_w, head_w)

    weights = owned(input_weight, pair_weight, proj_weight, head_weight)
    *grads, scalars = train(
        turned_first(features), turned_first(neighbors), turned_first(edge_counts),
        degree[None, :], node_counts[None, :], labels[None, :], live_nodes, *weights,
    )
    *results, mean_loss, weight_mean = update(
        scalars,
        weights,
        owned(input_first, pair_first, proj_first, head_first),
        owned(input_second, pair_second, proj_second, head_second),
        grads,
    )
    placed = []
    for kind in range(4):
        placed += owned(*results[4 * kind : 4 * kind + 4])
    return (mean_loss.reshape(()), weight_mean.reshape(()), *placed)


def normalize(preact):
    active = jax.nn.gelu(preact)
    return active * lax.rsqrt(jnp.mean(active * active, axis=-1, keepdims=True) + norm_eps)


def slot_terms(neighbors, degree, live_count):
    count_nodes, fanout = neighbors.shape
    node_live = jnp.arange(count_nodes, dtype=jnp.int32) < live_count
    used = (
        (jnp.arange(fanout, dtype=jnp.int32)[None, :] < degree[:, None])
        & (neighbors < live_count)
        & node_live[:, None]
    )
    return (node_live, used)


def coefficients(used, node_counts, edge_counts, total_node, total_edge):
    node_float = node_counts.astype(jnp.float32)
    edge_float = edge_counts.astype(jnp.float32)
    spread = jnp.maximum(jnp.sum(used.astype(jnp.float32), axis=1), 1.0)
    value = node_float[:, None] * total_edge / (edge_float * total_node * spread[:, None])
    return jnp.where(used, value, 0.0)


def contract_rows(left, right):
    return lax.dot_general(
        left, right, (((0,), (0,)), ((), ())), preferred_element_type=jnp.float32
    )


def contract_cols(left, right):
    return lax.dot_general(
        left, right, (((1,), (1,)), ((), ())), preferred_element_type=jnp.float32
    )


def coef_matrix(neighbors, coefs):
    count_nodes = neighbors.shape[0]
    columns = lax.iota(jnp.int32, count_nodes)[None, :]
    matrix = jnp.zeros((count_nodes, count_nodes), jnp.float32)
    for neighbor_slot in range(neighbors.shape[1]):
        matrix = matrix + jnp.where(
            neighbors[:, neighbor_slot : neighbor_slot + 1] == columns,
            coefs[:, neighbor_slot : neighbor_slot + 1],
            0.0,
        )
    return matrix


def layer_forward(hidden, pair_w, proj_w, matrix):
    width = pair_w.shape[0]
    pooled = jnp.dot(
        matrix,
        hidden.astype(jnp.float32),
        precision=lax.Precision.HIGHEST,
        preferred_element_type=jnp.float32,
    ).astype(jnp.bfloat16)
    self_part = jnp.dot(hidden, pair_w[:, :width], preferred_element_type=jnp.float32)
    nbr_part = jnp.dot(pooled, pair_w[:, width:], preferred_element_type=jnp.float32)
    joined = jnp.concatenate([self_part, nbr_part], axis=1).astype(jnp.bfloat16)
    preact = jnp.dot(joined, proj_w, preferred_element_type=jnp.float32)
    return (normalize(preact).astype(jnp.bfloat16), (hidden, pooled, joined, preact))


def layer_backward(grad_out, saved, pair_w, proj_w, matrix):
    hidden, pooled, joined, preact = saved
    width = pair_w.shape[0]
    _, pullback = jax.vjp(normalize, preact)
    grad_preact = pullback(grad_out)[0].astype(jnp.bfloat16)
    grad_proj = contract_rows(joined, grad_preact)
    grad_joined = contract_cols(grad_preact, proj_w).astype(jnp.bfloat16)
    grad_pair = jnp.concatenate(
        [
            contract_rows(hidden, grad_joined[:, :width]),
            contract_rows(pooled, grad_joined[:, width:]),
        ],
        axis=1,
    )
    grad_hidden = contract_cols(grad_joined[:, :width], pair_w[:, :width])
    grad_pooled = contract_cols(grad_joined[:, width:], pair_w[:, width:])
    grad_hidden = grad_hidden + lax.dot_general(
        matrix,
        grad_pooled,
        (((0,), (0,)), ((), ())),
        precision=lax.Precision.HIGHEST,
        preferred_element_type=jnp.float32,
    )
    return (grad_hidden, grad_pair, grad_proj)


def plain_body(
    features,
    labels,
    neighbors,
    degree,
    node_counts,
    edge_counts,
    live_nodes,
    input_weight,
    pair_weight,
    proj_weight,
    head_weight,
    input_first,
    pair_first,
    proj_first,
    head_first,
    input_second,
    pair_second,
    proj_second,
    head_second,
):
    count_nodes = features.shape[0]
    all_nodes = jnp.float32(count_nodes * lax.axis_size(("dp", "group")))
    node_live, used = slot_terms(neighbors, degree, live_nodes[0])
    node_float = node_counts.astype(jnp.float32)
    node_local = jnp.sum(jnp.where(node_live, node_float, 0.0))
    edge_local = jnp.sum(jnp.where(used, edge_counts.astype(jnp.float32), 0.0))
    total_node, total_edge = lax.psum((node_local, edge_local), ("dp", "group"))
    weights = jnp.where(node_live, total_node / (node_float * all_nodes), 0.0)
    coefs = coefficients(used, node_counts, edge_counts, total_node, total_edge)
    matrix = coef_matrix(neighbors, coefs)
    input_b, pair_b, proj_b, head_b = (
        lax.all_gather(input_weight.astype(jnp.bfloat16), ("dp", "group"), axis=1, tiled=True),
        lax.all_gather(pair_weight.astype(jnp.bfloat16), ("dp", "group"), axis=2, tiled=True),
        lax.all_gather(proj_weight.astype(jnp.bfloat16), ("dp", "group"), axis=1, tiled=True),
        lax.all_gather(head_weight.astype(jnp.bfloat16), ("dp", "group"), axis=0, tiled=True),
    )
    hidden = jnp.dot(features, input_b, preferred_element_type=jnp.float32).astype(jnp.bfloat16)
    kept = []
    for layer_index in range(LAYERS):
        hidden, saved = layer_forward(hidden, pair_b[layer_index], proj_b[layer_index], matrix)
        kept.append(saved)
    logits = jnp.dot(hidden, head_b, preferred_element_type=jnp.float32)
    log_total = jax.nn.logsumexp(logits, axis=1)
    targets = (labels[:, None] == lax.iota(jnp.int32, logits.shape[1])[None, :]).astype(jnp.float32)
    loss_local = jnp.sum(weights * (log_total - jnp.sum(logits * targets, axis=1)))
    loss_sum, weight_sum = lax.psum((loss_local, jnp.sum(weights)), ("dp", "group"))
    grad_logits = (
        (weights / weight_sum)[:, None] * (jnp.exp(logits - log_total[:, None]) - targets)
    ).astype(jnp.bfloat16)
    grad_head = contract_rows(hidden, grad_logits)
    grad_hidden = contract_cols(grad_logits, head_b)
    pair_grads = [None] * LAYERS
    proj_grads = [None] * LAYERS
    for layer_index in reversed(range(LAYERS)):
        grad_hidden, grad_pair, grad_proj = layer_backward(
            grad_hidden, kept[layer_index], pair_b[layer_index], proj_b[layer_index], matrix
        )
        pair_grads[layer_index] = grad_pair
        proj_grads[layer_index] = grad_proj
    grad_input = contract_rows(features, grad_hidden.astype(jnp.bfloat16))
    grad_input, grad_pairs, grad_projs, grad_head = (
        lax.psum_scatter(grad_input, ("dp", "group"), scatter_dimension=1, tiled=True),
        lax.psum_scatter(jnp.stack(pair_grads), ("dp", "group"), scatter_dimension=2, tiled=True),
        lax.psum_scatter(jnp.stack(proj_grads), ("dp", "group"), scatter_dimension=1, tiled=True),
        lax.psum_scatter(grad_head, ("dp", "group"), scatter_dimension=0, tiled=True),
    )
    input_new, input_first_new, input_second_new = adamw_update(
        input_weight, input_first, input_second, grad_input
    )
    pair_new, pair_first_new, pair_second_new = adamw_update(
        pair_weight, pair_first, pair_second, grad_pairs
    )
    proj_new, proj_first_new, proj_second_new = adamw_update(
        proj_weight, proj_first, proj_second, grad_projs
    )
    head_new, head_first_new, head_second_new = adamw_update(
        head_weight, head_first, head_second, grad_head
    )
    return (
        loss_sum / weight_sum,
        weight_sum / all_nodes,
        input_new,
        pair_new,
        proj_new,
        head_new,
        input_first_new,
        pair_first_new,
        proj_first_new,
        head_first_new,
        input_second_new,
        pair_second_new,
        proj_second_new,
        head_second_new,
        input_new.astype(jnp.bfloat16),
        pair_new.astype(jnp.bfloat16),
        proj_new.astype(jnp.bfloat16),
        head_new.astype(jnp.bfloat16),
    )


def solution(mesh):
    placed = (
        P(("dp", "group"), None),
        P(("dp", "group")),
        P(("dp", "group"), None),
        P(("dp", "group")),
        P(("dp", "group")),
        P(("dp", "group"), None),
        P(("dp", "group")),
        P(None, ("dp", "group")),
        P(None, None, ("dp", "group")),
        P(None, ("dp", "group"), None),
        P(("dp", "group"), None),
        P(None, ("dp", "group")),
        P(None, None, ("dp", "group")),
        P(None, ("dp", "group"), None),
        P(("dp", "group"), None),
        P(None, ("dp", "group")),
        P(None, None, ("dp", "group")),
        P(None, ("dp", "group"), None),
        P(("dp", "group"), None),
    )
    fits = dict(mesh.shape) == {"dp": 8, "group": 4}
    return jax.shard_map(
        body if fits else plain_body,
        mesh=mesh,
        in_specs=placed,
        out_specs=(
            P(),
            P(),
            P(None, ("dp", "group")),
            P(None, None, ("dp", "group")),
            P(None, ("dp", "group"), None),
            P(("dp", "group"), None),
            P(None, ("dp", "group")),
            P(None, None, ("dp", "group")),
            P(None, ("dp", "group"), None),
            P(("dp", "group"), None),
            P(None, ("dp", "group")),
            P(None, None, ("dp", "group")),
            P(None, ("dp", "group"), None),
            P(("dp", "group"), None),
            P(None, ("dp", "group")),
            P(None, None, ("dp", "group")),
            P(None, ("dp", "group"), None),
            P(("dp", "group"), None),
        ),
        check_vma=False,
    )
```
